32 devices in a mesh: batch: 8 (over y, x, core), blk: 4 (over z).
Axes of the slice: x: 2, y: 2, z: 4, core: 2. Of those that a mesh axis runs over, the one named last changes fastest.
Arguments:
- tokens: bfloat16 [24, 2048, 512], P('batch', 'blk'), may hold values from -6 to 6
- lengths: int32 [24], P('batch'), may hold values from 1024 to 2048, as said below
- w_query: bfloat16 [512, 512], replicated, may hold values from -0.25 to 0.25
- w_key: bfloat16 [512, 512], replicated, may hold values from -0.25 to 0.25
- w_value: bfloat16 [512, 512], replicated, may hold values from -0.25 to 0.25
- w_out: bfloat16 [512, 512], replicated, may hold values from -4 to 4
- b_query: float32 [512], replicated, may hold values from -1.5 to 1.5
- b_value: float32 [512], replicated, may hold values from -1.5 to 1.5
- b_out: float32 [512], replicated, may hold values from -1.5 to 1.5
- norm1_gain: float32 [512], replicated, may hold values from 0.25 to 1.75
- norm1_bias: float32 [512], replicated, may hold values from -1.5 to 1.5
- norm2_gain: float32 [512], replicated, may hold values from 0.25 to 1.75
- norm2_bias: float32 [512], replicated, may hold values from -1.5 to 1.5
- final_gain: float32 [512], replicated, may hold values from 0.25 to 1.75
- final_bias: float32 [512], replicated, may hold values from -1.5 to 1.5
- w_inner: bfloat16 [512, 2048], replicated, may hold values from -0.25 to 0.25
- b_inner: float32 [2048], replicated, may hold values from -1.5 to 1.5
- w_outer: bfloat16 [2048, 512], replicated, may hold values from -0.125 to 0.125
- b_outer: float32 [512], replicated, may hold values from -1.5 to 1.5
- cotangent: bfloat16 [24, 2048, 512], P('batch', 'blk'), may hold values from -6 to 6
Outputs:
- layer_out: bfloat16 [24, 2048, 512], P('batch', 'blk')
- grad_tokens: float32 [24, 2048, 512], P('batch', 'blk')
- grad_w_query: float32 [512, 512], replicated
- grad_w_key: float32 [512, 512], replicated
- grad_w_value: float32 [512, 512], replicated
- grad_w_out: float32 [512, 512], replicated
- grad_b_query: float32 [512], replicated
- grad_b_value: float32 [512], replicated
- grad_b_out: float32 [512], replicated
- grad_norm1_gain: float32 [512], replicated
- grad_norm1_bias: float32 [512], replicated
- grad_norm2_gain: float32 [512], replicated
- grad_norm2_bias: float32 [512], replicated
- grad_final_gain: float32 [512], replicated
- grad_final_bias: float32 [512], replicated
- grad_w_inner: float32 [512, 2048], replicated
- grad_b_inner: float32 [2048], replicated
- grad_w_outer: float32 [2048, 512], replicated
- grad_b_outer: float32 [512], replicated
The draws below stay inside these ranges and needn't reach their ends.
Inputs may be any that keep to these rules, and one draw needn't show every extreme that they name: `lengths`: in each aligned block of 3 entries (the buckets of one index of batch) one entry equals 2048; every entry is at least 1024.
All inputs are finite; a program needn't handle non-finite values.
Results may differ from the reference program's by a relative error of at most 0.025.
Values may be sent and summed in bfloat16 or wider, within the bound.
No kernel may reach another device: no remote copies, remote signals or barrier semaphores. Data moves between devices by JAX's collectives and lax.ppermute only.
A program may use at most 256 MiB of HBM per device.

```python
import jax
import jax.numpy as jnp
from jax import lax

D = 512
HEADS = 8
HEAD_DIM = 64
FF = 2048
BUCKETS = 3
SEQ_LEN = 2048
BATCHES = 24


def draw_lengths(key, part):
    key = jax.random.fold_in(key, 11)
    first_key, second_key = jax.random.split(key)
    group_count = BATCHES // BUCKETS
    random_lengths = jax.random.randint(first_key, (group_count, BUCKETS), SEQ_LEN // 2, SEQ_LEN + 1)
    full_slot = jax.random.randint(second_key, (group_count, 1), 0, BUCKETS)
    picked = jnp.arange(BUCKETS, dtype=jnp.int32)[None, :] == full_slot
    return jnp.where(picked, SEQ_LEN, random_lengths).reshape(-1).astype(jnp.int32)


def block_scale(stream_key, dims, shards, low, top_value):
    level = 1.0
    for axis_at, blocks in shards:
        steps = jax.random.uniform(jax.random.fold_in(jax.random.fold_in(stream_key, 6), axis_at), (blocks,), jnp.float32, low / len(shards), top_value / len(shards))
        level = level * jnp.repeat(jnp.exp(steps), dims[axis_at] // blocks).reshape((-1,) + (1,) * (len(dims) - 1 - axis_at))
    return level


def centred(own_key, shape, scale, limit, pieces=(), kind=jnp.bfloat16):
    values = jax.random.normal(own_key, shape, jnp.float32) * scale
    if len(pieces) > 0:
        values = block_scale(own_key, shape, pieces, -0.22, 0.18) * values
    return jnp.clip(values, min=-limit, max=limit).astype(kind)


def setup_inputs(seed: int = 0) -> dict:
    streams_of = jax.random.split(jax.random.key(seed), 21)
    return {
        "tokens": centred(streams_of[0], (BATCHES, SEQ_LEN, D), 1.0, 6.0, ((0, 8), (1, 4))),
        "lengths": draw_lengths(jax.random.fold_in(streams_of[20], 71), 0),
        "w_query": centred(streams_of[2], (D, D), D ** -0.5, 0.25),
        "w_key": centred(streams_of[3], (D, D), D ** -0.5, 0.25),
        "w_value": centred(streams_of[4], (D, D), D ** -0.5, 0.25),
        "w_out": centred(streams_of[5], (D, D), 1.0, 4.0),
        "b_query": centred(streams_of[6], (D,), 0.3, 1.5, (), jnp.float32),
        "b_value": centred(streams_of[7], (D,), 0.3, 1.5, (), jnp.float32),
        "b_out": centred(streams_of[8], (D,), 0.3, 1.5, (), jnp.float32),
        "norm1_gain": jnp.clip(1.0 + 0.15 * jax.random.normal(streams_of[9], (D,), jnp.float32), 0.25, 1.75),
        "norm1_bias": centred(streams_of[10], (D,), 0.3, 1.5, (), jnp.float32),
        "norm2_gain": jnp.clip(1.0 + 0.15 * jax.random.normal(streams_of[11], (D,), jnp.float32), 0.25, 1.75),
        "norm2_bias": centred(streams_of[12], (D,), 0.3, 1.5, (), jnp.float32),
        "final_gain": jnp.clip(1.0 + 0.15 * jax.random.normal(streams_of[13], (D,), jnp.float32), 0.25, 1.75),
        "final_bias": centred(streams_of[14], (D,), 0.3, 1.5, (), jnp.float32),
        "w_inner": centred(streams_of[15], (D, FF), D ** -0.5, 0.25),
        "b_inner": centred(streams_of[16], (FF,), 0.3, 1.5, (), jnp.float32),
        "w_outer": centred(streams_of[17], (FF, D), FF ** -0.5, 0.125),
        "b_outer": centred(streams_of[18], (D,), 0.3, 1.5, (), jnp.float32),
        "cotangent": centred(streams_of[19], (BATCHES, SEQ_LEN, D), 1.0, 6.0, ((0, 8), (1, 4))),
    }


@jax.custom_vjp
def low(v):
    return lax.optimization_barrier(v.astype(jnp.bfloat16)).astype(jnp.float32)

@jax.custom_vjp
def low_back(v):
    return v

def low_keep(v):
    return (low(v), None)

def low_pass(kept, grad):
    return (grad,)

def back_keep(v):
    return (v, None)

def back_low(kept, grad):
    return (low(grad),)
low.defvjp(low_keep, low_pass)
low_back.defvjp(back_keep, back_low)
norm_eps = 1e-05
big_negative = -1e+30
top_precision = lax.Precision.HIGHEST

def both_round(tensor):
    return low(low_back(tensor))

def layer_norm(inputs, norm_gain, norm_shift):
    row_mean = lax.optimization_barrier(jnp.mean(inputs, axis=-1, keepdims=True))
    centered = inputs - row_mean
    variance = lax.optimization_barrier(jnp.mean(centered * centered, axis=-1, keepdims=True))
    return centered * lax.rsqrt(variance + norm_eps) * norm_gain + norm_shift

def matmul(left_side, right_side):
    return jnp.dot(left_side, right_side, precision=top_precision)

def layer(x_float, params, limit_rows):
    w_query, w_key, w_value, w_out, b_query, b_value, b_out, norm1_gain, norm1_bias, norm2_gain, norm2_bias, final_gain, final_bias, w_inner, b_inner, w_outer, b_outer = params
    seq_count = x_float.shape[0]
    query = both_round(matmul(x_float, w_query) + b_query).reshape(seq_count, HEADS, HEAD_DIM)
    keys = both_round(matmul(x_float, w_key)).reshape(seq_count, HEADS, HEAD_DIM)
    values = both_round(matmul(x_float, w_value) + b_value).reshape(seq_count, HEADS, HEAD_DIM)
    logits = jnp.einsum('qhe,khe->hqk', query, keys, precision=top_precision) * HEAD_DIM ** (-0.5)
    logits = low_back(logits)
    key_rows = jnp.arange(seq_count, dtype=jnp.int32)
    visible = key_rows[None, :] <= limit_rows[:, None]
    logits = jnp.where(visible[None], logits, big_negative)
    probs = low(jax.nn.softmax(logits, axis=-1))
    attention = jnp.einsum('hqk,khe->qhe', probs, values, precision=top_precision).reshape(seq_count, HEADS * HEAD_DIM)
    attention = both_round(attention)
    branch_one = low_back(matmul(attention, w_out) + b_out)
    pre_one = x_float + branch_one
    normed_one = layer_norm(pre_one, norm1_gain, norm1_bias)
    dual_one = x_float + branch_one
    hidden = low_back(matmul(low(normed_one), w_inner) + b_inner)
    active = low(jax.nn.gelu(hidden))
    branch_two = low_back(matmul(active, w_outer) + b_outer)
    pre_two = normed_one + branch_two
    dual_two = dual_one + branch_two
    return layer_norm(pre_two, norm2_gain, norm2_bias) + layer_norm(dual_two, final_gain, final_bias)

def add_pair(first_tree, second_tree):
    return first_tree + second_tree

def reference(tokens, lengths, w_query, w_key, w_value, w_out, b_query, b_value, b_out, norm1_gain, norm1_bias, norm2_gain, norm2_bias, final_gain, final_bias, w_inner, b_inner, w_outer, b_outer, cotangent):
    params = (w_query.astype(jnp.float32), w_key.astype(jnp.float32), w_value.astype(jnp.float32), w_out.astype(jnp.float32), b_query.astype(jnp.float32), b_value.astype(jnp.float32), b_out.astype(jnp.float32), norm1_gain.astype(jnp.float32), norm1_bias.astype(jnp.float32), norm2_gain.astype(jnp.float32), norm2_bias.astype(jnp.float32), final_gain.astype(jnp.float32), final_bias.astype(jnp.float32), w_inner.astype(jnp.float32), b_inner.astype(jnp.float32), w_outer.astype(jnp.float32), b_outer.astype(jnp.float32))
    positions = jnp.arange(SEQ_LEN, dtype=jnp.int32)

    def one_bucket(totals, inputs):
        token_rows, length_now, cot_rows = inputs
        limit_rows = jnp.minimum(positions, length_now - 1)
        valid_rows = (positions < length_now).astype(jnp.float32)
        x_float = token_rows.astype(jnp.float32)

        def forward(x_in, params_in):
            return layer(x_in, params_in, limit_rows)
        result, pullback = jax.vjp(forward, x_float, params)
        grad_x, grad_params = pullback(cot_rows.astype(jnp.float32) * valid_rows[:, None])
        totals = jax.tree.map(add_pair, totals, grad_params)
        return (totals, (result.astype(jnp.bfloat16), grad_x))
    zeros_tree = jax.tree.map(jnp.zeros_like, params)
    totals, stacked = lax.scan(one_bucket, zeros_tree, (tokens, lengths, cotangent))
    layer_out, grad_tokens = stacked
    g_wq, g_wk, g_wv, g_wo, g_bq, g_bv, g_bo, g_n1g, g_n1b, g_n2g, g_n2b, g_fg, g_fb, g_wi, g_bi, g_wu, g_bu = totals
    return (layer_out, grad_tokens, g_wq, g_wk, g_wv, g_wo, g_bq, g_bv, g_bo, g_n1g, g_n1b, g_n2g, g_n2b, g_fg, g_fb, g_wi, g_bi, g_wu, g_bu)
```

```python
import functools
import math

import jax
import jax.numpy as jnp
from jax import lax
from jax.experimental import pallas as pl
from jax.experimental.pallas import tpu as pltpu
from jax.sharding import PartitionSpec as P

HEADS = 8
F32 = jnp.float32
BF16 = jnp.bfloat16
FAR = -1e30
EPS = 1e-05
LOG2E = math.log2(math.e)
LN2 = math.log(2.0)
GELU_C = math.sqrt(2.0 / math.pi)
GELU_K = 0.044715
VEC_ROWS = 256
WG_ROWS = 256

VM = pl.BlockSpec(memory_space=pltpu.VMEM)
SM = pl.BlockSpec(memory_space=pltpu.SMEM)
S = jax.ShapeDtypeStruct


def dot(a, b, dims):
    return lax.dot_general(a, b, (dims, ((), ())), preferred_element_type=F32)


def nn(a, b):
    return dot(a, b, ((1,), (0,)))


def nt(a, b):
    return dot(a, b, ((1,), (1,)))


def tn(a, b):
    return dot(a, b, ((0,), (0,)))


def params(mib=56):
    return pltpu.CompilerParams(vmem_limit_bytes=mib * 2**20)


def cost(flops, bytes_accessed):
    return pl.CostEstimate(flops=int(flops), bytes_accessed=int(bytes_accessed), transcendentals=0)


def head_size(features):
    return features // HEADS


def project_heads(out, w_t, rows_ref, bias, scale=None):
    full = nt(w_t, rows_ref)
    if bias is not None:
        full = full + bias
    if scale is not None:
        full = full * scale
    out[...] = full.astype(BF16).reshape(out.shape)


def visible_tile(keys_from, rows_from, shape, length):
    c = keys_from + lax.broadcasted_iota(jnp.int32, shape, 0)
    p = rows_from + lax.broadcasted_iota(jnp.int32, shape, 1)
    return c <= jnp.minimum(p, length - 1)


def attend(slot, masked, me, length, q, k, v, top_s, tot_s, acc_s):
    heads, _, rows = acc_s.shape
    tile = min(256, rows) if slot == 0 else rows
    unroll = 4

    def body(step, carry):
        for i in range(unroll):
            h = step * unroll + i
            for at in range(0, rows, tile):
                ps = slice(at, at + tile)
                keys = at + tile if slot == 0 else rows
                logits = tn(k[h, :, :keys], q[h, :, ps])
                if masked:
                    seen = visible_tile((me - slot) * rows, me * rows + at, logits.shape, length)
                    logits = jnp.where(seen, logits, FAR)
                old = top_s[h, :, ps]
                top = jnp.maximum(jnp.max(logits, axis=0, keepdims=True), old)
                factor = jnp.exp2(old - top)
                weights = jnp.exp2(logits - top)
                tot_s[h, :, ps] = jnp.sum(weights, axis=0, keepdims=True) + factor * tot_s[h, :, ps]
                acc_s[h, :, ps] = nn(v[h, :, :keys], weights.astype(BF16)) + factor * acc_s[h, :, ps]
                top_s[h, :, ps] = top
        return carry

    lax.fori_loop(0, heads // unroll, body, 0)


def own_kernel(me_ref, len_ref, x, wq, wk, wv, bq, bv, q_o, top_o, tot_o, acc_o, k_s, v_s):
    me = me_ref[0]
    length = len_ref[pl.program_id(0)]
    rows = x.shape[1]
    scale = head_size(x.shape[2]) ** -0.5 * LOG2E
    project_heads(q_o.at[0], wq[...], x[0], bq[...], scale)
    top_o[...] = jnp.full(top_o.shape, FAR, F32)
    tot_o[...] = jnp.zeros(tot_o.shape, F32)
    acc_o[...] = jnp.zeros(acc_o.shape, F32)

    @pl.when(me * rows < length)
    def _():
        project_heads(k_s, wk[...], x[0], None)
        project_heads(v_s, wv[...], x[0], bv[...])
        attend(0, True, me, length, q_o.at[0], k_s, v_s, top_o.at[0], tot_o.at[0], acc_o.at[0])


def own_call(me, lengths, tokens, wq, wk, wv, bq, bv):
    buckets, rows, d = tokens.shape
    hd = head_size(d)
    whole = lambda b: (0, 0)
    per = lambda b: (b, 0, 0)
    per4 = lambda b: (b, 0, 0, 0)
    w_spec = pl.BlockSpec((d, d), whole)
    b_spec = pl.BlockSpec((d, 1), whole)
    return pl.pallas_call(
        own_kernel,
        grid=(buckets,),
        out_shape=(
            S((buckets, HEADS, hd, rows), BF16),
            S((buckets, HEADS, 1, rows), F32),
            S((buckets, HEADS, 1, rows), F32),
            S((buckets, HEADS, hd, rows), F32),
        ),
        in_specs=[SM, SM, pl.BlockSpec((1, rows, d), per)] + [w_spec] * 3 + [b_spec] * 2,
        out_specs=(
            pl.BlockSpec((1, HEADS, hd, rows), per4),
            pl.BlockSpec((1, HEADS, 1, rows), per4),
            pl.BlockSpec((1, HEADS, 1, rows), per4),
            pl.BlockSpec((1, HEADS, hd, rows), per4),
        ),
        scratch_shapes=[pltpu.VMEM((HEADS, hd, rows), BF16)] * 2,
        compiler_params=params(),
        cost_estimate=cost(buckets * 8e9, 12e6),
        name="attend_own",
    )(me, lengths, tokens, wq, wk, wv, bq, bv)


def far_kernel(bucket, count, me_ref, len_ref, *refs):
    xs = refs[:count]
    q, top_i, tot_i, acc_i, wk, wv, bv, out_o, lse_o, top_s, tot_s, acc_s, k_s, v_s = refs[count:]
    me = me_ref[0]
    length = len_ref[bucket]
    rows = xs[0].shape[0]
    top_s[...] = top_i[0]
    tot_s[...] = tot_i[0]
    acc_s[...] = acc_i[0]
    for i in range(count):
        slot = i + 1
        first = (me - slot) * rows

        @pl.when((me >= slot) & (first < length))
        def _(slot=slot, first=first, x=xs[i]):
            project_heads(k_s, wk[...], x[...], None)
            project_heads(v_s, wv[...], x[...], bv[...])
            run = lambda masked: attend(slot, masked, me, length, q.at[0], k_s, v_s, top_s, tot_s, acc_s)

            @pl.when(first + rows <= length)
            def _():
                run(False)

            @pl.when(first + rows > length)
            def _():
                run(True)

    out_o[...] = (acc_s[...] / tot_s[...]).astype(BF16)
    lse_o[...] = top_s[...] + jnp.log2(tot_s[...])


def far_call(bucket, me, lengths, xs, q, top, tot, acc, wk, wv, bv):
    rows, d = xs[0].shape
    hd = head_size(d)
    one = lambda i: (bucket, 0, 0, 0)
    wide = pl.BlockSpec((1, HEADS, hd, rows), one)
    thin = pl.BlockSpec((1, HEADS, 1, rows), one)
    return pl.pallas_call(
        functools.partial(far_kernel, bucket, len(xs)),
        grid=(1,),
        out_shape=(S((HEADS, hd, rows), BF16), S((HEADS, 1, rows), F32)),
        in_specs=[SM, SM] + [VM] * len(xs) + [wide, thin, thin, wide] + [VM] * 3,
        out_specs=(VM, VM),
        scratch_shapes=[
            pltpu.VMEM((HEADS, 1, rows), F32),
            pltpu.VMEM((HEADS, 1, rows), F32),
            pltpu.VMEM((HEADS, hd, rows), F32),
            pltpu.VMEM((HEADS, hd, rows), BF16),
            pltpu.VMEM((HEADS, hd, rows), BF16),
        ],
        compiler_params=params(),
        cost_estimate=cost(15e9, 5e6),
        name=f"attend_far_{bucket}",
    )(me, lengths, *xs, q, top, tot, acc, wk, wv, bv)


def norm_stats(v):
    centered = v - jnp.mean(v, axis=-1, keepdims=True)
    r = lax.rsqrt(jnp.mean(centered * centered, axis=-1, keepdims=True) + EPS)
    return centered * r, r


def norm_grad(n, r, gain, upstream):
    gu = gain * upstream
    return r * (gu - jnp.mean(gu, axis=-1, keepdims=True) - n * jnp.mean(gu * n, axis=-1, keepdims=True))


def over_rows(v):
    return jnp.sum(v.astype(F32), axis=0, keepdims=True)


def mid_kernel(bucket, me_ref, len_ref, attn, x, cot, w_out, w_inner, w_outer, vecs, b_inner,
               out_o, branch_o, g_o, delta_o, normed_o, active_o, ghid_o, gtwo_o, gb_o, sums_o,
               slope_s, acc_s):
    me = me_ref[0]
    length = len_ref[bucket]
    rows, d = out_o.shape
    ff = active_o.shape[1]
    step = min(512, ff)
    b_out, gain1, shift1, gain2, shift2, gain_f, shift_f, b_outer = (vecs[i : i + 1] for i in range(8))
    attn_t = attn[...].reshape(d, rows)
    pre_one = x[0].astype(F32) + (tn(attn_t, w_out[...]) + b_out)
    n1, r1 = norm_stats(pre_one)
    normed = n1 * gain1 + shift1
    normed_o[...] = normed.astype(BF16)
    acc_s[...] = jnp.zeros(acc_s.shape, F32)

    def up(i, carry):
        f = pl.ds(pl.multiple_of(i * step, step), step)
        h = nn(normed_o[...], w_inner[:, f]) + b_inner[:, f]
        square = h * h
        t = jnp.tanh(GELU_C * (h + GELU_K * (square * h)))
        half = 0.5 * (1.0 + t)
        active = (h * half).astype(BF16)
        active_o[:, f] = active
        slope_s[:, f] = half + (0.5 * h) * (1.0 - t * t) * (GELU_C + (3.0 * GELU_C * GELU_K) * square)
        acc_s[...] += nn(active, w_outer[f, :])
        return carry

    lax.fori_loop(0, ff // step, up, 0)
    branch_two = acc_s[...] + b_outer
    n2, r2 = norm_stats(normed + branch_two)
    nf, rf = norm_stats(pre_one + branch_two)
    out_o[...] = ((n2 * gain2 + shift2) + (nf * gain_f + shift_f)).astype(BF16)

    @pl.when(me * rows < length)
    def _():
        p = me * rows + lax.broadcasted_iota(jnp.int32, (rows, 1), 0)
        g_out = jnp.where(p < length, cot[0].astype(F32), 0.0)
        g_shift = over_rows(g_out)
        sums_o[0:1] = over_rows(g_out * n2)
        sums_o[1:2] = g_shift
        sums_o[2:3] = over_rows(g_out * nf)
        sums_o[3:4] = g_shift
        g_dual = norm_grad(nf, rf, gain_f, g_out)
        g_two = norm_grad(n2, r2, gain2, g_out)
        g_branch_two = (g_two + g_dual).astype(BF16)
        gtwo_o[...] = g_branch_two
        sums_o[4:5] = over_rows(g_branch_two)
        acc_s[...] = g_two

        def down(i, carry):
            f = pl.ds(pl.multiple_of(i * step, step), step)
            g_hidden = (nt(gtwo_o[...], w_outer[f, :]) * slope_s[:, f]).astype(BF16)
            ghid_o[:, f] = g_hidden
            sums_o[pl.ds(8 + i, 1)] = over_rows(g_hidden)
            acc_s[...] += nt(g_hidden, w_inner[:, f])
            return carry

        lax.fori_loop(0, ff // step, down, 0)
        g_normed = acc_s[...]
        sums_o[5:6] = over_rows(g_normed * n1)
        sums_o[6:7] = over_rows(g_normed)
        g_branch = norm_grad(n1, r1, gain1, g_normed) + g_dual
        branch_o[...] = g_branch
        g_b = g_branch.astype(BF16)
        gb_o[...] = g_b
        sums_o[7:8] = over_rows(g_b)
        g_t = nt(w_out[...], g_b).astype(BF16).reshape(g_o.shape)
        g_o[...] = g_t
        delta_o[...] = jnp.sum(g_t.astype(F32) * attn[...].astype(F32), axis=1, keepdims=True)

    @pl.when(me * rows >= length)
    def _():
        for ref in (branch_o, g_o, delta_o, ghid_o, gtwo_o, gb_o, sums_o):
            ref[...] = jnp.zeros(ref.shape, ref.dtype)


def mid_call(bucket, me, lengths, attn, tokens, cotangent, w_out, w_inner, w_outer, vecs, b_inner):
    _, rows, d = tokens.shape
    ff = w_inner.shape[1]
    hd = head_size(d)
    one = pl.BlockSpec((1, rows, d), lambda i: (bucket, 0, 0))
    return pl.pallas_call(
        functools.partial(mid_kernel, bucket),
        grid=(1,),
        out_shape=(
            S((rows, d), BF16),
            S((rows, d), F32),
            S((HEADS, hd, rows), BF16),
            S((HEADS, 1, rows), F32),
            S((rows, d), BF16),
            S((rows, ff), BF16),
            S((rows, ff), BF16),
            S((rows, d), BF16),
            S((rows, d), BF16),
            S((16, d), F32),
        ),
        in_specs=[SM, SM, VM, one, one] + [VM] * 5,
        out_specs=(VM,) * 10,
        scratch_shapes=[pltpu.VMEM((rows, ff), F32), pltpu.VMEM((rows, d), F32)],
        compiler_params=params(),
        cost_estimate=cost(15e9, 14e6),
        name=f"feed_forward_{bucket}",
    )(me, lengths, attn, tokens, cotangent, w_out, w_inner, w_outer, vecs, b_inner)


def wgrad_kernel(buckets, ff_steps, in_steps, out_steps, *refs):
    groups = [refs[i * buckets : (i + 1) * buckets] for i in range(7)]
    active, g_two, normed, g_hidden, attn, g_b, sums = groups
    out = refs[7 * buckets]
    j = pl.program_id(0)

    @pl.when(j < ff_steps)
    def _():
        out[...] = sum(tn(a[...], g[...]) for a, g in zip(active, g_two)).astype(BF16)

    @pl.when((j >= ff_steps) & (j < ff_steps + in_steps))
    def _():
        out[...] = sum(tn(a[...], g[...]) for a, g in zip(normed, g_hidden)).astype(BF16)

    @pl.when((j >= ff_steps + in_steps) & (j < ff_steps + in_steps + out_steps))
    def _():
        out[...] = sum(nn(a[...], g[...]) for a, g in zip(attn, g_b)).astype(BF16)

    @pl.when(j >= ff_steps + in_steps + out_steps)
    def _():
        out[...] = jnp.zeros(out.shape, BF16)
        out[0:16] = sum(s[...] for s in sums).astype(BF16)


def wgrad_call(active, g_two, normed, g_hidden, attn, g_b, sums):
    buckets = len(active)
    rows, ff = active[0].shape
    d = g_two[0].shape[1]
    step = WG_ROWS
    ff_steps = ff // step
    per_block = d // step
    in_steps = (ff // d) * per_block
    out_steps = d // step
    steps = ff_steps + in_steps + out_steps + VEC_ROWS // step
    clip = lambda v, top: jnp.minimum(jnp.maximum(v, 0), top)
    active_spec = pl.BlockSpec((rows, step), lambda j: (0, clip(j, ff_steps - 1)))
    hid_spec = pl.BlockSpec((rows, d), lambda j: (0, clip(j - ff_steps, in_steps - 1) // per_block))
    norm_spec = pl.BlockSpec((rows, step), lambda j: (0, clip(j - ff_steps, in_steps - 1) % per_block))
    attn_spec = pl.BlockSpec((step, rows), lambda j: (clip(j - ff_steps - in_steps, out_steps - 1), 0))
    full = pl.BlockSpec((rows, d), lambda j: (0, 0))
    attn2 = [a.reshape(d, rows) for a in attn]
    return pl.pallas_call(
        functools.partial(wgrad_kernel, buckets, ff_steps, in_steps, out_steps),
        grid=(steps,),
        out_shape=S((steps * step, d), BF16),
        in_specs=[active_spec] * buckets + [full] * buckets + [norm_spec] * buckets + [hid_spec] * buckets
        + [attn_spec] * buckets + [full] * buckets + [pl.BlockSpec((16, d), lambda j: (0, 0))] * buckets,
        out_specs=pl.BlockSpec((step, d), lambda j: (j, 0)),
        compiler_params=params(),
        cost_estimate=cost(buckets * 3e9, 20e6),
        name="weight_gradients",
    )(*active, *g_two, *normed, *g_hidden, *attn2, *g_b, *sums)


def attend_back(slot, masked, me, length, q, g, k, v, lse, delta, dq, dk, dv):
    heads, _, rows = dq.shape
    tile = min(256, rows) if slot == 0 else rows
    unroll = 4

    def body(step, carry):
        for i in range(unroll):
            h = step * unroll + i
            for at in range(0, rows, tile):
                ps = slice(at, at + tile)
                keys = at + tile if slot == 0 else rows
                q_t, g_t = q[h, :, ps], g[h, :, ps]
                probs = jnp.exp2(tn(k[h, :, :keys], q_t) - lse[h, :, ps])
                if masked:
                    seen = visible_tile((me - slot) * rows, me * rows + at, probs.shape, length)
                    probs = jnp.where(seen, probs, 0.0)
                g_probs = tn(v[h, :, :keys], g_t)
                g_logits = (probs * (g_probs - delta[h, :, ps])).astype(BF16)
                dv[h, :, :keys] += nt(g_t, probs.astype(BF16))
                dk[h, :, :keys] += nt(q_t, g_logits)
                dq[h, :, ps] += nn(k[h, :, :keys], g_logits)
        return carry

    lax.fori_loop(0, heads // unroll, body, 0)


def back_kernel(bucket, slots, fresh, me_ref, len_ref, *refs):
    count = len(slots)
    own = slots[-1] == 0
    refs = list(refs)
    take = lambda n: [refs.pop(0) for _ in range(n)]
    xs = take(count)
    q, g, lse, delta, wq, wk, wv, bv = take(8)
    branch = take(1)[0] if own else None
    dq_i = None if fresh else take(1)[0]
    sums_i = take(1)[0]
    dx_o = take(count - 1 if own else count)
    if own:
        own_o = take(1)[0]
    else:
        dq_o = take(1)[0]
    sums_o = take(1)[0]
    k_s, v_s, dk_s, dv_s, dq_s = refs
    me = me_ref[0]
    length = len_ref[bucket]
    rows, d = xs[0].shape
    live = me * rows < length
    dq_s[...] = jnp.zeros(dq_s.shape, F32) if fresh else dq_i[...]
    sums_o[...] = sums_i[...]
    ones = jnp.ones((8, rows), BF16)
    if own:
        own_o[...] = branch[...]

    for at, slot in enumerate(slots):
        first = (me - slot) * rows

        @pl.when(live & (me >= slot))
        def _(at=at, slot=slot, first=first, x=xs[at]):
            project_heads(k_s, wk[...], x[...], None)
            project_heads(v_s, wv[...], x[...], bv[...])
            dk_s[...] = jnp.zeros(dk_s.shape, F32)
            dv_s[...] = jnp.zeros(dv_s.shape, F32)
            run = lambda masked: attend_back(
                slot, masked, me, length, q.at[0], g, k_s, v_s, lse, delta, dq_s, dk_s, dv_s
            )
            if slot == 0:
                run(True)
            else:

                @pl.when(first + rows <= length)
                def _():
                    run(False)

                @pl.when(first + rows > length)
                def _():
                    run(True)

            dk = (dk_s[...] * LN2).astype(BF16).reshape(d, rows)
            dv = dv_s[...].astype(BF16).reshape(d, rows)
            sums_o[d : 2 * d] += nn(dk, x[...])
            sums_o[2 * d : 3 * d] += nn(dv, x[...])
            sums_o[3 * d + 8 : 3 * d + 16] += nt(ones, dv)
            dx = tn(dk, wk[...]) + tn(dv, wv[...])
            if slot == 0:
                scale = head_size(d) ** -0.5
                dq = (dq_s[...] * scale).astype(BF16).reshape(d, rows)
                own_o[...] += dx + tn(dq, wq[...])
                sums_o[0:d] += nn(dq, x[...])
                sums_o[3 * d : 3 * d + 8] += nt(ones, dq)
            else:
                dx_o[at][...] = dx.astype(BF16)

        if slot != 0:

            @pl.when(jnp.logical_not(live & (me >= slot)))
            def _(at=at):
                dx_o[at][...] = jnp.zeros((rows, d), BF16)

    if not own:
        dq_o[...] = dq_s[...]


def back_call(bucket, slots, me, lengths, xs, q, g, lse, delta, wq, wk, wv, bv, branch, dq, sums):
    rows, d = xs[0].shape
    hd = head_size(d)
    own = slots[-1] == 0
    fresh = dq is None
    one = pl.BlockSpec((1, HEADS, hd, rows), lambda i: (bucket, 0, 0, 0))
    operands = [me, lengths, *xs, q, g, lse, delta, wq, wk, wv, bv]
    specs = [SM, SM] + [VM] * len(xs) + [one] + [VM] * 7
    if own:
        operands.append(branch)
        specs.append(VM)
    if not fresh:
        operands.append(dq)
        specs.append(VM)
    operands.append(sums)
    specs.append(VM)
    far = [s for s in slots if s > 0]
    out_shape = [S((rows, d), BF16) for _ in far]
    out_shape.append(S((rows, d), F32) if own else S((HEADS, hd, rows), F32))
    out_shape.append(S(sums.shape, F32))
    outs = pl.pallas_call(
        functools.partial(back_kernel, bucket, tuple(slots), fresh),
        grid=(1,),
        out_shape=tuple(out_shape),
        in_specs=specs,
        out_specs=(VM,) * len(out_shape),
        scratch_shapes=[pltpu.VMEM((HEADS, hd, rows), BF16)] * 2 + [pltpu.VMEM((HEADS, hd, rows), F32)] * 3,
        compiler_params=params(),
        cost_estimate=cost(10e9 * len(slots), 14e6),
        name=f"attend_back_{bucket}_{slots[0]}",
    )(*operands)
    return outs[: len(far)], outs[-2], outs[-1]


def swap(value, axis, bit):
    size = lax.axis_size(axis)
    return lax.ppermute(value, axis, [(i, i ^ bit) for i in range(size)])


def bit_steps(first_axis):
    steps = [(first_axis, 1 << i) for i in range((lax.axis_size(first_axis) - 1).bit_length())]
    return steps + [("blk", 1 << i) for i in range((lax.axis_size("blk") - 1).bit_length())]


def sum_devices(buffer):
    steps = bit_steps("batch")
    part = buffer
    for axis, bit in steps:
        mine = (lax.axis_index(axis) // bit) % 2
        half = part.shape[0] // 2
        sent = lax.dynamic_slice_in_dim(part, (1 - mine) * half, half)
        kept = lax.dynamic_slice_in_dim(part, mine * half, half)
        got = swap(sent, axis, bit)
        part = (kept.astype(F32) + got.astype(F32)).astype(BF16)
    for axis, bit in reversed(steps):
        mine = (lax.axis_index(axis) // bit) % 2
        got = swap(part, axis, bit)
        low = jnp.where(mine == 0, part, got)
        high = jnp.where(mine == 0, got, part)
        part = jnp.concatenate([low, high], axis=0)
    return part


def on_device(
    tokens, lengths, w_query, w_key, w_value, w_out, b_query, b_value, b_out, norm1_gain, norm1_bias,
    norm2_gain, norm2_bias, final_gain, final_bias, w_inner, b_inner, w_outer, b_outer, cotangent,
):
    buckets, rows, d = tokens.shape
    ff = w_inner.shape[1]
    n = lax.axis_size("blk")
    me = lax.axis_index("blk").astype(jnp.int32).reshape(1)
    wq, wk, wv = w_query.T, w_key.T, w_value.T
    bq, bv = b_query.reshape(d, 1), b_value.reshape(d, 1)
    vecs = jnp.stack([b_out, norm1_gain, norm1_bias, norm2_gain, norm2_bias, final_gain, final_bias, b_outer])

    held = [[tokens[b]] for b in range(buckets)]
    for b in range(buckets):
        for slot in range(1, n):
            pairs = [(i, i + 1) for i in range(slot - 1, n - 1)]
            held[b].append(lax.ppermute(held[b][-1], "blk", pairs))

    q, top, tot, acc = own_call(me, lengths, tokens, wq, wk, wv, bq, bv)
    mids, attns, lses = [], [], []
    for b in range(buckets):
        attn, lse = far_call(b, me, lengths, held[b][1:], q, top, tot, acc, wk, wv, bv)
        attns.append(attn)
        lses.append(lse)
        mids.append(
            mid_call(b, me, lengths, attn, tokens, cotangent, w_out, w_inner, w_outer, vecs, b_inner.reshape(1, ff))
        )
    column = lambda i: [m[i] for m in mids]
    out = jnp.stack(column(0))
    grads = wgrad_call(column(5), column(7), column(4), column(6), attns, column(8), column(9))
    summed = sum_devices(grads)

    sums = jnp.zeros((3 * d + 32, d), F32)
    grad_tokens = []
    for b in range(buckets):
        g, delta, branch = mids[b][2], mids[b][3], mids[b][1]
        cut = max(1, n // 2)
        high, low = list(range(n - 1, cut - 1, -1)), list(range(cut - 1, -1, -1))
        args = (q, g, lses[b], delta, wq, wk, wv, bv, branch)
        dx = {}
        got, dq, sums = back_call(b, high, me, lengths, [held[b][s] for s in high], *args, None, sums)
        dx.update(zip(high, got))
        got, own, sums = back_call(b, low, me, lengths, [held[b][s] for s in low], *args, dq, sums)
        dx.update(zip(low, got))
        carry = None
        for slot in range(n - 1, 0, -1):
            message = dx[slot] if carry is None else (dx[slot].astype(F32) + carry.astype(F32)).astype(BF16)
            carry = lax.ppermute(message, "blk", [(i, i - 1) for i in range(slot, n)])
        grad_tokens.append(own + carry.astype(F32))
    grad_x = jnp.stack(grad_tokens)

    small = sum_devices(sums.astype(BF16)).astype(F32)
    grad_wq, grad_wk, grad_wv = (small[i * d : (i + 1) * d].T for i in range(3))
    grad_bq, grad_bv = small[3 * d], small[3 * d + 8]

    big = summed.astype(F32)
    grad_w_outer = big[:ff]
    grad_w_inner = jnp.concatenate([big[ff + i * d : ff + (i + 1) * d] for i in range(ff // d)], axis=1)
    grad_w_out = big[2 * ff : 2 * ff + d]
    v = big[2 * ff + d :]
    return (
        out, grad_x, grad_wq, grad_wk, grad_wv, grad_w_out, grad_bq, grad_bv, v[7],
        v[5], v[6], v[0], v[1], v[2], v[3],
        grad_w_inner, v[8 : 8 + ff // d].reshape(ff), grad_w_outer, v[4],
    )


def solution(mesh):
    rows = P("batch", "blk", None)
    in_specs = (rows, P("batch")) + (P(),) * 17 + (rows,)
    out_specs = (rows, rows) + (P(),) * 17
    return jax.shard_map(on_device, mesh=mesh, in_specs=in_specs, out_specs=out_specs, check_vma=False)
```

```python
import functools
import math

import jax
import jax.numpy as jnp
from jax import lax
from jax.experimental import pallas as pl
from jax.experimental.pallas import tpu as pltpu
from jax.sharding import PartitionSpec as P

HEADS = 8
F32 = jnp.float32
BF16 = jnp.bfloat16
FAR = -1e30
EPS = 1e-05
SPLIT_FROM = 1
LOG2E = math.log2(math.e)
LN2 = math.log(2.0)
GELU_C = math.sqrt(2.0 / math.pi)
GELU_K = 0.044715

VM = pl.BlockSpec(memory_space=pltpu.VMEM)
SM = pl.BlockSpec(memory_space=pltpu.SMEM)
ANY = pl.BlockSpec(memory_space=pl.ANY)
S = jax.ShapeDtypeStruct


def dot(a, b, dims):
    return lax.dot_general(a, b, (dims, ((), ())), preferred_element_type=F32)


def nn(a, b):
    return dot(a, b, ((1,), (0,)))


def nt(a, b):
    return dot(a, b, ((1,), (1,)))


def tn(a, b):
    return dot(a, b, ((0,), (0,)))


def params(mib=56):
    return pltpu.CompilerParams(vmem_limit_bytes=mib * 2**20)


def cost(flops, bytes_accessed):
    return pl.CostEstimate(flops=int(flops), bytes_accessed=int(bytes_accessed), transcendentals=0)


def head_size(features):
    return features // HEADS


def set_bias(bias, slot, me, length):
    rows = bias.shape[0]
    first = (me - slot) * rows
    partial = (slot == 0) | (first + rows > length)

    @pl.when(partial)
    def _():
        c = first + lax.broadcasted_iota(jnp.int32, bias.shape, 0)
        p = me * rows + lax.broadcasted_iota(jnp.int32, bias.shape, 1)
        bias[...] = jnp.where(c <= jnp.minimum(p, length - 1), 0.0, FAR)

    @pl.when(jnp.logical_not(partial))
    def _():
        bias[...] = jnp.zeros(bias.shape, F32)


def project_pair(w_kv, b_kv, x):
    kv = (nt(w_kv, x) + b_kv).astype(BF16)
    hd = kv.shape[0] // 4
    return [kv[:hd], kv[hd : 2 * hd]], [kv[2 * hd : 3 * hd], kv[3 * hd :]]


def attend_slot(x, q, w_kv, b_kv, bias, top_s, acc_s):
    pairs = w_kv.shape[0]
    rows = x.shape[0]

    def body(pair, carry):
        ks, vs = project_pair(w_kv[pair], b_kv[pair], x[...])
        for i in range(2):
            h = pair * 2 + i
            logits = tn(ks[i], q[h]) + bias[...]
            old = top_s[h]
            top = jnp.maximum(jnp.max(logits, axis=0, keepdims=True), old)
            weights = jnp.exp2(logits - top).astype(BF16)
            v_one = jnp.concatenate([vs[i], jnp.ones((16, rows), BF16)], axis=0)
            acc_s[h] = nn(v_one, weights) + jnp.exp2(old - top) * acc_s[h]
            top_s[h] = top
        return carry

    lax.fori_loop(0, pairs, body, 0)


def own_kernel(bucket, ahead, me_ref, len_ref, x, wq, bq, w_kv, b_kv, *refs):
    more = refs[0]
    refs = refs[len(refs) - 4 - (ahead > 0) :]
    q_o, top_o, acc_o = refs[:3]
    bias = refs[-1]
    me = me_ref[0]
    length = len_ref[bucket]
    rows = x.shape[1]
    scale = head_size(x.shape[2]) ** -0.5 * LOG2E
    pairs = w_kv.shape[0]
    hd = q_o.shape[1]
    if ahead:
        refs[3][...] = more[0]

    def body(pair, carry):
        q = ((nt(wq[pair], x[0]) + bq[pair]) * scale).astype(BF16)
        q_o[2 * pair] = q[:hd]
        q_o[2 * pair + 1] = q[hd:]
        return carry

    lax.fori_loop(0, pairs, body, 0)
    top_o[...] = jnp.full(top_o.shape, FAR, F32)
    acc_o[...] = jnp.zeros(acc_o.shape, F32)

    @pl.when(me * rows < length)
    def _():
        set_bias(bias, 0, me, length)
        attend_slot(x.at[0], q_o, w_kv, b_kv, bias, top_o, acc_o)


def own_call(bucket, me, lengths, tokens, wq, bq, w_kv, b_kv, ahead, after):
    _, rows, d = tokens.shape
    hd = head_size(d)
    shapes = [S((HEADS, hd, rows), BF16), S((HEADS, 1, rows), F32), S((HEADS, hd + 16, rows), F32)]
    one = lambda b: pl.BlockSpec((1, rows, d), lambda i: (b, 0, 0))
    extra = [one(ahead)] if ahead else []
    shapes += [S((rows, d), BF16)] * len(extra)
    return pl.pallas_call(
        functools.partial(own_kernel, bucket, ahead),
        grid=(1,),
        out_shape=tuple(shapes),
        in_specs=[SM, SM, one(bucket)] + [VM] * 4 + extra + [ANY] * len(after),
        out_specs=(VM,) * len(shapes),
        scratch_shapes=[pltpu.VMEM((rows, rows), F32)],
        compiler_params=params(),
        cost_estimate=cost(8e9, 4e6),
        name=f"attend_own_{bucket}",
    )(me, lengths, tokens, wq, bq, w_kv, b_kv, *([tokens] if ahead else []), *after)


def far_kernel(bucket, count, me_ref, len_ref, *refs):
    xs = refs[:count]
    q, top_i, acc_i, w_kv, b_kv = refs[count : count + 5]
    out_o, lse_o, x_s, top_s, acc_s, bias = refs[len(refs) - 6 :]
    me = me_ref[0]
    length = len_ref[bucket]
    rows = xs[0].shape[0]
    hd = out_o.shape[1]
    top_s[...] = top_i[...]
    acc_s[...] = acc_i[...]
    for i in range(count):

        @pl.when(me > i)
        def _(i=i):
            x_s[i] = xs[i][...]

    def body(slot, carry):
        first = (me - slot) * rows

        @pl.when(first < length)
        def _():
            set_bias(bias, slot, me, length)
            attend_slot(x_s.at[slot - 1], q, w_kv, b_kv, bias, top_s, acc_s)

        return carry

    lax.fori_loop(1, jnp.minimum(me, count) + 1, body, 0)

    def finish(h, carry):
        total = acc_s[h, hd : hd + 1]
        out_o[h] = (acc_s[h, :hd] / total).astype(BF16)
        lse_o[h] = top_s[h] + jnp.log2(total)
        return carry

    lax.fori_loop(0, HEADS, finish, 0)


def far_call(bucket, me, lengths, xs, q, top, acc, w_kv, b_kv, after):
    rows, d = xs[0].shape
    hd = head_size(d)
    shapes = ((HEADS, hd, rows), (HEADS, 1, rows), (HEADS, hd + 16, rows))
    operands = [me, lengths, *xs, q, top, acc, w_kv, b_kv]
    specs = [SM, SM] + [VM] * (len(xs) + 5)
    out_shape = [S(shapes[0], BF16), S(shapes[1], F32)]
    return pl.pallas_call(
        functools.partial(far_kernel, bucket, len(xs)),
        grid=(1,),
        out_shape=tuple(out_shape),
        in_specs=specs + [ANY] * len(after),
        out_specs=(VM,) * len(out_shape),
        scratch_shapes=[
            pltpu.VMEM((len(xs), rows, d), BF16),
            pltpu.VMEM(shapes[1], F32),
            pltpu.VMEM(shapes[2], F32),
            pltpu.VMEM((rows, rows), F32),
        ],
        compiler_params=params(),
        cost_estimate=cost(18e9, 5e6),
        name=f"attend_far_{bucket}",
    )(*operands, *after)


def norm_stats(v):
    centered = v - jnp.mean(v, axis=-1, keepdims=True)
    r = lax.rsqrt(jnp.mean(centered * centered, axis=-1, keepdims=True) + EPS)
    return centered * r, r


def norm_grad(n, r, gain, upstream):
    gu = gain * upstream
    return r * (gu - jnp.mean(gu, axis=-1, keepdims=True) - n * jnp.mean(gu * n, axis=-1, keepdims=True))


def over_rows(v):
    return jnp.sum(v.astype(F32), axis=0, keepdims=True)


def mid_kernel(bucket, me_ref, len_ref, attn, x, cot, w_out, w_inner, w_outer, vecs, b_inner, *refs):
    (out_o, branch_o, g_o, delta_o, normed_o, active_o, ghid_o, gtwo_o, gb_o, sums_o,
     pre_s, n1_s, r1_s, dual_s, slope_s, acc_s) = refs[len(refs) - 16 :]
    me = me_ref[0]
    length = len_ref[bucket]
    _, rows, d = out_o.shape
    ff = active_o.shape[1]
    up_step = min(512, ff)
    down_step = min(512, ff)
    block = min(256, rows)
    b_out, gain1, shift1, gain2, shift2, gain_f, shift_f, b_outer = (vecs[i : i + 1] for i in range(8))
    attn_t = attn[...].reshape(d, rows)
    pre_s[...] = tn(attn_t, w_out[...])

    def over_blocks(work):
        def body(i, carry):
            work(pl.ds(pl.multiple_of(i * block, block), block), i * block)
            return carry

        lax.fori_loop(0, rows // block, body, 0)

    def first_norm(at, _):
        pre = x[0, at].astype(F32) + (pre_s[at] + b_out)
        n1, r1 = norm_stats(pre)
        pre_s[at] = pre
        n1_s[at] = n1
        r1_s[at] = r1
        normed_o[at] = (n1 * gain1 + shift1).astype(BF16)

    over_blocks(first_norm)
    acc_s[...] = jnp.zeros(acc_s.shape, F32)

    def lift(i):
        f = pl.ds(pl.multiple_of(i * up_step, up_step), up_step)
        return nn(normed_o[...], w_inner[:, f]) + b_inner[:, f]


    def up(i, carry):
        f = pl.ds(pl.multiple_of(i * up_step, up_step), up_step)
        h = lift(i)
        square = h * h
        t = jnp.tanh(h * (GELU_C + (GELU_C * GELU_K) * square))
        half = 0.5 + 0.5 * t
        active = (h * half).astype(BF16)
        active_o[:, f] = active
        slope_s[:, f] = half + (0.5 * h) * (1.0 - t * t) * (GELU_C + (3.0 * GELU_C * GELU_K) * square)
        acc_s[...] += nn(active, w_outer[f, :])
        return carry

    lax.fori_loop(0, ff // up_step, up, 0)
    sums_o[...] = jnp.zeros(sums_o.shape, F32)

    def last_norms(at, start):
        branch_two = acc_s[at] + b_outer
        normed = n1_s[at] * gain1 + shift1
        n2, r2 = norm_stats(normed + branch_two)
        nf, rf = norm_stats(pre_s[at] + branch_two)
        out_o[0, at] = ((n2 * gain2 + shift2) + (nf * gain_f + shift_f)).astype(BF16)
        p = me * rows + start + lax.broadcasted_iota(jnp.int32, (block, 1), 0)
        g_out = jnp.where(p < length, cot[0, at].astype(F32), 0.0)
        g_dual = norm_grad(nf, rf, gain_f, g_out)
        g_two = norm_grad(n2, r2, gain2, g_out)
        g_branch_two = (g_two + g_dual).astype(BF16)
        gtwo_o[at] = g_branch_two
        dual_s[at] = g_dual
        acc_s[at] = g_two
        sums_o[0:1] += over_rows(g_out * n2)
        sums_o[1:2] += over_rows(g_out)
        sums_o[2:3] += over_rows(g_out * nf)
        sums_o[4:5] += over_rows(g_branch_two)

    over_blocks(last_norms)
    sums_o[3:4] = sums_o[1:2]

    @pl.when(me * rows < length)
    def _():
        def down(i, carry):
            f = pl.ds(pl.multiple_of(i * down_step, down_step), down_step)
            g_hidden = (nt(gtwo_o[...], w_outer[f, :]) * slope_s[:, f]).astype(BF16)
            ghid_o[:, f] = g_hidden
            sums_o[pl.ds(8 + i, 1)] = over_rows(g_hidden)
            acc_s[...] += nt(g_hidden, w_inner[:, f])
            return carry

        lax.fori_loop(0, ff // down_step, down, 0)

        def first_back(at, _):
            g_normed = acc_s[at]
            n1 = n1_s[at]
            g_branch = norm_grad(n1, r1_s[at], gain1, g_normed) + dual_s[at]
            branch_o[at] = g_branch
            g_b = g_branch.astype(BF16)
            gb_o[at] = g_b
            sums_o[5:6] += over_rows(g_normed * n1)
            sums_o[6:7] += over_rows(g_normed)
            sums_o[7:8] += over_rows(g_b)

        over_blocks(first_back)
        g_o[...] = nt(w_out[...], gb_o[...]).astype(BF16).reshape(g_o.shape)

        def head_delta(h, carry):
            delta_o[h] = jnp.sum(g_o[h].astype(F32) * attn[h].astype(F32), axis=0, keepdims=True)
            return carry

        lax.fori_loop(0, HEADS, head_delta, 0)

    @pl.when(me * rows >= length)
    def _():
        for ref in (branch_o, g_o, delta_o, ghid_o, gb_o):
            ref[...] = jnp.zeros(ref.shape, ref.dtype)


def mid_call(bucket, me, lengths, attn, tokens, cotangent, w_out, w_inner, w_outer, vecs, b_inner, out, after):
    buckets, rows, d = tokens.shape
    ff = w_inner.shape[1]
    hd = head_size(d)
    one = pl.BlockSpec((1, rows, d), lambda i: (bucket, 0, 0))
    return pl.pallas_call(
        functools.partial(mid_kernel, bucket),
        grid=(1,),
        out_shape=(
            S((buckets, rows, d), BF16),
            S((rows, d), F32),
            S((HEADS, hd, rows), BF16),
            S((HEADS, 1, rows), F32),
            S((rows, d), BF16),
            S((rows, ff), BF16),
            S((rows, ff), BF16),
            S((rows, d), BF16),
            S((rows, d), BF16),
            S((16, d), F32),
        ),
        in_specs=[SM, SM, VM, one, one] + [VM] * 5 + [ANY] * (len(out) + len(after)),
        out_specs=(one,) + (VM,) * 9,
        input_output_aliases={10: 0} if out else {},
        scratch_shapes=[
            pltpu.VMEM((rows, d), F32),
            pltpu.VMEM((rows, d), F32),
            pltpu.VMEM((rows, 1), F32),
            pltpu.VMEM((rows, d), F32),
            pltpu.VMEM((rows, ff), F32),
            pltpu.VMEM((rows, d), F32),
        ],
        compiler_params=params(),
        cost_estimate=cost(12e9, 14e6),
        name=f"feed_forward_{bucket}",
    )(me, lengths, attn, tokens, cotangent, w_out, w_inner, w_outer, vecs, b_inner, *out, *after)


def wgrad_job(step, half, core):
    return step % half + jnp.where(step < half, 1 - core, core) * half


def wgrad_kernel(buckets, count, half, places, *refs):
    groups = [refs[i * buckets : (i + 1) * buckets] for i in range(7)]
    active, g_two, normed, g_hidden, attn, g_b, sums = groups
    kept_o, sent_o = refs[7 * buckets :]
    step = pl.program_id(0)
    job = wgrad_job(step, half, places[0])

    def put(value):
        @pl.when(step < half)
        def _():
            sent_o[...] = value

        @pl.when(step >= half)
        def _():
            kept_o[...] = value

    @pl.when(job < count)
    def _():
        put(sum(tn(a[...], g[...]) for a, g in zip(active, g_two)).astype(BF16))

    @pl.when((job >= count) & (job < 2 * count))
    def _():
        put(sum(tn(a[...], g[...]) for a, g in zip(normed, g_hidden)).astype(BF16))

    @pl.when(job == 2 * count)
    def _():
        put(sum(nn(a[...], g[...]) for a, g in zip(attn, g_b)).astype(BF16))

    @pl.when(job > 2 * count)
    def _():
        put(jnp.zeros(kept_o.shape, BF16))

    @pl.when(job == 2 * count + 1)
    def _():
        value = sum(s[...] for s in sums).astype(BF16)

        @pl.when(step < half)
        def _():
            sent_o[:16] = value

        @pl.when(step >= half)
        def _():
            kept_o[:16] = value


def wgrad_call(places, devices, active, g_two, normed, g_hidden, attn, g_b, sums):
    buckets = len(active)
    rows, ff = active[0].shape
    d = g_two[0].shape[1]
    count = ff // d
    half = count + 1
    while 2 * half * d % (16 * devices):
        half += 1
    clip = lambda v, top: jnp.minimum(jnp.maximum(v, 0), top)
    job = lambda j, p: wgrad_job(j, half, p[0])
    full = pl.BlockSpec((rows, d), lambda j, p: (0, 0))
    tall = pl.BlockSpec((d, rows), lambda j, p: (0, 0))
    active_spec = pl.BlockSpec((rows, d), lambda j, p: (0, clip(job(j, p), count - 1)))
    hid_spec = pl.BlockSpec((rows, d), lambda j, p: (0, clip(job(j, p) - count, count - 1)))
    attn2 = [a.reshape(d, rows) for a in attn]
    return pl.pallas_call(
        functools.partial(wgrad_kernel, buckets, count, half),
        grid_spec=pltpu.PrefetchScalarGridSpec(
            num_scalar_prefetch=1,
            grid=(2 * half,),
            in_specs=[active_spec] * buckets + [full] * buckets + [full] * buckets + [hid_spec] * buckets
            + [tall] * buckets + [full] * buckets + [pl.BlockSpec((16, d), lambda j, p: (0, 0))] * buckets,
            out_specs=(
                pl.BlockSpec((d, d), lambda j, p: (jnp.maximum(j - half, 0), 0)),
                pl.BlockSpec((d, d), lambda j, p: (jnp.minimum(j, half - 1), 0)),
            ),
        ),
        out_shape=(S((half * d, d), BF16),) * 2,
        compiler_params=params(),
        cost_estimate=cost(buckets * 5e9, 20e6),
        name="weight_gradients",
    )(places, *active, *g_two, *normed, *g_hidden, *attn2, *g_b, *sums)


def attend_back(x, q, g, w_kv, b_kv, lse, delta, bias, dq_s, dx_s, dkv_s, sums_s):
    pairs, width, _ = w_kv.shape
    hd = width // 4
    rows = x.shape[0]

    def body(pair, carry):
        ks, vs = project_pair(w_kv[pair], b_kv[pair], x[...])
        for i in range(2):
            h = pair * 2 + i
            q_t, g_t = q[h], g[h]
            probs = jnp.exp2(tn(ks[i], q_t) + bias[...] - lse[h])
            g_probs = tn(vs[i], g_t)
            g_logits = (probs * (g_probs - delta[h])).astype(BF16)
            dkv_s[(2 + i) * hd : (3 + i) * hd] = nt(g_t, probs.astype(BF16)).astype(BF16)
            dkv_s[i * hd : (i + 1) * hd] = (nt(q_t, g_logits) * LN2).astype(BF16)
            dq_s[h] += nn(ks[i], g_logits)
        dkv = dkv_s[...]
        dx_s[...] += tn(dkv, w_kv[pair])
        sums_s[pair, 2 * hd : 2 * hd + width] += nn(dkv, x[...])
        sums_s[pair, 6 * hd : 6 * hd + 8, :width] += nt(jnp.ones((8, rows), BF16), dkv)
        return carry

    lax.fori_loop(0, pairs, body, 0)


def back_kernel(bucket, low, high, fresh, first, final, places, me_ref, len_ref, *refs):
    count = high - low + 1
    refs = list(refs)
    take = lambda n: [refs.pop(0) for _ in range(n)]
    xs = take(count)
    q, g, lse, delta, w_kv, b_kv = take(6)
    wq, branch = take(2) if low == 0 else (None, None)
    dq_i = None if fresh else take(1)[0]
    sums_i = None if first else take(1)[0]
    x_s, dkv_s, dq_s, dx_s, sums_s, bias = refs[len(refs) - 6 :]
    refs = refs[len(refs) - 8 - final - (high > 0) : len(refs) - 6]
    dx_o = refs.pop(0) if high > 0 else None
    last_o, *sums_o = refs
    me = me_ref[0]
    length = len_ref[bucket]
    rows, d = xs[0].shape
    hd = g.shape[1]
    live = me * rows < length
    dq_s[...] = jnp.zeros(dq_s.shape, F32) if fresh else dq_i[...]
    sums_s[...] = jnp.zeros(sums_s.shape, F32) if first else sums_i[...].astype(F32)
    for i in range(count):

        @pl.when(live & (me >= high - i))
        def _(i=i):
            x_s[i] = xs[i][...]

    def body(i, carry):
        slot = high - i
        active = live & (me >= slot)
        dx_s[...] = jnp.zeros(dx_s.shape, F32)

        @pl.when(active)
        def _():
            set_bias(bias, slot, me, length)
            attend_back(x_s.at[i], q, g, w_kv, b_kv, lse, delta, bias, dq_s, dx_s, dkv_s, sums_s)

        if high > 0:

            @pl.when(slot > 0)
            def _():
                dx_o[i] = dx_s[...].astype(BF16)

        return carry

    lax.fori_loop(0, count, body, 0)
    if low == 0:
        last_o[...] = branch[...] + dx_s[...]

        @pl.when(live)
        def _():
            dq = (dq_s[...] * hd**-0.5).astype(BF16).reshape(d, rows)
            last_o[...] += tn(dq, wq[...])
            dwq = nn(dq, x_s[count - 1])
            dbq = nt(jnp.ones((8, rows), BF16), dq)
            for pair in range(HEADS // 2):
                at = slice(2 * hd * pair, 2 * hd * pair + 2 * hd)
                sums_s[pair, : 2 * hd] += dwq[at]
                sums_s[pair, 6 * hd : 6 * hd + 8, 4 * hd : 6 * hd] += dbq[:, at]
    else:
        last_o[...] = dq_s[...]
    if final:
        half = HEADS // 4
        for ref, core in zip(sums_o, (places[0], 1 - places[0])):
            for i in range(half):
                ref[8 * hd * i : 8 * hd * i + 8 * hd] = sums_s[core * half + i].astype(BF16)
    else:
        sums_o[0][...] = sums_s[...].astype(BF16)


def back_call(
    bucket, low, high, places, me, lengths, xs, q, g, lse, delta, w_kv, b_kv, wq, branch, dq, sums, final, after
):
    rows, d = xs[0].shape
    hd = head_size(d)
    own = low == 0
    fresh = dq is None
    far = high - max(low, 1) + 1
    operands = [places, me, lengths, *xs, q, g, lse, delta, w_kv, b_kv]
    specs = [SM] * 3 + [VM] * (len(xs) + 6)
    if own:
        operands += [wq.reshape(d, d), branch]
        specs += [VM, VM]
    if not fresh:
        operands.append(dq)
        specs.append(VM)
    if sums is not None:
        operands.append(sums)
        specs.append(VM)
    sums_shape = (HEADS // 2, 8 * hd, d)
    out_shape = [S((far, rows, d), BF16)] if far else []
    out_shape += [S((rows, d), F32) if own else S((HEADS, hd, rows), F32)]
    out_shape += [S((HEADS // 4 * 8 * hd, d), BF16)] * 2 if final else [S(sums_shape, BF16)]
    outs = pl.pallas_call(
        functools.partial(back_kernel, bucket, low, high, fresh, sums is None, final),
        grid=(1,),
        out_shape=tuple(out_shape),
        in_specs=specs + [ANY] * len(after),
        out_specs=(VM,) * len(out_shape),
        scratch_shapes=[
            pltpu.VMEM((len(xs), rows, d), BF16),
            pltpu.VMEM((4 * hd, rows), BF16),
            pltpu.VMEM((HEADS, hd, rows), F32),
            pltpu.VMEM((rows, d), F32),
            pltpu.VMEM(sums_shape, F32),
            pltpu.VMEM((rows, rows), F32),
        ],
        compiler_params=params(),
        cost_estimate=cost(10e9 * len(xs), 14e6),
        name=f"attend_back_{bucket}_{high}",
    )(*operands, *after)
    last = len(out_shape) - (3 if final else 2)
    return (outs[0] if far else None), outs[last], (outs[last + 1 :] if final else outs[-1])


def step_call(name, places, jobs, after):
    operands, specs, shapes, bodies = [places], [SM], [], []
    for job_in, job_specs, job_out, body in jobs:
        bodies.append((len(job_in), len(job_out), body))
        operands += job_in
        specs += job_specs
        shapes += job_out
    first_out = len(operands) + len(after)

    def kernel(places_ref, *refs):
        at_in, at_out = 0, first_out - 1
        for n_in, n_out, body in bodies:
            body(places_ref, *refs[at_in : at_in + n_in], *refs[at_out : at_out + n_out])
            at_in += n_in
            at_out += n_out

    outs = pl.pallas_call(
        kernel,
        grid=(1,),
        out_shape=tuple(shapes),
        in_specs=specs + [ANY] * len(after),
        out_specs=(VM,) * len(shapes),
        compiler_params=params(),
        cost_estimate=cost(2e9, 4e6),
        name=name,
    )(*operands, *after)
    found = []
    for _, n_out, _ in bodies:
        found.append(outs[:n_out])
        outs = outs[n_out:]
    return found


def gate(arrays, after):
    outs = pl.pallas_call(
        lambda *refs: None,
        out_shape=tuple(S(a.shape, a.dtype) for a in arrays),
        in_specs=[ANY] * (len(arrays) + len(after)),
        out_specs=(ANY,) * len(arrays),
        input_output_aliases={i: i for i in range(len(arrays))},
        name="gate",
    )(*arrays, *after)
    return list(outs)


class Group:
    def __init__(self, index, axis, low, high):
        self.index, self.axis, self.low, self.count = index, axis, low, 1 << (high - low)
        self.place = (lax.axis_index(axis) >> low) & (self.count - 1)

    def swap(self, value, mask):
        size = lax.axis_size(self.axis)
        return lax.ppermute(value, self.axis, [(i, i ^ (mask << self.low)) for i in range(size)])


def part_rows(place, mask, size):
    return pl.ds(pl.multiple_of((place ^ mask) * size, size), size)


def total(kept, got, at):
    return (kept[at].astype(F32) + sum(g[at].astype(F32) for g in got)).astype(BF16)


def split_job(kept, got, group):
    rows, d = kept.shape
    count = group.count if group else 1
    size = rows // count

    def body(places, kept, *refs):
        arrived, outs = refs[: len(got)], refs[len(got) :]
        for m in range(count):
            at = part_rows(places[group.index], m, size) if group else slice(None)
            outs[m][...] = total(kept, arrived, at)

    return [kept, *got], [VM] * (1 + len(got)), [S((size, d), BF16)] * count, body


def join_job(part, got, group):
    size, d = part.shape

    def body(places, *refs):
        for m in range(group.count):
            refs[-1][part_rows(places[group.index], m, size)] = refs[m][...]

    return [part, *got], [VM] * (1 + len(got)), [S((size * group.count, d), BF16)], body


def message_job(dx, at, carry):
    _, rows, d = dx.shape
    more = [] if carry is None else [carry]

    def body(places, dx, *refs):
        if more:
            refs[-1][...] = (dx[0].astype(F32) + refs[0][...].astype(F32)).astype(BF16)
        else:
            refs[-1][...] = dx[0]

    specs = [pl.BlockSpec((1, rows, d), lambda i: (at, 0, 0))] + [VM] * len(more)
    return [dx, *more], specs, [S((rows, d), BF16)], body


def sum_over_devices(kept, sent, groups):
    first, *rest = groups
    got = [first.swap(sent, 1)]
    for group in rest:
        kept, *shards = yield split_job(kept, got, group)
        got = [group.swap(s, m + 1) for m, s in enumerate(shards)]
    (part,) = yield split_job(kept, got, None)
    for group in reversed(rest):
        got = [group.swap(part, m) for m in range(1, group.count)]
        (part,) = yield join_job(part, got, group)
    return part, first.swap(part, 1)


def send_back(pieces, n):
    carry = None
    for i, slot in enumerate(range(n - 1, 0, -1)):
        (message,) = yield message_job(*pieces(i), carry)
        carry = lax.ppermute(message, "blk", [(j, j - 1) for j in range(slot, n)])
    return carry


class Process:
    def __init__(self, steps):
        self.steps, self.result = steps, None
        self.job = next(steps)

    def advance(self, outs):
        try:
            self.job = self.steps.send(outs)
        except StopIteration as end:
            self.job, self.result = None, end.value


class Board:
    def __init__(self, places):
        self.places, self.active, self.ticks = places, [], 0

    def start(self, steps):
        self.active.append(Process(steps))
        return self.active[-1]

    def tick(self, after):
        self.ticks += 1
        outs = step_call(f"step_{self.ticks}", self.places, [p.job for p in self.active], after)
        for p, o in zip(list(self.active), outs):
            p.advance(o)
        self.active = [p for p in self.active if p.job is not None]
        return [o for group in outs for o in group]


def big_kernel(ff, places, mine, got, *refs):
    outer_o, inner_o, out_o, vec_o = refs[len(refs) - 4 :]
    half, d = mine.shape
    count = ff // d
    for own_half in range(2):

        @pl.when(places[0] == own_half)
        def _(own_half=own_half):
            for i in range(2 * half // d):
                src = mine if i // (half // d) == own_half else got
                at = (i % (half // d)) * d
                value = src[at : at + d]
                if i < count:
                    outer_o[i * d : i * d + d] = value.astype(F32)
                elif i < 2 * count:
                    inner_o[:, (i - count) * d : (i - count) * d + d] = value.astype(F32)
                elif i == 2 * count:
                    out_o[...] = value.astype(F32)
                elif i == 2 * count + 1:
                    vec_o[...] = value[:16].astype(F32)


def big_call(places, mine, got, ff, after):
    d = mine.shape[1]
    shapes = (S((ff, d), F32), S((d, ff), F32), S((d, d), F32), S((16, d), F32))
    return pl.pallas_call(
        functools.partial(big_kernel, ff),
        grid=(1,),
        out_shape=shapes,
        in_specs=[SM, VM, VM] + [ANY] * len(after),
        out_specs=(VM,) * 4,
        compiler_params=params(),
        cost_estimate=cost(5e9, 14e6),
        name="feed_forward_sums",
    )(places, mine, got, *after)


def small_kernel(places, mine, got, *refs):
    weights, bias_o = refs[len(refs) - 4 : len(refs) - 1], refs[-1]
    d = weights[0].shape[0]
    hd = head_size(d)
    half = HEADS // 4
    bias_o[...] = jnp.zeros(bias_o.shape, F32)
    for own_half in range(2):

        @pl.when(places[0] == own_half)
        def _(own_half=own_half):
            for pair in range(HEADS // 2):
                src = mine if pair // half == own_half else got
                at = (pair % half) * 8 * hd
                lanes = slice(2 * hd * pair, 2 * hd * pair + 2 * hd)
                for k in range(3):
                    rows = src[at + 2 * hd * k : at + 2 * hd * k + 2 * hd].astype(F32)
                    weights[k][:, lanes] = rows.T
                bias = src[at + 6 * hd : at + 6 * hd + 16].astype(F32)
                bias_o[0:1, lanes] = bias[:1, 4 * hd : 6 * hd]
                bias_o[1:2, lanes] = bias[:1, 2 * hd : 4 * hd]


def small_call(places, mine, got):
    d = mine.shape[1]
    return pl.pallas_call(
        small_kernel,
        grid=(1,),
        out_shape=(S((d, d), F32),) * 3 + (S((8, d), F32),),
        in_specs=[SM, VM, VM],
        out_specs=(VM,) * 4,
        compiler_params=params(),
        cost_estimate=cost(2e9, 5e6),
        name="attention_sums",
    )(places, mine, got)


def tokens_kernel(mine, carry, *refs):
    refs[-1][0] = mine[...] + carry[...].astype(F32)


def tokens_call(bucket, buckets, mine, carry, whole, after):
    rows, d = mine.shape
    return pl.pallas_call(
        tokens_kernel,
        grid=(1,),
        out_shape=S((buckets, rows, d), F32),
        in_specs=[VM, VM] + [ANY] * (len(whole) + len(after)),
        out_specs=pl.BlockSpec((1, rows, d), lambda i: (bucket, 0, 0)),
        input_output_aliases={2: 0} if whole else {},
        compiler_params=params(),
        cost_estimate=cost(2e9, 3e6),
        name=f"token_gradients_{bucket}",
    )(mine, carry, *whole, *after)


def on_device(
    tokens, lengths, w_query, w_key, w_value, w_out, b_query, b_value, b_out, norm1_gain, norm1_bias,
    norm2_gain, norm2_bias, final_gain, final_bias, w_inner, b_inner, w_outer, b_outer, cotangent,
):
    buckets, rows, d = tokens.shape
    ff = w_inner.shape[1]
    hd = head_size(d)
    pairs = HEADS // 2
    n = lax.axis_size("blk")
    me = lax.axis_index("blk").astype(jnp.int32).reshape(1)
    bits = lambda axis: (lax.axis_size(axis) - 1).bit_length()
    groups = [Group(0, "batch", 0, 1), Group(1, "batch", 1, bits("batch")), Group(2, "blk", 0, bits("blk"))]
    places = jnp.stack([g.place for g in groups]).astype(jnp.int32)
    devices = math.prod(g.count for g in groups)
    groups = [groups[0]] + [g for g in groups[1:] if g.count > 1]

    paired = lambda w: w.T.reshape(pairs, 2 * hd, d)
    wq = paired(w_query)
    bq = b_query.reshape(pairs, 2 * hd, 1)
    w_kv = jnp.concatenate([paired(w_key), paired(w_value)], axis=1)
    b_v = b_value.reshape(pairs, 2 * hd, 1)
    b_kv = jnp.concatenate([jnp.zeros_like(b_v), b_v], axis=1)
    vecs = jnp.stack([b_out, norm1_gain, norm1_bias, norm2_gain, norm2_bias, final_gain, final_bias, b_outer])
    b_in = b_inner.reshape(1, ff)

    def hop(value, slot):
        return lax.ppermute(value, "blk", [(i, i + 1) for i in range(slot - 1, n - 1)])

    run_own = lambda b, after: own_call(b, me, lengths, tokens, wq, bq, w_kv, b_kv, (b + 1) % buckets, after)
    run_far = lambda b, after: far_call(b, me, lengths, held[b][1:], own[b][0], own[b][1], own[b][2], w_kv, b_kv, after)
    run_mid = lambda b, out, after: mid_call(
        b, me, lengths, attns[b], tokens, cotangent, w_out, w_inner, w_outer, vecs, b_in, out, after
    )
    held = [[tokens[b]] for b in range(buckets)]
    own, mids, attns, lses, out = [], [], [], [], []
    moving = {}
    if n == 4 and buckets == 3:
        plan = [
            ([(0, 1)], [(0, 2), (1, 1)]),
            ([(0, 2), (1, 1)], [(0, 3)]),
            ([(0, 3)], [(1, 2), (2, 1)]),
            ([(1, 2)], [(1, 3)]),
            ([(1, 3), (2, 1)], [(2, 2)]),
            ([(2, 2)], [(2, 3)]),
            ([(2, 3)], []),
        ]
    else:
        plan = []
        for b in range(buckets):
            for slot in range(1, n):
                source = held[b][-1]
                held[b].append(hop(source, slot))
    if plan:
        moving[0, 1] = hop(tokens[0], 1)

    def passing(kernel, last):
        if kernel >= len(plan):
            return [last]
        arrived, next_hops = plan[kernel]
        fresh = [b for b, slot in next_hops if slot == 1]
        held_on = [(b, slot - 1) for b, slot in next_hops if slot > 1 and (b, slot - 1) not in arrived]
        values = [moving.pop(k) for k in arrived] + [held[b][slot] for b, slot in held_on]
        passed = gate(values + [own[b - 1][3] for b in fresh], [last])
        for k, value in zip(arrived, passed):
            held[k[0]].append(value)
        for (b, slot), value in zip(held_on, passed[len(arrived) :]):
            held[b][slot] = value
        starts = dict(zip(fresh, passed[len(values) :]))
        for b, slot in next_hops:
            moving[b, slot] = hop(starts[b] if slot == 1 else held[b][slot - 1], slot)
        return passed[:1]

    after = [vecs, b_in]
    for b in range(buckets):
        own.append(run_own(b, after))
        after = passing(b, own[b][0])
    for b in range(buckets):
        attn, lse = run_far(b, after)
        attns.append(attn)
        lses.append(lse)
        after = passing(buckets + 2 * b, lse)
        mids.append(run_mid(b, out, after))
        out = [mids[b][0]]
        after = passing(buckets + 2 * b + 1, mids[b][9])
    column = lambda i: [m[i] for m in mids]
    kept, sent = wgrad_call(
        places, devices, column(5), column(7), column(4), column(6), attns, column(8), column(9)
    )

    board = Board(places)
    big = board.start(sum_over_devices(kept, sent, groups))
    waiting = [sent]
    mine, returns = [], []
    sums = None
    for b in range(buckets):
        g, delta, branch = mids[b][2], mids[b][3], mids[b][1]
        args = (own[b][0], g, lses[b], delta, w_kv, b_kv, wq, branch)
        dx = {}
        last = b + 1 == buckets
        cut = max(1, n // 2) if b >= SPLIT_FROM else 0
        pieces = lambda i, dx=dx, cut=cut: (dx[0], i) if i < n - max(cut, 1) else (dx[1], i - (n - cut))
        if cut:
            there = held[b][n - 1 : cut - 1 : -1]
            dx[0], dq, sums = back_call(b, cut, n - 1, places, me, lengths, there, *args, None, sums, False, waiting)
            returns.append(board.start(send_back(pieces, n)))
            waiting = board.tick([sums])
            there = held[b][cut - 1 :: -1]
            dx[1], own_part, sums = back_call(b, 0, cut - 1, places, me, lengths, there, *args, dq, sums, last, waiting)
            if not last:
                waiting = board.tick([sums])
        else:
            dx[0], own_part, sums = back_call(b, 0, n - 1, places, me, lengths, held[b][::-1], *args, None, sums, last, waiting)
            returns.append(board.start(send_back(pieces, n)))
            waiting = board.tick([sums])
        mine.append(own_part)
    small = sum_over_devices(*sums, groups)
    small_first = Process(small)
    after = [sums[1]]
    whole, grads, done = [], None, set()
    started = False
    while board.active or not started:
        sent = board.tick(after + [r.result for r in returns if r.result is not None])
        if not started:
            board.active.append(small_first)
            started = True
        after = []
        ready = [b for b in range(buckets) if b not in done and returns[b].result is not None]
        if grads is None and big.result is not None:
            grads = big_call(places, *big.result, ff, sent)
            after = [grads[3]]
        elif ready:
            b = ready[0]
            whole = [tokens_call(b, buckets, mine[b], returns[b].result, whole, sent)]
            done.add(b)
            after = whole
    for b in range(buckets):
        if b not in done:
            whole = [tokens_call(b, buckets, mine[b], returns[b].result, whole, [])]
    grad_wq, grad_wk, grad_wv, bias = small_call(places, *small_first.result)
    grad_w_outer, grad_w_inner, grad_w_out, v = grads
    return (
        out[0], whole[0], grad_wq, grad_wk, grad_wv, grad_w_out, bias[0], bias[1], v[7],
        v[5], v[6], v[0], v[1], v[2], v[3],
        grad_w_inner, v[8 : 8 + ff // d].reshape(ff), grad_w_outer, v[4],
    )


def solution(mesh):
    rows = P("batch", "blk", None)
    in_specs = (rows, P("batch")) + (P(),) * 17 + (rows,)
    out_specs = (rows, rows) + (P(),) * 17
    return jax.shard_map(on_device, mesh=mesh, in_specs=in_specs, out_specs=out_specs, check_vma=False)
```

```python
import functools
import math

import jax
import jax.numpy as jnp
from jax import lax
from jax.experimental import pallas as pl
from jax.experimental.pallas import tpu as pltpu
from jax.sharding import PartitionSpec as P

HEADS = 8
F32 = jnp.float32
BF16 = jnp.bfloat16
FAR = -1e30
EPS = 1e-05
SPLIT_FROM = 1
LOG2E = math.log2(math.e)
LN2 = math.log(2.0)
GELU_C = math.sqrt(2.0 / math.pi)
GELU_K = 0.044715

VM = pl.BlockSpec(memory_space=pltpu.VMEM)
SM = pl.BlockSpec(memory_space=pltpu.SMEM)
ANY = pl.BlockSpec(memory_space=pl.ANY)
S = jax.ShapeDtypeStruct


def dot(a, b, dims):
    return lax.dot_general(a, b, (dims, ((), ())), preferred_element_type=F32)


def nn(a, b):
    return dot(a, b, ((1,), (0,)))


def nt(a, b):
    return dot(a, b, ((1,), (1,)))


def tn(a, b):
    return dot(a, b, ((0,), (0,)))


def params(mib=56):
    return pltpu.CompilerParams(vmem_limit_bytes=mib * 2**20)


def cost(flops, bytes_accessed):
    return pl.CostEstimate(flops=int(flops), bytes_accessed=int(bytes_accessed), transcendentals=0)


def head_size(features):
    return features // HEADS


def set_bias(bias, slot, me, length):
    rows = bias.shape[0]
    first = (me - slot) * rows
    partial = (slot == 0) | (first + rows > length)

    @pl.when(partial)
    def _():
        c = first + lax.broadcasted_iota(jnp.int32, bias.shape, 0)
        p = me * rows + lax.broadcasted_iota(jnp.int32, bias.shape, 1)
        bias[...] = jnp.where(c <= jnp.minimum(p, length - 1), 0.0, FAR)

    @pl.when(jnp.logical_not(partial))
    def _():
        bias[...] = jnp.zeros(bias.shape, F32)


def project_pair(w_kv, b_kv, x):
    kv = (nt(w_kv, x) + b_kv).astype(BF16)
    hd = kv.shape[0] // 4
    return [kv[:hd], kv[hd : 2 * hd]], [kv[2 * hd : 3 * hd], kv[3 * hd :]]


def attend_slot(x, q, w_kv, b_kv, bias, top_s, acc_s):
    pairs = w_kv.shape[0]
    rows = x.shape[0]

    def body(step, carry):
        for j in range(2):
            one_pair(step * 2 + j)
        return carry

    def one_pair(pair):
        ks, vs = project_pair(w_kv[pair], b_kv[pair], x[...])
        for i in range(2):
            h = pair * 2 + i
            logits = tn(ks[i], q[h]) + bias[...]
            old = top_s[h]
            top = jnp.maximum(jnp.max(logits, axis=0, keepdims=True), old)
            weights = jnp.exp2(logits - top).astype(BF16)
            v_one = jnp.concatenate([vs[i], jnp.ones((16, rows), BF16)], axis=0)
            acc_s[h] = nn(v_one, weights) + jnp.exp2(old - top) * acc_s[h]
            top_s[h] = top

    lax.fori_loop(0, pairs // 2, body, 0)


def own_kernel(bucket, ahead, me_ref, len_ref, x, wq, bq, w_kv, b_kv, *refs):
    more = refs[0]
    refs = refs[len(refs) - 4 - (ahead > 0) :]
    q_o, top_o, acc_o = refs[:3]
    bias = refs[-1]
    me = me_ref[0]
    length = len_ref[bucket]
    rows = x.shape[1]
    scale = head_size(x.shape[2]) ** -0.5 * LOG2E
    pairs = w_kv.shape[0]
    hd = q_o.shape[1]
    if ahead:
        refs[3][...] = more[0]

    def body(pair, carry):
        q = ((nt(wq[pair], x[0]) + bq[pair]) * scale).astype(BF16)
        q_o[2 * pair] = q[:hd]
        q_o[2 * pair + 1] = q[hd:]
        return carry

    lax.fori_loop(0, pairs, body, 0)
    top_o[...] = jnp.full(top_o.shape, FAR, F32)
    acc_o[...] = jnp.zeros(acc_o.shape, F32)

    @pl.when(me * rows < length)
    def _():
        set_bias(bias, 0, me, length)
        attend_slot(x.at[0], q_o, w_kv, b_kv, bias, top_o, acc_o)


def own_call(bucket, me, lengths, tokens, wq, bq, w_kv, b_kv, ahead, after):
    _, rows, d = tokens.shape
    hd = head_size(d)
    shapes = [S((HEADS, hd, rows), BF16), S((HEADS, 1, rows), F32), S((HEADS, hd + 16, rows), F32)]
    one = lambda b: pl.BlockSpec((1, rows, d), lambda i: (b, 0, 0))
    extra = [one(ahead)] if ahead else []
    shapes += [S((rows, d), BF16)] * len(extra)
    return pl.pallas_call(
        functools.partial(own_kernel, bucket, ahead),
        grid=(1,),
        out_shape=tuple(shapes),
        in_specs=[SM, SM, one(bucket)] + [VM] * 4 + extra + [ANY] * len(after),
        out_specs=(VM,) * len(shapes),
        scratch_shapes=[pltpu.VMEM((rows, rows), F32)],
        compiler_params=params(),
        cost_estimate=cost(8e9, 4e6),
        name=f"attend_own_{bucket}",
    )(me, lengths, tokens, wq, bq, w_kv, b_kv, *([tokens] if ahead else []), *after)


def far_kernel(bucket, count, me_ref, len_ref, *refs):
    xs = refs[:count]
    q, top_i, acc_i, w_kv, b_kv = refs[count : count + 5]
    out_o, lse_o, x_s, top_s, acc_s, bias = refs[len(refs) - 6 :]
    me = me_ref[0]
    length = len_ref[bucket]
    rows = xs[0].shape[0]
    hd = out_o.shape[1]
    top_s[...] = top_i[...]
    acc_s[...] = acc_i[...]
    for i in range(count):

        @pl.when(me > i)
        def _(i=i):
            x_s[i] = xs[i][...]

    def body(slot, carry):
        first = (me - slot) * rows

        @pl.when(first < length)
        def _():
            set_bias(bias, slot, me, length)
            attend_slot(x_s.at[slot - 1], q, w_kv, b_kv, bias, top_s, acc_s)

        return carry

    lax.fori_loop(1, jnp.minimum(me, count) + 1, body, 0)

    def finish(h, carry):
        total = acc_s[h, hd : hd + 1]
        out_o[h] = (acc_s[h, :hd] / total).astype(BF16)
        lse_o[h] = top_s[h] + jnp.log2(total)
        return carry

    lax.fori_loop(0, HEADS, finish, 0)


def far_call(bucket, me, lengths, xs, q, top, acc, w_kv, b_kv, after):
    rows, d = xs[0].shape
    hd = head_size(d)
    shapes = ((HEADS, hd, rows), (HEADS, 1, rows), (HEADS, hd + 16, rows))
    operands = [me, lengths, *xs, q, top, acc, w_kv, b_kv]
    specs = [SM, SM] + [VM] * (len(xs) + 5)
    out_shape = [S(shapes[0], BF16), S(shapes[1], F32)]
    return pl.pallas_call(
        functools.partial(far_kernel, bucket, len(xs)),
        grid=(1,),
        out_shape=tuple(out_shape),
        in_specs=specs + [ANY] * len(after),
        out_specs=(VM,) * len(out_shape),
        scratch_shapes=[
            pltpu.VMEM((len(xs), rows, d), BF16),
            pltpu.VMEM(shapes[1], F32),
            pltpu.VMEM(shapes[2], F32),
            pltpu.VMEM((rows, rows), F32),
        ],
        compiler_params=params(),
        cost_estimate=cost(18e9, 5e6),
        name=f"attend_far_{bucket}",
    )(*operands, *after)


def norm_stats(v):
    centered = v - jnp.mean(v, axis=-1, keepdims=True)
    r = lax.rsqrt(jnp.mean(centered * centered, axis=-1, keepdims=True) + EPS)
    return centered * r, r


def norm_grad(n, r, gain, upstream):
    gu = gain * upstream
    return r * (gu - jnp.mean(gu, axis=-1, keepdims=True) - n * jnp.mean(gu * n, axis=-1, keepdims=True))


def over_rows(v):
    return jnp.sum(v.astype(F32), axis=0, keepdims=True)


def mid_kernel(bucket, me_ref, len_ref, attn, x, cot, w_out, w_inner, w_outer, vecs, b_inner, *refs):
    (out_o, branch_o, g_o, delta_o, normed_o, active_o, ghid_o, gtwo_o, gb_o, sums_o,
     pre_s, n1_s, r1_s, dual_s, slope_s, acc_s,
     inner_s, outer_s, cot_s, normed_s, active_s, ghid_s, gtwo_s, sems) = refs[len(refs) - 24 :]
    copies_in = [
        pltpu.make_async_copy(a, b, sems.at[i])
        for i, (a, b) in enumerate([(w_inner, inner_s), (w_outer, outer_s), (cot.at[bucket], cot_s)])
    ]
    for copy in copies_in:
        copy.start()
    w_inner, w_outer, cot = inner_s, outer_s, cot_s
    copies_out = [
        pltpu.make_async_copy(a, b, sems.at[3 + i])
        for i, (a, b) in enumerate([(normed_s, normed_o), (active_s, active_o), (gtwo_s, gtwo_o), (ghid_s, ghid_o)])
    ]
    me = me_ref[0]
    length = len_ref[bucket]
    _, rows, d = out_o.shape
    ff = active_s.shape[1]
    up_step = min(512, ff)
    down_step = min(512, ff)
    block = min(256, rows)
    b_out, gain1, shift1, gain2, shift2, gain_f, shift_f, b_outer = (vecs[i : i + 1] for i in range(8))
    attn_t = attn[...].reshape(d, rows)
    pre_s[...] = tn(attn_t, w_out[...])

    def over_blocks(work):
        def body(i, carry):
            work(pl.ds(pl.multiple_of(i * block, block), block), i * block)
            return carry

        lax.fori_loop(0, rows // block, body, 0)

    def first_norm(at, _):
        pre = x[0, at].astype(F32) + (pre_s[at] + b_out)
        n1, r1 = norm_stats(pre)
        pre_s[at] = pre
        n1_s[at] = n1
        r1_s[at] = r1
        normed_s[at] = (n1 * gain1 + shift1).astype(BF16)

    over_blocks(first_norm)
    copies_out[0].start()
    copies_in[0].wait()
    copies_in[1].wait()
    acc_s[...] = jnp.zeros(acc_s.shape, F32)

    def lift(i):
        f = pl.ds(pl.multiple_of(i * up_step, up_step), up_step)
        return nn(normed_s[...], w_inner[:, f]) + b_inner[:, f]


    def up(i, carry):
        f = pl.ds(pl.multiple_of(i * up_step, up_step), up_step)
        h = lift(i)
        square = h * h
        t = jnp.tanh(h * (GELU_C + (GELU_C * GELU_K) * square))
        half = 0.5 + 0.5 * t
        active = (h * half).astype(BF16)
        active_s[:, f] = active
        slope_s[:, f] = half + (0.5 * h) * (1.0 - t * t) * (GELU_C + (3.0 * GELU_C * GELU_K) * square)
        acc_s[...] += nn(active, w_outer[f, :])
        return carry

    lax.fori_loop(0, ff // up_step, up, 0)
    copies_out[1].start()
    sums_o[...] = jnp.zeros(sums_o.shape, F32)
    copies_in[2].wait()

    def last_norms(at, start):
        branch_two = acc_s[at] + b_outer
        normed = n1_s[at] * gain1 + shift1
        n2, r2 = norm_stats(normed + branch_two)
        nf, rf = norm_stats(pre_s[at] + branch_two)
        out_o[0, at] = ((n2 * gain2 + shift2) + (nf * gain_f + shift_f)).astype(BF16)
        p = me * rows + start + lax.broadcasted_iota(jnp.int32, (block, 1), 0)
        g_out = jnp.where(p < length, cot[at].astype(F32), 0.0)
        g_dual = norm_grad(nf, rf, gain_f, g_out)
        g_two = norm_grad(n2, r2, gain2, g_out)
        g_branch_two = (g_two + g_dual).astype(BF16)
        gtwo_s[at] = g_branch_two
        dual_s[at] = g_dual
        acc_s[at] = g_two
        sums_o[0:1] += over_rows(g_out * n2)
        sums_o[1:2] += over_rows(g_out)
        sums_o[2:3] += over_rows(g_out * nf)
        sums_o[4:5] += over_rows(g_branch_two)

    over_blocks(last_norms)
    copies_out[2].start()
    sums_o[3:4] = sums_o[1:2]

    @pl.when(me * rows < length)
    def _():
        def down(i, carry):
            f = pl.ds(pl.multiple_of(i * down_step, down_step), down_step)
            g_hidden = (nt(gtwo_s[...], w_outer[f, :]) * slope_s[:, f]).astype(BF16)
            ghid_s[:, f] = g_hidden
            sums_o[pl.ds(8 + i, 1)] = over_rows(g_hidden)
            acc_s[...] += nt(g_hidden, w_inner[:, f])
            return carry

        lax.fori_loop(0, ff // down_step, down, 0)
        copies_out[3].start()

        def first_back(at, _):
            g_normed = acc_s[at]
            n1 = n1_s[at]
            g_branch = norm_grad(n1, r1_s[at], gain1, g_normed) + dual_s[at]
            branch_o[at] = g_branch
            g_b = g_branch.astype(BF16)
            gb_o[at] = g_b
            sums_o[5:6] += over_rows(g_normed * n1)
            sums_o[6:7] += over_rows(g_normed)
            sums_o[7:8] += over_rows(g_b)

        over_blocks(first_back)
        g_o[...] = nt(w_out[...], gb_o[...]).astype(BF16).reshape(g_o.shape)

        def head_delta(h, carry):
            delta_o[h] = jnp.sum(g_o[h].astype(F32) * attn[h].astype(F32), axis=0, keepdims=True)
            return carry

        lax.fori_loop(0, HEADS, head_delta, 0)

    @pl.when(me * rows >= length)
    def _():
        for ref in (branch_o, g_o, delta_o, ghid_s, gb_o):
            ref[...] = jnp.zeros(ref.shape, ref.dtype)
        copies_out[3].start()

    for copy in copies_out:
        copy.wait()


def mid_call(bucket, me, lengths, attn, tokens, cotangent, w_out, w_inner, w_outer, vecs, b_inner, out, after):
    buckets, rows, d = tokens.shape
    ff = w_inner.shape[1]
    hd = head_size(d)
    one = pl.BlockSpec((1, rows, d), lambda i: (bucket, 0, 0))
    return pl.pallas_call(
        functools.partial(mid_kernel, bucket),
        grid=(1,),
        out_shape=(
            S((buckets, rows, d), BF16),
            S((rows, d), F32),
            S((HEADS, hd, rows), BF16),
            S((HEADS, 1, rows), F32),
            S((rows, d), BF16),
            S((rows, ff), BF16),
            S((rows, ff), BF16),
            S((rows, d), BF16),
            S((rows, d), BF16),
            S((16, d), F32),
        ),
        in_specs=[SM, SM, VM, one, ANY, VM, ANY, ANY, VM, VM] + [ANY] * (len(out) + len(after)),
        out_specs=(one, VM, VM, VM, ANY, ANY, ANY, ANY, VM, VM),
        input_output_aliases={10: 0} if out else {},
        scratch_shapes=[
            pltpu.VMEM((rows, d), F32),
            pltpu.VMEM((rows, d), F32),
            pltpu.VMEM((rows, 1), F32),
            pltpu.VMEM((rows, d), F32),
            pltpu.VMEM((rows, ff), F32),
            pltpu.VMEM((rows, d), F32),
            pltpu.VMEM((d, ff), BF16),
            pltpu.VMEM((ff, d), BF16),
            pltpu.VMEM((rows, d), BF16),
            pltpu.VMEM((rows, d), BF16),
            pltpu.VMEM((rows, ff), BF16),
            pltpu.VMEM((rows, ff), BF16),
            pltpu.VMEM((rows, d), BF16),
            pltpu.SemaphoreType.DMA((7,)),
        ],
        compiler_params=params(),
        cost_estimate=cost(12e9, 14e6),
        name=f"feed_forward_{bucket}",
    )(me, lengths, attn, tokens, cotangent, w_out, w_inner, w_outer, vecs, b_inner, *out, *after)


def wgrad_job(step, half, core):
    return step % half + jnp.where(step < half, 1 - core, core) * half


def rows_of(refs):
    return jnp.concatenate([r[...] for r in refs], axis=0)


def wgrad_kernel(buckets, count, half, places, *refs):
    groups = [refs[i * buckets : (i + 1) * buckets] for i in range(7)]
    active, g_two, normed, g_hidden, attn, g_b, sums = groups
    kept_o, sent_o = refs[7 * buckets :]
    step = pl.program_id(0)
    job = wgrad_job(step, half, places[0])

    def put(value):
        @pl.when(step < half)
        def _():
            sent_o[...] = value

        @pl.when(step >= half)
        def _():
            kept_o[...] = value

    @pl.when(job < count)
    def _():
        put(tn(rows_of(active), rows_of(g_two)).astype(BF16))

    @pl.when((job >= count) & (job < 2 * count))
    def _():
        put(tn(rows_of(normed), rows_of(g_hidden)).astype(BF16))

    @pl.when(job == 2 * count)
    def _():
        put(sum(nn(a[...], g[...]) for a, g in zip(attn, g_b)).astype(BF16))

    @pl.when(job > 2 * count)
    def _():
        put(jnp.zeros(kept_o.shape, BF16))

    @pl.when(job == 2 * count + 1)
    def _():
        value = sum(s[...] for s in sums).astype(BF16)

        @pl.when(step < half)
        def _():
            sent_o[:16] = value

        @pl.when(step >= half)
        def _():
            kept_o[:16] = value


def wgrad_call(places, devices, active, g_two, normed, g_hidden, attn, g_b, sums):
    buckets = len(active)
    rows, ff = active[0].shape
    d = g_two[0].shape[1]
    count = ff // d
    half = count + 1
    while 2 * half * d % (16 * devices):
        half += 1
    clip = lambda v, top: jnp.minimum(jnp.maximum(v, 0), top)
    job = lambda j, p: wgrad_job(j, half, p[0])
    full = pl.BlockSpec((rows, d), lambda j, p: (0, 0))
    tall = pl.BlockSpec((d, rows), lambda j, p: (0, 0))
    active_spec = pl.BlockSpec((rows, d), lambda j, p: (0, clip(job(j, p), count - 1)))
    hid_spec = pl.BlockSpec((rows, d), lambda j, p: (0, clip(job(j, p) - count, count - 1)))
    attn2 = [a.reshape(d, rows) for a in attn]
    return pl.pallas_call(
        functools.partial(wgrad_kernel, buckets, count, half),
        grid_spec=pltpu.PrefetchScalarGridSpec(
            num_scalar_prefetch=1,
            grid=(2 * half,),
            in_specs=[active_spec] * buckets + [full] * buckets + [full] * buckets + [hid_spec] * buckets
            + [tall] * buckets + [full] * buckets + [pl.BlockSpec((16, d), lambda j, p: (0, 0))] * buckets,
            out_specs=(
                pl.BlockSpec((d, d), lambda j, p: (jnp.maximum(j - half, 0), 0)),
                pl.BlockSpec((d, d), lambda j, p: (jnp.minimum(j, half - 1), 0)),
            ),
        ),
        out_shape=(S((half * d, d), BF16),) * 2,
        compiler_params=params(),
        cost_estimate=cost(buckets * 5e9, 20e6),
        name="weight_gradients",
    )(places, *active, *g_two, *normed, *g_hidden, *attn2, *g_b, *sums)


def attend_back(x, q, g, w_kv, b_kv, lse, delta, bias, dq_s, kv_s, dkv_s):
    pairs, width, d = w_kv.shape
    hd = width // 4
    rows = x.shape[0]
    block = 2 * width

    def project(i, carry):
        at = pl.ds(pl.multiple_of(i * block, block), block)
        w = w_kv[pl.ds(2 * i, 2)].reshape(block, d)
        kv_s[at] = (nt(w, x[...]) + b_kv[pl.ds(2 * i, 2)].reshape(block, 1)).astype(BF16)
        return carry

    lax.fori_loop(0, pairs // 2, project, 0)

    def body(step, carry):
        for j in range(2):
            one_pair(step * 2 + j)
        return carry

    def one_pair(pair):
        base = pl.multiple_of(pair * width, width)
        for i in range(2):
            h = pair * 2 + i
            at_k = pl.ds(base + i * hd, hd)
            at_v = pl.ds(base + (2 + i) * hd, hd)
            k = kv_s[at_k]
            q_t, g_t = q[h], g[h]
            probs = jnp.exp2(tn(k, q_t) + bias[...] - lse[h])
            g_probs = tn(kv_s[at_v], g_t)
            g_logits = (probs * (g_probs - delta[h])).astype(BF16)
            dkv_s[at_v] = nt(g_t, probs.astype(BF16)).astype(BF16)
            dkv_s[at_k] = (nt(q_t, g_logits) * LN2).astype(BF16)
            dq_s[h] += nn(k, g_logits)

    lax.fori_loop(0, pairs // 2, body, 0)


def back_kernel(bucket, low, high, fresh, first, final, places, me_ref, len_ref, *refs):
    count = high - low + 1
    refs = list(refs)
    take = lambda n: [refs.pop(0) for _ in range(n)]
    xs = take(count)
    q, g, lse, delta, w_kv, b_kv = take(6)
    sems = refs.pop()
    wq, branch = take(2) if low == 0 else (None, None)
    dq_i = None if fresh else take(1)[0]
    sums_i = None if first else take(1)[0]
    x_s, kv_s, dkv_s, dq_s, dx_s, bias, *late = refs[len(refs) - 6 - (low == 0) - (not first) :]
    refs = refs[: len(refs) - 6 - len(late)]
    refs = refs[len(refs) - 2 - final - (high > 0) :]
    dx_o = refs.pop(0) if high > 0 else None
    last_o, *sums_o = refs
    me = me_ref[0]
    length = len_ref[bucket]
    rows, d = xs[0].shape
    hd = g.shape[1]
    live = me * rows < length
    dq_s[...] = jnp.zeros(dq_s.shape, F32) if fresh else dq_i[...]
    rows_in = [
        pltpu.make_async_copy(xs[i], x_s.at[pl.ds(i * rows, rows)], sems.at[i]) for i in range(count)
    ]
    late_in = [
        pltpu.make_async_copy(source, to, sems.at[count + j])
        for j, (source, to) in enumerate(zip([branch] * (low == 0) + [sums_i] * (not first), late))
    ]
    for copy in rows_in + late_in:
        copy.start()

    def take_rows(i):
        for j in range(count):

            @pl.when(i == j)
            def _(j=j):
                rows_in[j].wait()

    def dx_out(i):
        return pltpu.make_async_copy(dx_s.at[i], dx_o.at[i], sems.at[count + 2 + i])

    def body(i, carry):
        slot = high - i
        at = pl.ds(pl.multiple_of(i * rows, rows), rows)
        active = live & (me >= slot)
        take_rows(i)

        @pl.when(active)
        def _():
            set_bias(bias, slot, me, length)
            attend_back(x_s.at[at], q, g, w_kv, b_kv, lse, delta, bias, dq_s, kv_s, dkv_s.at[:, at])

        @pl.when(active & (slot > 0))
        def _():
            dx_s[i] = tn(dkv_s[:, at], w_kv[...].reshape(2 * d, d)).astype(BF16)

        @pl.when(jnp.logical_not(active))
        def _():
            dkv_s[:, at] = jnp.zeros((2 * d, rows), BF16)

        @pl.when(jnp.logical_not(active) & (slot > 0))
        def _():
            dx_s[i] = jnp.zeros((rows, d), BF16)

        @pl.when(slot > 0)
        def _():
            dx_out(i).start()

        return carry

    lax.fori_loop(0, count, body, 0)
    pairs = HEADS // 2
    dq = (dq_s[...] * hd**-0.5).astype(BF16).reshape(d, rows)
    here = slice((count - 1) * rows, count * rows)
    for copy in late_in:
        copy.wait()
    if low == 0:
        last_o[...] = late[0][...]

        @pl.when(live)
        def _():
            last_o[...] += tn(dkv_s[:, here], w_kv[...].reshape(2 * d, d)) + tn(dq, wq[...])
    else:
        last_o[...] = dq_s[...]

    half = HEADS // 4
    ones = jnp.ones((8, count * rows), BF16)

    def add(pair, carry):
        at = pl.ds(pl.multiple_of(pair * 4 * hd, 4 * hd), 4 * hd)
        dkv = dkv_s[at, :]
        parts = [None, nn(dkv, x_s[...]), None]
        bias_sums = [nt(ones, dkv), jnp.zeros((8, d - 4 * hd), F32)]
        if low == 0:
            dq_pair = (dq_s[pl.ds(2 * pair, 2)] * hd**-0.5).astype(BF16).reshape(2 * hd, rows)
            parts[0] = nn(dq_pair, x_s[here])
            bias_sums[1:] = [nt(ones[:, :rows], dq_pair), jnp.zeros((8, d - 6 * hd), F32)]
        else:
            parts[0] = jnp.zeros((2 * hd, d), F32)
        parts[2] = jnp.concatenate([jnp.concatenate(bias_sums, axis=1), jnp.zeros((8, d), F32)])
        value = jnp.concatenate(parts, axis=0)
        if not first:
            value = value + late[-1][pair].astype(F32)
        value = value.astype(BF16)
        if final:
            kept = pair // half == places[0]
            to = pl.ds(pl.multiple_of((pair % half) * 6 * hd, 6 * hd), 6 * hd)
            to_bias = pl.ds(pl.multiple_of(half * 6 * hd + (pair % half) * 16, 16), 16)

            def put(ref):
                ref[to] = value[: 6 * hd]
                ref[to_bias] = value[6 * hd :]

            @pl.when(kept)
            def _():
                put(sums_o[0])

            @pl.when(jnp.logical_not(kept))
            def _():
                put(sums_o[1])
        else:
            sums_o[0][pair] = value
        return carry

    if final:
        used = half * (6 * hd + 16)
        for ref in sums_o:
            if used < ref.shape[0]:
                ref[used:] = jnp.zeros((ref.shape[0] - used, d), BF16)
    lax.fori_loop(0, pairs, add, 0)
    for i in range(count - (low == 0)):
        dx_out(i).wait()


def back_call(
    bucket, low, high, places, me, lengths, xs, q, g, lse, delta, w_kv, b_kv, wq, branch, dq, sums, final, after
):
    rows, d = xs[0].shape
    hd = head_size(d)
    own = low == 0
    fresh = dq is None
    far = high - max(low, 1) + 1
    operands = [places, me, lengths, *xs, q, g, lse, delta, w_kv, b_kv]
    specs = [SM] * 3 + [ANY] * len(xs) + [VM] * 6
    late = []
    if own:
        operands += [wq.reshape(d, d), branch]
        specs += [VM, ANY]
        late.append(branch)
    if not fresh:
        operands.append(dq)
        specs.append(VM)
    if sums is not None:
        operands.append(sums)
        specs.append(ANY)
        late.append(sums)
    sums_shape = (HEADS // 2, 6 * hd + 16, d)
    out_shape = [S((far, rows, d), BF16)] if far else []
    out_shape += [S((rows, d), F32) if own else S((HEADS, hd, rows), F32)]
    out_shape += [S((final, d), BF16)] * 2 if final else [S(sums_shape, BF16)]
    outs = pl.pallas_call(
        functools.partial(back_kernel, bucket, low, high, fresh, sums is None, final > 0),
        grid=(1,),
        out_shape=tuple(out_shape),
        in_specs=specs + [ANY] * len(after),
        out_specs=((ANY,) if far else ()) + (VM,) * (len(out_shape) - (far > 0)),
        scratch_shapes=[
            pltpu.VMEM((len(xs) * rows, d), BF16),
            pltpu.VMEM((2 * d, rows), BF16),
            pltpu.VMEM((2 * d, len(xs) * rows), BF16),
            pltpu.VMEM((HEADS, hd, rows), F32),
            pltpu.VMEM((max(far, 1), rows, d), BF16),
            pltpu.VMEM((rows, rows), F32),
            *[pltpu.VMEM(a.shape, a.dtype) for a in late],
            pltpu.SemaphoreType.DMA((2 * len(xs) + 2,)),
        ],
        compiler_params=params(),
        cost_estimate=cost(10e9 * len(xs), 14e6),
        name=f"attend_back_{bucket}_{high}",
    )(*operands, *after)
    last = len(out_shape) - (3 if final else 2)
    return (outs[0] if far else None), outs[last], (outs[last + 1 :] if final else outs[-1])


def step_call(name, places, jobs, after):
    operands, specs, shapes, bodies = [places], [SM], [], []
    for job_in, job_specs, job_out, body in jobs:
        bodies.append((len(job_in), len(job_out), body))
        operands += job_in
        specs += job_specs
        shapes += job_out
    first_out = len(operands) + len(after)

    def kernel(places_ref, *refs):
        at_in, at_out = 0, first_out - 1
        for n_in, n_out, body in bodies:
            body(places_ref, *refs[at_in : at_in + n_in], *refs[at_out : at_out + n_out])
            at_in += n_in
            at_out += n_out

    outs = pl.pallas_call(
        kernel,
        grid=(1,),
        out_shape=tuple(shapes),
        in_specs=specs + [ANY] * len(after),
        out_specs=(VM,) * len(shapes),
        compiler_params=params(),
        cost_estimate=cost(2e9, 4e6),
        name=name,
    )(*operands, *after)
    found = []
    for _, n_out, _ in bodies:
        found.append(outs[:n_out])
        outs = outs[n_out:]
    return found


def gate(arrays, after):
    outs = pl.pallas_call(
        lambda *refs: None,
        out_shape=tuple(S(a.shape, a.dtype) for a in arrays),
        in_specs=[ANY] * (len(arrays) + len(after)),
        out_specs=(ANY,) * len(arrays),
        input_output_aliases={i: i for i in range(len(arrays))},
        name="gate",
    )(*arrays, *after)
    return list(outs)


class Group:
    def __init__(self, index, axis, low, high):
        self.index, self.axis, self.low, self.count = index, axis, low, 1 << (high - low)
        self.place = (lax.axis_index(axis) >> low) & (self.count - 1)

    def swap(self, value, mask):
        size = lax.axis_size(self.axis)
        return lax.ppermute(value, self.axis, [(i, i ^ (mask << self.low)) for i in range(size)])


def part_rows(place, mask, size):
    return pl.ds(pl.multiple_of((place ^ mask) * size, size), size)


def total(kept, got, at):
    values = [r[at].astype(F32) for r in [kept, *got]]
    while len(values) > 1:
        values = [a + b for a, b in zip(values[::2], values[1::2])]
    return values[0].astype(BF16)


def split_job(kept, got, group):
    rows, d = kept.shape
    count = group.count if group else 1
    size = rows // count

    def body(places, kept, *refs):
        arrived, outs = refs[: len(got)], refs[len(got) :]
        for m in range(count):
            at = part_rows(places[group.index], m, size) if group else slice(None)
            outs[m][...] = total(kept, arrived, at)

    return [kept, *got], [VM] * (1 + len(got)), [S((size, d), BF16)] * count, body


def join_job(part, got, group):
    size, d = part.shape

    def body(places, *refs):
        for m in range(group.count):
            refs[-1][part_rows(places[group.index], m, size)] = refs[m][...]

    return [part, *got], [VM] * (1 + len(got)), [S((size * group.count, d), BF16)], body


def message_job(dx, at, carry):
    _, rows, d = dx.shape
    more = [] if carry is None else [carry]

    def body(places, dx, *refs):
        if more:
            refs[-1][...] = (dx[0].astype(F32) + refs[0][...].astype(F32)).astype(BF16)
        else:
            refs[-1][...] = dx[0]

    specs = [pl.BlockSpec((1, rows, d), lambda i: (at, 0, 0))] + [VM] * len(more)
    return [dx, *more], specs, [S((rows, d), BF16)], body


def sum_over_devices(kept, sent, groups, full=False):
    first, *rest = groups
    got = [first.swap(sent, 1)]
    scatter = rest[:-1] if full else rest
    for group in scatter:
        kept, *shards = yield split_job(kept, got, group)
        got = [group.swap(s, m + 1) for m, s in enumerate(shards)]
    (part,) = yield split_job(kept, got, None)
    if full and rest:
        got = [rest[-1].swap(part, m) for m in range(1, rest[-1].count)]
        (part,) = yield split_job(part, got, None)
    for group in reversed(scatter):
        got = [group.swap(part, m) for m in range(1, group.count)]
        (part,) = yield join_job(part, got, group)
    return part, first.swap(part, 1)


def send_back(pieces, n):
    carry = None
    for i, slot in enumerate(range(n - 1, 0, -1)):
        (message,) = yield message_job(*pieces(i), carry)
        carry = lax.ppermute(message, "blk", [(j, j - 1) for j in range(slot, n)])
    return carry


class Process:
    def __init__(self, steps):
        self.steps, self.result = steps, None
        self.job = next(steps)

    def advance(self, outs):
        try:
            self.job = self.steps.send(outs)
        except StopIteration as end:
            self.job, self.result = None, end.value


class Board:
    def __init__(self, places):
        self.places, self.active, self.ticks = places, [], 0

    def start(self, steps):
        self.active.append(Process(steps))
        return self.active[-1]

    def tick(self, after, only=None):
        self.ticks += 1
        now = self.active if only is None else only
        outs = step_call(f"step_{self.ticks}", self.places, [p.job for p in now], after)
        for p, o in zip(list(now), outs):
            p.advance(o)
        self.active = [p for p in self.active if p.job is not None]
        return [o for group in outs for o in group]


def big_kernel(ff, places, mine, got, *refs):
    outer_o, inner_o, out_o, vec_o = refs[len(refs) - 4 :]
    half, d = mine.shape
    count = ff // d
    for own_half in range(2):

        @pl.when(places[0] == own_half)
        def _(own_half=own_half):
            for i in range(2 * half // d):
                src = mine if i // (half // d) == own_half else got
                at = (i % (half // d)) * d
                value = src[at : at + d]
                if i < count:
                    outer_o[i * d : i * d + d] = value.astype(F32)
                elif i < 2 * count:
                    inner_o[:, (i - count) * d : (i - count) * d + d] = value.astype(F32)
                elif i == 2 * count:
                    out_o[...] = value.astype(F32)
                elif i == 2 * count + 1:
                    vec_o[...] = value[:16].astype(F32)


def big_call(places, mine, got, ff, after):
    d = mine.shape[1]
    shapes = (S((ff, d), F32), S((d, ff), F32), S((d, d), F32), S((16, d), F32))
    return pl.pallas_call(
        functools.partial(big_kernel, ff),
        grid=(1,),
        out_shape=shapes,
        in_specs=[SM, VM, VM] + [ANY] * len(after),
        out_specs=(VM,) * 4,
        compiler_params=params(),
        cost_estimate=cost(5e9, 14e6),
        name="feed_forward_sums",
    )(places, mine, got, *after)


def small_kernel(places, mine, got, *refs):
    weights, bias_o = refs[len(refs) - 4 : len(refs) - 1], refs[-1]
    d = weights[0].shape[0]
    hd = head_size(d)
    half = HEADS // 4
    bias_o[...] = jnp.zeros(bias_o.shape, F32)
    for own_half in range(2):

        @pl.when(places[0] == own_half)
        def _(own_half=own_half):
            for pair in range(HEADS // 2):
                src = mine if pair // half == own_half else got
                at = (pair % half) * 6 * hd
                at_bias = half * 6 * hd + (pair % half) * 16
                lanes = slice(2 * hd * pair, 2 * hd * pair + 2 * hd)
                for k in range(3):
                    rows = src[at + 2 * hd * k : at + 2 * hd * k + 2 * hd].astype(F32)
                    weights[k][:, lanes] = rows.T
                bias = src[at_bias : at_bias + 16].astype(F32)
                bias_o[0:1, lanes] = bias[:1, 4 * hd : 6 * hd]
                bias_o[1:2, lanes] = bias[:1, 2 * hd : 4 * hd]


def small_call(places, mine, got):
    d = mine.shape[1]
    return pl.pallas_call(
        small_kernel,
        grid=(1,),
        out_shape=(S((d, d), F32),) * 3 + (S((8, d), F32),),
        in_specs=[SM, VM, VM],
        out_specs=(VM,) * 4,
        compiler_params=params(),
        cost_estimate=cost(2e9, 5e6),
        name="attention_sums",
    )(places, mine, got)


def tokens_kernel(mine, carry, *refs):
    refs[-1][0] = mine[...] + carry[...].astype(F32)


def tokens_call(bucket, buckets, mine, carry, whole, after):
    rows, d = mine.shape
    return pl.pallas_call(
        tokens_kernel,
        grid=(1,),
        out_shape=S((buckets, rows, d), F32),
        in_specs=[VM, VM] + [ANY] * (len(whole) + len(after)),
        out_specs=pl.BlockSpec((1, rows, d), lambda i: (bucket, 0, 0)),
        input_output_aliases={2: 0} if whole else {},
        compiler_params=params(),
        cost_estimate=cost(2e9, 3e6),
        name=f"token_gradients_{bucket}",
    )(mine, carry, *whole, *after)


def on_device(
    tokens, lengths, w_query, w_key, w_value, w_out, b_query, b_value, b_out, norm1_gain, norm1_bias,
    norm2_gain, norm2_bias, final_gain, final_bias, w_inner, b_inner, w_outer, b_outer, cotangent,
):
    buckets, rows, d = tokens.shape
    ff = w_inner.shape[1]
    hd = head_size(d)
    pairs = HEADS // 2
    n = lax.axis_size("blk")
    me = lax.axis_index("blk").astype(jnp.int32).reshape(1)
    bits = lambda axis: (lax.axis_size(axis) - 1).bit_length()
    groups = [Group(0, "batch", 0, 1), Group(1, "batch", 1, bits("batch")), Group(2, "blk", 0, bits("blk"))]
    places = jnp.stack([g.place for g in groups]).astype(jnp.int32)
    devices = math.prod(g.count for g in groups)
    groups = [groups[0]] + [g for g in groups[1:] if g.count > 1]

    paired = lambda w: w.T.reshape(pairs, 2 * hd, d)
    wq = paired(w_query)
    bq = b_query.reshape(pairs, 2 * hd, 1)
    w_kv = jnp.concatenate([paired(w_key), paired(w_value)], axis=1)
    b_v = b_value.reshape(pairs, 2 * hd, 1)
    b_kv = jnp.concatenate([jnp.zeros_like(b_v), b_v], axis=1)
    vecs = jnp.stack([b_out, norm1_gain, norm1_bias, norm2_gain, norm2_bias, final_gain, final_bias, b_outer])
    b_in = b_inner.reshape(1, ff)

    def hop(value, slot):
        return lax.ppermute(value, "blk", [(i, i + 1) for i in range(slot - 1, n - 1)])

    run_own = lambda b, after: own_call(b, me, lengths, tokens, wq, bq, w_kv, b_kv, (b + 1) % buckets, after)
    run_far = lambda b, after: far_call(b, me, lengths, held[b][1:], own[b][0], own[b][1], own[b][2], w_kv, b_kv, after)
    run_mid = lambda b, out, after: mid_call(
        b, me, lengths, attns[b], tokens, cotangent, w_out, w_inner, w_outer, vecs, b_in, out, after
    )
    held = [[tokens[b]] for b in range(buckets)]
    own, mids, attns, lses, out = [], [], [], [], []
    moving = {}
    if n == 4 and buckets == 3:
        plan = [
            ([(0, 1)], [(0, 2), (1, 1)]),
            ([(0, 2), (1, 1)], [(0, 3)]),
            ([(0, 3)], [(1, 2), (2, 1)]),
            ([(1, 2)], [(1, 3)]),
            ([(1, 3), (2, 1)], [(2, 2)]),
            ([(2, 2)], [(2, 3)]),
            ([(2, 3)], []),
        ]
    else:
        plan = []
        for b in range(buckets):
            for slot in range(1, n):
                source = held[b][-1]
                held[b].append(hop(source, slot))
    if plan:
        moving[0, 1] = hop(tokens[0], 1)

    def passing(kernel, last):
        if kernel >= len(plan):
            return [last]
        arrived, next_hops = plan[kernel]
        fresh = [b for b, slot in next_hops if slot == 1]
        held_on = [(b, slot - 1) for b, slot in next_hops if slot > 1 and (b, slot - 1) not in arrived]
        values = [moving.pop(k) for k in arrived] + [held[b][slot] for b, slot in held_on]
        passed = gate(values + [own[b - 1][3] for b in fresh], [last])
        for k, value in zip(arrived, passed):
            held[k[0]].append(value)
        for (b, slot), value in zip(held_on, passed[len(arrived) :]):
            held[b][slot] = value
        starts = dict(zip(fresh, passed[len(values) :]))
        for b, slot in next_hops:
            moving[b, slot] = hop(starts[b] if slot == 1 else held[b][slot - 1], slot)
        return passed[:1]

    after = [vecs, b_in]
    for b in range(buckets):
        own.append(run_own(b, after))
        after = passing(b, own[b][0])
    for b in range(buckets):
        attn, lse = run_far(b, after)
        attns.append(attn)
        lses.append(lse)
        after = passing(buckets + 2 * b, lse)
        mids.append(run_mid(b, out, after))
        out = [mids[b][0]]
        after = passing(buckets + 2 * b + 1, mids[b][9])
    column = lambda i: [m[i] for m in mids]
    kept, sent = wgrad_call(
        places, devices, column(5), column(7), column(4), column(6), attns, column(8), column(9)
    )

    final_rows = HEADS // 4 * (6 * hd + 16)
    final_rows += -final_rows % (16 * lax.axis_size("batch") // 2)

    board = Board(places)
    big = board.start(sum_over_devices(kept, sent, groups))
    waiting = [sent]
    mine, returns = [], []
    sums = None
    for b in range(buckets):
        g, delta, branch = mids[b][2], mids[b][3], mids[b][1]
        args = (own[b][0], g, lses[b], delta, w_kv, b_kv, wq, branch)
        dx = {}
        last = final_rows if b + 1 == buckets else 0
        cut = max(1, n // 2) if b >= SPLIT_FROM else 0
        pieces = lambda i, dx=dx, cut=cut: (dx[0], i) if i < n - max(cut, 1) else (dx[1], i - (n - cut))
        if cut:
            there = held[b][n - 1 : cut - 1 : -1]
            dx[0], dq, sums = back_call(b, cut, n - 1, places, me, lengths, there, *args, None, sums, 0, waiting)
            returns.append(board.start(send_back(pieces, n)))
            waiting = board.tick([sums])
            there = held[b][cut - 1 :: -1]
            dx[1], own_part, sums = back_call(b, 0, cut - 1, places, me, lengths, there, *args, dq, sums, last, waiting)
            if not last:
                waiting = board.tick([sums])
        else:
            dx[0], own_part, sums = back_call(b, 0, n - 1, places, me, lengths, held[b][::-1], *args, None, sums, last, waiting)
            returns.append(board.start(send_back(pieces, n)))
            waiting = board.tick([sums])
        mine.append(own_part)
    small = sum_over_devices(*sums, groups, n > 1)
    small_first = Process(small)
    after = [sums[1]]
    whole, grads, done = [], None, set()
    alone = 2
    landed = lambda: [r.result for r in returns if r.result is not None]
    after = board.tick(after + landed())[:1] if board.active else after
    board.active.append(small_first)
    while board.active:
        sent = board.tick(landed() + after, [small_first] if alone > 0 else None)
        alone, after = alone - 1, sent[:1]
        ready = [b for b in range(buckets) if b not in done and returns[b].result is not None]
        if grads is None and big.result is not None:
            grads = big_call(places, *big.result, ff, sent)
            after = [grads[3]]
        elif ready:
            b = ready[0]
            whole = [tokens_call(b, buckets, mine[b], returns[b].result, whole, sent)]
            done.add(b)
            after = whole
    for b in range(buckets):
        if b not in done:
            whole = [tokens_call(b, buckets, mine[b], returns[b].result, whole, [])]
    grad_wq, grad_wk, grad_wv, bias = small_call(places, *small_first.result)
    grad_w_outer, grad_w_inner, grad_w_out, v = grads
    return (
        out[0], whole[0], grad_wq, grad_wk, grad_wv, grad_w_out, bias[0], bias[1], v[7],
        v[5], v[6], v[0], v[1], v[2], v[3],
        grad_w_inner, v[8 : 8 + ff // d].reshape(ff), grad_w_outer, v[4],
    )


def solution(mesh):
    rows = P("batch", "blk", None)
    in_specs = (rows, P("batch")) + (P(),) * 17 + (rows,)
    out_specs = (rows, rows) + (P(),) * 17
    return jax.shard_map(on_device, mesh=mesh, in_specs=in_specs, out_specs=out_specs, check_vma=False)
```

```python
import functools
import math

import jax
import jax.numpy as jnp
from jax import lax
from jax.experimental import pallas as pl
from jax.experimental.pallas import tpu as pltpu
from jax.sharding import PartitionSpec as P

HEADS = 8
F32 = jnp.float32
BF16 = jnp.bfloat16
FAR = -1e30
EPS = 1e-05
SPLIT_FROM = 1
LOG2E = math.log2(math.e)
LN2 = math.log(2.0)
GELU_C = math.sqrt(2.0 / math.pi)
GELU_K = 0.044715

VM = pl.BlockSpec(memory_space=pltpu.VMEM)
SM = pl.BlockSpec(memory_space=pltpu.SMEM)
ANY = pl.BlockSpec(memory_space=pl.ANY)
S = jax.ShapeDtypeStruct


def dot(a, b, dims):
    return lax.dot_general(a, b, (dims, ((), ())), preferred_element_type=F32)


def nn(a, b):
    return dot(a, b, ((1,), (0,)))


def nt(a, b):
    return dot(a, b, ((1,), (1,)))


def tn(a, b):
    return dot(a, b, ((0,), (0,)))


def params(mib=56):
    return pltpu.CompilerParams(vmem_limit_bytes=mib * 2**20)


def cost(flops, bytes_accessed):
    return pl.CostEstimate(flops=int(flops), bytes_accessed=int(bytes_accessed), transcendentals=0)


def head_size(features):
    return features // HEADS


def set_bias(bias, slot, me, length):
    rows = bias.shape[0]
    first = (me - slot) * rows
    partial = (slot == 0) | (first + rows > length)

    @pl.when(partial)
    def _():
        c = first + lax.broadcasted_iota(jnp.int32, bias.shape, 0)
        p = me * rows + lax.broadcasted_iota(jnp.int32, bias.shape, 1)
        bias[...] = jnp.where(c <= jnp.minimum(p, length - 1), 0.0, FAR)

    @pl.when(jnp.logical_not(partial))
    def _():
        bias[...] = jnp.zeros(bias.shape, F32)


def project_pair(w_kv, b_kv, x):
    kv = (nt(w_kv, x) + b_kv).astype(BF16)
    hd = kv.shape[0] // 4
    return [kv[:hd], kv[hd : 2 * hd]], [kv[2 * hd : 3 * hd], kv[3 * hd :]]


def attend_slot(x, q, w_kv, b_kv, bias, top_s, acc_s):
    pairs = w_kv.shape[0]
    rows = x.shape[0]

    def body(step, carry):
        for j in range(2):
            one_pair(step * 2 + j)
        return carry

    def one_pair(pair):
        ks, vs = project_pair(w_kv[pair], b_kv[pair], x[...])
        for i in range(2):
            h = pair * 2 + i
            logits = tn(ks[i], q[h]) + bias[...]
            old = top_s[h]
            top = jnp.maximum(jnp.max(logits, axis=0, keepdims=True), old)
            weights = jnp.exp2(logits - top).astype(BF16)
            v_one = jnp.concatenate([vs[i], jnp.ones((16, rows), BF16)], axis=0)
            acc_s[h] = nn(v_one, weights) + jnp.exp2(old - top) * acc_s[h]
            top_s[h] = top

    lax.fori_loop(0, pairs // 2, body, 0)


def own_kernel(bucket, ahead, me_ref, len_ref, x, wq, bq, w_kv, b_kv, *refs):
    more = refs[0]
    refs = refs[len(refs) - 4 - (ahead > 0) :]
    q_o, top_o, acc_o = refs[:3]
    bias = refs[-1]
    me = me_ref[0]
    length = len_ref[bucket]
    rows = x.shape[1]
    scale = head_size(x.shape[2]) ** -0.5 * LOG2E
    pairs = w_kv.shape[0]
    hd = q_o.shape[1]
    if ahead:
        refs[3][...] = more[0]

    def body(pair, carry):
        q = ((nt(wq[pair], x[0]) + bq[pair]) * scale).astype(BF16)
        q_o[2 * pair] = q[:hd]
        q_o[2 * pair + 1] = q[hd:]
        return carry

    lax.fori_loop(0, pairs, body, 0)
    top_o[...] = jnp.full(top_o.shape, FAR, F32)
    acc_o[...] = jnp.zeros(acc_o.shape, F32)

    @pl.when(me * rows < length)
    def _():
        set_bias(bias, 0, me, length)
        attend_slot(x.at[0], q_o, w_kv, b_kv, bias, top_o, acc_o)


def own_call(bucket, me, lengths, tokens, wq, bq, w_kv, b_kv, ahead, after):
    _, rows, d = tokens.shape
    hd = head_size(d)
    shapes = [S((HEADS, hd, rows), BF16), S((HEADS, 1, rows), F32), S((HEADS, hd + 16, rows), F32)]
    one = lambda b: pl.BlockSpec((1, rows, d), lambda i: (b, 0, 0))
    extra = [one(ahead)] if ahead else []
    shapes += [S((rows, d), BF16)] * len(extra)
    return pl.pallas_call(
        functools.partial(own_kernel, bucket, ahead),
        grid=(1,),
        out_shape=tuple(shapes),
        in_specs=[SM, SM, one(bucket)] + [VM] * 4 + extra + [ANY] * len(after),
        out_specs=(VM,) * len(shapes),
        scratch_shapes=[pltpu.VMEM((rows, rows), F32)],
        compiler_params=params(),
        cost_estimate=cost(8e9, 4e6),
        name=f"attend_own_{bucket}",
    )(me, lengths, tokens, wq, bq, w_kv, b_kv, *([tokens] if ahead else []), *after)


def far_kernel(bucket, count, me_ref, len_ref, *refs):
    xs = refs[:count]
    q, top_i, acc_i, w_kv, b_kv = refs[count : count + 5]
    out_o, lse_o, x_s, top_s, acc_s, bias = refs[len(refs) - 6 :]
    me = me_ref[0]
    length = len_ref[bucket]
    rows = xs[0].shape[0]
    hd = out_o.shape[1]
    top_s[...] = top_i[...]
    acc_s[...] = acc_i[...]
    for i in range(count):

        @pl.when(me > i)
        def _(i=i):
            x_s[i] = xs[i][...]

    def body(slot, carry):
        first = (me - slot) * rows

        @pl.when(first < length)
        def _():
            set_bias(bias, slot, me, length)
            attend_slot(x_s.at[slot - 1], q, w_kv, b_kv, bias, top_s, acc_s)

        return carry

    lax.fori_loop(1, jnp.minimum(me, count) + 1, body, 0)

    def finish(h, carry):
        total = acc_s[h, hd : hd + 1]
        out_o[h] = (acc_s[h, :hd] / total).astype(BF16)
        lse_o[h] = top_s[h] + jnp.log2(total)
        return carry

    lax.fori_loop(0, HEADS, finish, 0)


def far_call(bucket, me, lengths, xs, q, top, acc, w_kv, b_kv, after):
    rows, d = xs[0].shape
    hd = head_size(d)
    shapes = ((HEADS, hd, rows), (HEADS, 1, rows), (HEADS, hd + 16, rows))
    operands = [me, lengths, *xs, q, top, acc, w_kv, b_kv]
    specs = [SM, SM] + [VM] * (len(xs) + 5)
    out_shape = [S(shapes[0], BF16), S(shapes[1], F32)]
    return pl.pallas_call(
        functools.partial(far_kernel, bucket, len(xs)),
        grid=(1,),
        out_shape=tuple(out_shape),
        in_specs=specs + [ANY] * len(after),
        out_specs=(VM,) * len(out_shape),
        scratch_shapes=[
            pltpu.VMEM((len(xs), rows, d), BF16),
            pltpu.VMEM(shapes[1], F32),
            pltpu.VMEM(shapes[2], F32),
            pltpu.VMEM((rows, rows), F32),
        ],
        compiler_params=params(),
        cost_estimate=cost(18e9, 5e6),
        name=f"attend_far_{bucket}",
    )(*operands, *after)


def norm_stats(v):
    centered = v - jnp.mean(v, axis=-1, keepdims=True)
    r = lax.rsqrt(jnp.mean(centered * centered, axis=-1, keepdims=True) + EPS)
    return centered * r, r


def norm_grad(n, r, gain, upstream):
    gu = gain * upstream
    return r * (gu - jnp.mean(gu, axis=-1, keepdims=True) - n * jnp.mean(gu * n, axis=-1, keepdims=True))


def over_rows(v):
    return jnp.sum(v.astype(F32), axis=0, keepdims=True)


def mid_kernel(bucket, me_ref, len_ref, attn, x, cot, w_out, w_inner, w_outer, vecs, b_inner, *refs):
    (out_o, branch_o, g_o, delta_o, normed_o, active_o, ghid_o, gtwo_o, gb_o, sums_o,
     pre_s, n1_s, r1_s, dual_s, slope_s, acc_s,
     inner_s, outer_s, cot_s, normed_s, active_s, ghid_s, gtwo_s, sems) = refs[len(refs) - 24 :]
    copies_in = [
        pltpu.make_async_copy(a, b, sems.at[i])
        for i, (a, b) in enumerate([(w_inner, inner_s), (w_outer, outer_s), (cot.at[bucket], cot_s)])
    ]
    for copy in copies_in:
        copy.start()
    w_inner, w_outer, cot = inner_s, outer_s, cot_s
    copies_out = [
        pltpu.make_async_copy(a, b, sems.at[3 + i])
        for i, (a, b) in enumerate([(normed_s, normed_o), (active_s, active_o), (gtwo_s, gtwo_o), (ghid_s, ghid_o)])
    ]
    me = me_ref[0]
    length = len_ref[bucket]
    _, rows, d = out_o.shape
    ff = active_s.shape[1]
    up_step = min(512, ff)
    down_step = min(512, ff)
    block = min(256, rows)
    b_out, gain1, shift1, gain2, shift2, gain_f, shift_f, b_outer = (vecs[i : i + 1] for i in range(8))
    attn_t = attn[...].reshape(d, rows)
    pre_s[...] = tn(attn_t, w_out[...])

    def over_blocks(work):
        def body(i, carry):
            work(pl.ds(pl.multiple_of(i * block, block), block), i * block)
            return carry

        lax.fori_loop(0, rows // block, body, 0)

    def first_norm(at, _):
        pre = x[0, at].astype(F32) + (pre_s[at] + b_out)
        n1, r1 = norm_stats(pre)
        pre_s[at] = pre
        n1_s[at] = n1
        r1_s[at] = r1
        normed_s[at] = (n1 * gain1 + shift1).astype(BF16)

    over_blocks(first_norm)
    copies_out[0].start()
    copies_in[0].wait()
    copies_in[1].wait()
    acc_s[...] = jnp.zeros(acc_s.shape, F32)

    def lift(i):
        f = pl.ds(pl.multiple_of(i * up_step, up_step), up_step)
        return nn(normed_s[...], w_inner[:, f]) + b_inner[:, f]


    def up(i, carry):
        f = pl.ds(pl.multiple_of(i * up_step, up_step), up_step)
        h = lift(i)
        square = h * h
        t = jnp.tanh(h * (GELU_C + (GELU_C * GELU_K) * square))
        half = 0.5 + 0.5 * t
        active = (h * half).astype(BF16)
        active_s[:, f] = active
        slope_s[:, f] = half + (0.5 * h) * (1.0 - t * t) * (GELU_C + (3.0 * GELU_C * GELU_K) * square)
        acc_s[...] += nn(active, w_outer[f, :])
        return carry

    lax.fori_loop(0, ff // up_step, up, 0)
    copies_out[1].start()
    sums_o[...] = jnp.zeros(sums_o.shape, F32)
    copies_in[2].wait()

    def last_norms(at, start):
        branch_two = acc_s[at] + b_outer
        normed = n1_s[at] * gain1 + shift1
        n2, r2 = norm_stats(normed + branch_two)
        nf, rf = norm_stats(pre_s[at] + branch_two)
        out_o[0, at] = ((n2 * gain2 + shift2) + (nf * gain_f + shift_f)).astype(BF16)
        p = me * rows + start + lax.broadcasted_iota(jnp.int32, (block, 1), 0)
        g_out = jnp.where(p < length, cot[at].astype(F32), 0.0)
        g_dual = norm_grad(nf, rf, gain_f, g_out)
        g_two = norm_grad(n2, r2, gain2, g_out)
        g_branch_two = (g_two + g_dual).astype(BF16)
        gtwo_s[at] = g_branch_two
        dual_s[at] = g_dual
        acc_s[at] = g_two
        sums_o[0:1] += over_rows(g_out * n2)
        sums_o[1:2] += over_rows(g_out)
        sums_o[2:3] += over_rows(g_out * nf)
        sums_o[4:5] += over_rows(g_branch_two)

    over_blocks(last_norms)
    copies_out[2].start()
    sums_o[3:4] = sums_o[1:2]

    @pl.when(me * rows < length)
    def _():
        def down(i, carry):
            f = pl.ds(pl.multiple_of(i * down_step, down_step), down_step)
            g_hidden = (nt(gtwo_s[...], w_outer[f, :]) * slope_s[:, f]).astype(BF16)
            ghid_s[:, f] = g_hidden
            sums_o[pl.ds(8 + i, 1)] = over_rows(g_hidden)
            acc_s[...] += nt(g_hidden, w_inner[:, f])
            return carry

        lax.fori_loop(0, ff // down_step, down, 0)
        copies_out[3].start()

        def first_back(at, _):
            g_normed = acc_s[at]
            n1 = n1_s[at]
            g_branch = norm_grad(n1, r1_s[at], gain1, g_normed) + dual_s[at]
            branch_o[at] = g_branch
            g_b = g_branch.astype(BF16)
            gb_o[at] = g_b
            sums_o[5:6] += over_rows(g_normed * n1)
            sums_o[6:7] += over_rows(g_normed)
            sums_o[7:8] += over_rows(g_b)

        over_blocks(first_back)
        g_o[...] = nt(w_out[...], gb_o[...]).astype(BF16).reshape(g_o.shape)

        def head_delta(h, carry):
            delta_o[h] = jnp.sum(g_o[h].astype(F32) * attn[h].astype(F32), axis=0, keepdims=True)
            return carry

        lax.fori_loop(0, HEADS, head_delta, 0)

    @pl.when(me * rows >= length)
    def _():
        for ref in (branch_o, g_o, delta_o, ghid_s, gb_o):
            ref[...] = jnp.zeros(ref.shape, ref.dtype)
        copies_out[3].start()

    for copy in copies_out:
        copy.wait()


def mid_call(bucket, me, lengths, attn, tokens, cotangent, w_out, w_inner, w_outer, vecs, b_inner, out, after):
    buckets, rows, d = tokens.shape
    ff = w_inner.shape[1]
    hd = head_size(d)
    one = pl.BlockSpec((1, rows, d), lambda i: (bucket, 0, 0))
    return pl.pallas_call(
        functools.partial(mid_kernel, bucket),
        grid=(1,),
        out_shape=(
            S((buckets, rows, d), BF16),
            S((rows, d), F32),
            S((HEADS, hd, rows), BF16),
            S((HEADS, 1, rows), F32),
            S((rows, d), BF16),
            S((rows, ff), BF16),
            S((rows, ff), BF16),
            S((rows, d), BF16),
            S((rows, d), BF16),
            S((16, d), F32),
        ),
        in_specs=[SM, SM, VM, one, ANY, VM, ANY, ANY, VM, VM] + [ANY] * (len(out) + len(after)),
        out_specs=(one, VM, VM, VM, ANY, ANY, ANY, ANY, VM, VM),
        input_output_aliases={10: 0} if out else {},
        scratch_shapes=[
            pltpu.VMEM((rows, d), F32),
            pltpu.VMEM((rows, d), F32),
            pltpu.VMEM((rows, 1), F32),
            pltpu.VMEM((rows, d), F32),
            pltpu.VMEM((rows, ff), F32),
            pltpu.VMEM((rows, d), F32),
            pltpu.VMEM((d, ff), BF16),
            pltpu.VMEM((ff, d), BF16),
            pltpu.VMEM((rows, d), BF16),
            pltpu.VMEM((rows, d), BF16),
            pltpu.VMEM((rows, ff), BF16),
            pltpu.VMEM((rows, ff), BF16),
            pltpu.VMEM((rows, d), BF16),
            pltpu.SemaphoreType.DMA((7,)),
        ],
        compiler_params=params(),
        cost_estimate=cost(12e9, 14e6),
        name=f"feed_forward_{bucket}",
    )(me, lengths, attn, tokens, cotangent, w_out, w_inner, w_outer, vecs, b_inner, *out, *after)


def wgrad_job(step, half, core):
    return step % half + jnp.where(step < half, 1 - core, core) * half


def rows_of(refs):
    return jnp.concatenate([r[...] for r in refs], axis=0)


def wgrad_kernel(buckets, count, half, places, *refs):
    groups = [refs[i * buckets : (i + 1) * buckets] for i in range(7)]
    active, g_two, normed, g_hidden, attn, g_b, sums = groups
    kept_o, sent_o = refs[7 * buckets :]
    step = pl.program_id(0)
    job = wgrad_job(step, half, places[0])

    def put(value):
        @pl.when(step < half)
        def _():
            sent_o[...] = value

        @pl.when(step >= half)
        def _():
            kept_o[...] = value

    @pl.when(job < count)
    def _():
        put(tn(rows_of(active), rows_of(g_two)).astype(BF16))

    @pl.when((job >= count) & (job < 2 * count))
    def _():
        put(tn(rows_of(normed), rows_of(g_hidden)).astype(BF16))

    @pl.when(job == 2 * count)
    def _():
        put(sum(nn(a[...], g[...]) for a, g in zip(attn, g_b)).astype(BF16))

    @pl.when(job > 2 * count)
    def _():
        put(jnp.zeros(kept_o.shape, BF16))

    @pl.when(job == 2 * count + 1)
    def _():
        value = sum(s[...] for s in sums).astype(BF16)

        @pl.when(step < half)
        def _():
            sent_o[:16] = value

        @pl.when(step >= half)
        def _():
            kept_o[:16] = value


def wgrad_call(places, devices, active, g_two, normed, g_hidden, attn, g_b, sums):
    buckets = len(active)
    rows, ff = active[0].shape
    d = g_two[0].shape[1]
    count = ff // d
    half = count + 1
    while 2 * half * d % (16 * devices):
        half += 1
    clip = lambda v, top: jnp.minimum(jnp.maximum(v, 0), top)
    job = lambda j, p: wgrad_job(j, half, p[0])
    full = pl.BlockSpec((rows, d), lambda j, p: (0, 0))
    tall = pl.BlockSpec((d, rows), lambda j, p: (0, 0))
    active_spec = pl.BlockSpec((rows, d), lambda j, p: (0, clip(job(j, p), count - 1)))
    hid_spec = pl.BlockSpec((rows, d), lambda j, p: (0, clip(job(j, p) - count, count - 1)))
    attn2 = [a.reshape(d, rows) for a in attn]
    return pl.pallas_call(
        functools.partial(wgrad_kernel, buckets, count, half),
        grid_spec=pltpu.PrefetchScalarGridSpec(
            num_scalar_prefetch=1,
            grid=(2 * half,),
            in_specs=[active_spec] * buckets + [full] * buckets + [full] * buckets + [hid_spec] * buckets
            + [tall] * buckets + [full] * buckets + [pl.BlockSpec((16, d), lambda j, p: (0, 0))] * buckets,
            out_specs=(
                pl.BlockSpec((d, d), lambda j, p: (jnp.maximum(j - half, 0), 0)),
                pl.BlockSpec((d, d), lambda j, p: (jnp.minimum(j, half - 1), 0)),
            ),
        ),
        out_shape=(S((half * d, d), BF16),) * 2,
        compiler_params=params(),
        cost_estimate=cost(buckets * 5e9, 20e6),
        name="weight_gradients",
    )(places, *active, *g_two, *normed, *g_hidden, *attn2, *g_b, *sums)


def attend_back(x, q, g, w_kv, b_kv, lse, delta, bias, dq_s, kv_s, dkv_s):
    pairs, width, d = w_kv.shape
    hd = width // 4
    rows = x.shape[0]
    block = 2 * width

    def project(i, carry):
        at = pl.ds(pl.multiple_of(i * block, block), block)
        w = w_kv[pl.ds(2 * i, 2)].reshape(block, d)
        kv_s[at] = (nt(w, x[...]) + b_kv[pl.ds(2 * i, 2)].reshape(block, 1)).astype(BF16)
        return carry

    lax.fori_loop(0, pairs // 2, project, 0)

    def body(step, carry):
        for j in range(2):
            one_pair(step * 2 + j)
        return carry

    def one_pair(pair):
        base = pl.multiple_of(pair * width, width)
        for i in range(2):
            h = pair * 2 + i
            at_k = pl.ds(base + i * hd, hd)
            at_v = pl.ds(base + (2 + i) * hd, hd)
            k = kv_s[at_k]
            q_t, g_t = q[h], g[h]
            probs = jnp.exp2(tn(k, q_t) + bias[...] - lse[h])
            g_probs = tn(kv_s[at_v], g_t)
            g_logits = (probs * (g_probs - delta[h])).astype(BF16)
            dkv_s[at_v] = nt(g_t, probs.astype(BF16)).astype(BF16)
            dkv_s[at_k] = (nt(q_t, g_logits) * LN2).astype(BF16)
            dq_s[h] += nn(k, g_logits)

    lax.fori_loop(0, pairs // 2, body, 0)


def back_kernel(bucket, low, high, fresh, first, final, places, me_ref, len_ref, *refs):
    count = high - low + 1
    refs = list(refs)
    take = lambda n: [refs.pop(0) for _ in range(n)]
    xs = take(count)
    q, g, lse, delta, w_kv, b_kv = take(6)
    sems = refs.pop()
    wq, branch = take(2) if low == 0 else (None, None)
    dq_i = None if fresh else take(1)[0]
    sums_i = None if first else take(1)[0]
    x_s, kv_s, dkv_s, dq_s, dx_s, bias, *late = refs[len(refs) - 6 - (low == 0) - (not first) :]
    refs = refs[: len(refs) - 6 - len(late)]
    refs = refs[len(refs) - 2 - final - (high > 0) :]
    dx_o = refs.pop(0) if high > 0 else None
    last_o, *sums_o = refs
    me = me_ref[0]
    length = len_ref[bucket]
    rows, d = xs[0].shape
    hd = g.shape[1]
    live = me * rows < length
    dq_s[...] = jnp.zeros(dq_s.shape, F32) if fresh else dq_i[...]
    rows_in = [
        pltpu.make_async_copy(xs[i], x_s.at[pl.ds(i * rows, rows)], sems.at[i]) for i in range(count)
    ]
    late_in = [
        pltpu.make_async_copy(source, to, sems.at[count + j])
        for j, (source, to) in enumerate(zip([branch] * (low == 0) + [sums_i] * (not first), late))
    ]
    for copy in rows_in + late_in:
        copy.start()

    def take_rows(i):
        for j in range(count):

            @pl.when(i == j)
            def _(j=j):
                rows_in[j].wait()

    def dx_out(i):
        return pltpu.make_async_copy(dx_s.at[i], dx_o.at[i], sems.at[count + 2 + i])

    def body(i, carry):
        slot = high - i
        at = pl.ds(pl.multiple_of(i * rows, rows), rows)
        active = live & (me >= slot)
        take_rows(i)

        @pl.when(active)
        def _():
            set_bias(bias, slot, me, length)
            attend_back(x_s.at[at], q, g, w_kv, b_kv, lse, delta, bias, dq_s, kv_s, dkv_s.at[:, at])

        @pl.when(active & (slot > 0))
        def _():
            dx_s[i] = tn(dkv_s[:, at], w_kv[...].reshape(2 * d, d)).astype(BF16)

        @pl.when(jnp.logical_not(active))
        def _():
            dkv_s[:, at] = jnp.zeros((2 * d, rows), BF16)

        @pl.when(jnp.logical_not(active) & (slot > 0))
        def _():
            dx_s[i] = jnp.zeros((rows, d), BF16)

        @pl.when(slot > 0)
        def _():
            dx_out(i).start()

        return carry

    lax.fori_loop(0, count, body, 0)
    pairs = HEADS // 2
    dq = (dq_s[...] * hd**-0.5).astype(BF16).reshape(d, rows)
    here = slice((count - 1) * rows, count * rows)
    for copy in late_in:
        copy.wait()
    if low == 0:
        last_o[...] = late[0][...]

        @pl.when(live)
        def _():
            last_o[...] += tn(dkv_s[:, here], w_kv[...].reshape(2 * d, d)) + tn(dq, wq[...])
    else:
        last_o[...] = dq_s[...]

    half = HEADS // 4
    ones = jnp.ones((8, count * rows), BF16)

    def add(pair, carry):
        at = pl.ds(pl.multiple_of(pair * 4 * hd, 4 * hd), 4 * hd)
        dkv = dkv_s[at, :]
        parts = [None, nn(dkv, x_s[...]), None]
        bias_sums = [nt(ones, dkv), jnp.zeros((8, d - 4 * hd), F32)]
        if low == 0:
            dq_pair = (dq_s[pl.ds(2 * pair, 2)] * hd**-0.5).astype(BF16).reshape(2 * hd, rows)
            parts[0] = nn(dq_pair, x_s[here])
            bias_sums[1:] = [nt(ones[:, :rows], dq_pair), jnp.zeros((8, d - 6 * hd), F32)]
        else:
            parts[0] = jnp.zeros((2 * hd, d), F32)
        parts[2] = jnp.concatenate([jnp.concatenate(bias_sums, axis=1), jnp.zeros((8, d), F32)])
        value = jnp.concatenate(parts, axis=0)
        if not first:
            value = value + late[-1][pair].astype(F32)
        value = value.astype(BF16)
        if final:
            kept = pair // half == places[0]
            to = pl.ds(pl.multiple_of((pair % half) * 6 * hd, 6 * hd), 6 * hd)
            to_bias = pl.ds(pl.multiple_of(half * 6 * hd + (pair % half) * 16, 16), 16)

            def put(ref):
                ref[to] = value[: 6 * hd]
                ref[to_bias] = value[6 * hd :]

            @pl.when(kept)
            def _():
                put(sums_o[0])

            @pl.when(jnp.logical_not(kept))
            def _():
                put(sums_o[1])
        else:
            sums_o[0][pair] = value
        return carry

    if final:
        used = half * (6 * hd + 16)
        for ref in sums_o:
            if used < ref.shape[0]:
                ref[used:] = jnp.zeros((ref.shape[0] - used, d), BF16)
    lax.fori_loop(0, pairs, add, 0)
    for i in range(count - (low == 0)):
        dx_out(i).wait()


def back_call(
    bucket, low, high, places, me, lengths, xs, q, g, lse, delta, w_kv, b_kv, wq, branch, dq, sums, final, after
):
    rows, d = xs[0].shape
    hd = head_size(d)
    own = low == 0
    fresh = dq is None
    far = high - max(low, 1) + 1
    operands = [places, me, lengths, *xs, q, g, lse, delta, w_kv, b_kv]
    specs = [SM] * 3 + [ANY] * len(xs) + [VM] * 6
    late = []
    if own:
        operands += [wq.reshape(d, d), branch]
        specs += [VM, ANY]
        late.append(branch)
    if not fresh:
        operands.append(dq)
        specs.append(VM)
    if sums is not None:
        operands.append(sums)
        specs.append(ANY)
        late.append(sums)
    sums_shape = (HEADS // 2, 6 * hd + 16, d)
    out_shape = [S((far, rows, d), BF16)] if far else []
    out_shape += [S((rows, d), F32) if own else S((HEADS, hd, rows), F32)]
    out_shape += [S((final, d), BF16)] * 2 if final else [S(sums_shape, BF16)]
    outs = pl.pallas_call(
        functools.partial(back_kernel, bucket, low, high, fresh, sums is None, final > 0),
        grid=(1,),
        out_shape=tuple(out_shape),
        in_specs=specs + [ANY] * len(after),
        out_specs=((ANY,) if far else ()) + (VM,) * (len(out_shape) - (far > 0)),
        scratch_shapes=[
            pltpu.VMEM((len(xs) * rows, d), BF16),
            pltpu.VMEM((2 * d, rows), BF16),
            pltpu.VMEM((2 * d, len(xs) * rows), BF16),
            pltpu.VMEM((HEADS, hd, rows), F32),
            pltpu.VMEM((max(far, 1), rows, d), BF16),
            pltpu.VMEM((rows, rows), F32),
            *[pltpu.VMEM(a.shape, a.dtype) for a in late],
            pltpu.SemaphoreType.DMA((2 * len(xs) + 2,)),
        ],
        compiler_params=params(36),
        cost_estimate=cost(10e9 * len(xs), 14e6),
        name=f"attend_back_{bucket}_{high}",
    )(*operands, *after)
    last = len(out_shape) - (3 if final else 2)
    return (outs[0] if far else None), outs[last], (outs[last + 1 :] if final else outs[-1])


def step_call(name, places, jobs, after):
    operands, specs, shapes, bodies = [places], [SM], [], []
    for job_in, job_specs, job_out, body in jobs:
        bodies.append((len(job_in), len(job_out), body))
        operands += job_in
        specs += job_specs
        shapes += job_out
    first_out = len(operands) + len(after)

    def kernel(places_ref, *refs):
        at_in, at_out = 0, first_out - 1
        for n_in, n_out, body in bodies:
            body(places_ref, *refs[at_in : at_in + n_in], *refs[at_out : at_out + n_out])
            at_in += n_in
            at_out += n_out

    outs = pl.pallas_call(
        kernel,
        grid=(1,),
        out_shape=tuple(shapes),
        in_specs=specs + [ANY] * len(after),
        out_specs=(VM,) * len(shapes),
        compiler_params=params(16),
        cost_estimate=cost(2e9, 4e6),
        name=name,
    )(*operands, *after)
    found = []
    for _, n_out, _ in bodies:
        found.append(outs[:n_out])
        outs = outs[n_out:]
    return found


def gate(arrays, after):
    outs = pl.pallas_call(
        lambda *refs: None,
        out_shape=tuple(S(a.shape, a.dtype) for a in arrays),
        in_specs=[ANY] * (len(arrays) + len(after)),
        out_specs=(ANY,) * len(arrays),
        input_output_aliases={i: i for i in range(len(arrays))},
        name="gate",
    )(*arrays, *after)
    return list(outs)


class Group:
    def __init__(self, index, axis, low, high):
        self.index, self.axis, self.low, self.count = index, axis, low, 1 << (high - low)
        self.place = (lax.axis_index(axis) >> low) & (self.count - 1)

    def swap(self, value, mask):
        size = lax.axis_size(self.axis)
        return lax.ppermute(value, self.axis, [(i, i ^ (mask << self.low)) for i in range(size)])


def part_rows(place, mask, size):
    return pl.ds(pl.multiple_of((place ^ mask) * size, size), size)


def total(kept, got, at):
    values = [r[at].astype(F32) for r in [kept, *got]]
    while len(values) > 1:
        values = [a + b for a, b in zip(values[::2], values[1::2])]
    return values[0].astype(BF16)


def split_job(kept, got, group):
    rows, d = kept.shape
    count = group.count if group else 1
    size = rows // count

    def body(places, kept, *refs):
        arrived, outs = refs[: len(got)], refs[len(got) :]
        for m in range(count):
            at = part_rows(places[group.index], m, size) if group else slice(None)
            outs[m][...] = total(kept, arrived, at)

    return [kept, *got], [VM] * (1 + len(got)), [S((size, d), BF16)] * count, body


def join_job(part, got, group):
    size, d = part.shape

    def body(places, *refs):
        for m in range(group.count):
            refs[-1][part_rows(places[group.index], m, size)] = refs[m][...]

    return [part, *got], [VM] * (1 + len(got)), [S((size * group.count, d), BF16)], body


def message_job(dx, at, carry):
    _, rows, d = dx.shape
    more = [] if carry is None else [carry]

    def body(places, dx, *refs):
        if more:
            refs[-1][...] = (dx[0].astype(F32) + refs[0][...].astype(F32)).astype(BF16)
        else:
            refs[-1][...] = dx[0]

    specs = [pl.BlockSpec((1, rows, d), lambda i: (at, 0, 0))] + [VM] * len(more)
    return [dx, *more], specs, [S((rows, d), BF16)], body


def sum_over_devices(kept, sent, groups, full=False):
    first, *rest = groups
    got = [first.swap(sent, 1)]
    scatter = rest[:-1] if full else rest
    for group in scatter:
        kept, *shards = yield split_job(kept, got, group)
        got = [group.swap(s, m + 1) for m, s in enumerate(shards)]
    (part,) = yield split_job(kept, got, None)
    if full and rest:
        got = [rest[-1].swap(part, m) for m in range(1, rest[-1].count)]
        (part,) = yield split_job(part, got, None)
    for group in reversed(scatter):
        got = [group.swap(part, m) for m in range(1, group.count)]
        (part,) = yield join_job(part, got, group)
    return part, first.swap(part, 1)


def send_back(pieces, n):
    carry = None
    for i, slot in enumerate(range(n - 1, 0, -1)):
        (message,) = yield message_job(*pieces(i), carry)
        carry = lax.ppermute(message, "blk", [(j, j - 1) for j in range(slot, n)])
    return carry


class Process:
    def __init__(self, steps):
        self.steps, self.result = steps, None
        self.job = next(steps)

    def advance(self, outs):
        try:
            self.job = self.steps.send(outs)
        except StopIteration as end:
            self.job, self.result = None, end.value


class Board:
    def __init__(self, places):
        self.places, self.active, self.ticks = places, [], 0

    def start(self, steps):
        self.active.append(Process(steps))
        return self.active[-1]

    def tick(self, after, only=None):
        self.ticks += 1
        now = self.active if only is None else only
        outs = step_call(f"step_{self.ticks}", self.places, [p.job for p in now], after)
        for p, o in zip(list(now), outs):
            p.advance(o)
        self.active = [p for p in self.active if p.job is not None]
        return [o for group in outs for o in group]


def big_kernel(ff, places, mine, got, *refs):
    outer_o, inner_o, out_o, vec_o = refs[len(refs) - 4 :]
    half, d = mine.shape
    count = ff // d
    for own_half in range(2):

        @pl.when(places[0] == own_half)
        def _(own_half=own_half):
            for i in range(2 * half // d):
                src = mine if i // (half // d) == own_half else got
                at = (i % (half // d)) * d
                value = src[at : at + d]
                if i < count:
                    outer_o[i * d : i * d + d] = value.astype(F32)
                elif i < 2 * count:
                    inner_o[:, (i - count) * d : (i - count) * d + d] = value.astype(F32)
                elif i == 2 * count:
                    out_o[...] = value.astype(F32)
                elif i == 2 * count + 1:
                    vec_o[...] = value[:16].astype(F32)


def big_call(places, mine, got, ff, after):
    d = mine.shape[1]
    shapes = (S((ff, d), F32), S((d, ff), F32), S((d, d), F32), S((16, d), F32))
    return pl.pallas_call(
        functools.partial(big_kernel, ff),
        grid=(1,),
        out_shape=shapes,
        in_specs=[SM, VM, VM] + [ANY] * len(after),
        out_specs=(VM,) * 4,
        compiler_params=params(24),
        cost_estimate=cost(5e9, 14e6),
        name="feed_forward_sums",
    )(places, mine, got, *after)


def small_kernel(places, mine, got, *refs):
    weights, bias_o = refs[len(refs) - 4 : len(refs) - 1], refs[-1]
    d = weights[0].shape[0]
    hd = head_size(d)
    half = HEADS // 4
    bias_o[...] = jnp.zeros(bias_o.shape, F32)
    for own_half in range(2):

        @pl.when(places[0] == own_half)
        def _(own_half=own_half):
            for pair in range(HEADS // 2):
                src = mine if pair // half == own_half else got
                at = (pair % half) * 6 * hd
                at_bias = half * 6 * hd + (pair % half) * 16
                lanes = slice(2 * hd * pair, 2 * hd * pair + 2 * hd)
                for k in range(3):
                    rows = src[at + 2 * hd * k : at + 2 * hd * k + 2 * hd].astype(F32)
                    weights[k][:, lanes] = rows.T
                bias = src[at_bias : at_bias + 16].astype(F32)
                bias_o[0:1, lanes] = bias[:1, 4 * hd : 6 * hd]
                bias_o[1:2, lanes] = bias[:1, 2 * hd : 4 * hd]


def small_call(places, mine, got):
    d = mine.shape[1]
    return pl.pallas_call(
        small_kernel,
        grid=(1,),
        out_shape=(S((d, d), F32),) * 3 + (S((8, d), F32),),
        in_specs=[SM, VM, VM],
        out_specs=(VM,) * 4,
        compiler_params=params(16),
        cost_estimate=cost(2e9, 5e6),
        name="attention_sums",
    )(places, mine, got)


def tokens_kernel(mine, carry, *refs):
    refs[-1][0] = mine[...] + carry[...].astype(F32)


def tokens_call(bucket, buckets, mine, carry, whole, after):
    rows, d = mine.shape
    return pl.pallas_call(
        tokens_kernel,
        grid=(1,),
        out_shape=S((buckets, rows, d), F32),
        in_specs=[VM, VM] + [ANY] * (len(whole) + len(after)),
        out_specs=pl.BlockSpec((1, rows, d), lambda i: (bucket, 0, 0)),
        input_output_aliases={2: 0} if whole else {},
        compiler_params=params(16),
        cost_estimate=cost(2e9, 3e6),
        name=f"token_gradients_{bucket}",
    )(mine, carry, *whole, *after)


def on_device(
    tokens, lengths, w_query, w_key, w_value, w_out, b_query, b_value, b_out, norm1_gain, norm1_bias,
    norm2_gain, norm2_bias, final_gain, final_bias, w_inner, b_inner, w_outer, b_outer, cotangent,
):
    buckets, rows, d = tokens.shape
    ff = w_inner.shape[1]
    hd = head_size(d)
    pairs = HEADS // 2
    n = lax.axis_size("blk")
    me = lax.axis_index("blk").astype(jnp.int32).reshape(1)
    bits = lambda axis: (lax.axis_size(axis) - 1).bit_length()
    groups = [Group(0, "batch", 0, 1), Group(1, "batch", 1, bits("batch")), Group(2, "blk", 0, bits("blk"))]
    places = jnp.stack([g.place for g in groups]).astype(jnp.int32)
    devices = math.prod(g.count for g in groups)
    groups = [groups[0]] + [g for g in groups[1:] if g.count > 1]

    paired = lambda w: w.T.reshape(pairs, 2 * hd, d)
    wq = paired(w_query)
    bq = b_query.reshape(pairs, 2 * hd, 1)
    w_kv = jnp.concatenate([paired(w_key), paired(w_value)], axis=1)
    b_v = b_value.reshape(pairs, 2 * hd, 1)
    b_kv = jnp.concatenate([jnp.zeros_like(b_v), b_v], axis=1)
    vecs = jnp.stack([b_out, norm1_gain, norm1_bias, norm2_gain, norm2_bias, final_gain, final_bias, b_outer])
    b_in = b_inner.reshape(1, ff)

    def hop(value, slot):
        return lax.ppermute(value, "blk", [(i, i + 1) for i in range(slot - 1, n - 1)])

    run_own = lambda b, after: own_call(b, me, lengths, tokens, wq, bq, w_kv, b_kv, (b + 1) % buckets, after)
    run_far = lambda b, after: far_call(b, me, lengths, held[b][1:], own[b][0], own[b][1], own[b][2], w_kv, b_kv, after)
    run_mid = lambda b, out, after: mid_call(
        b, me, lengths, attns[b], tokens, cotangent, w_out, w_inner, w_outer, vecs, b_in, out, after
    )
    held = [[tokens[b]] for b in range(buckets)]
    own, mids, attns, lses, out = [], [], [], [], []
    moving = {}
    if n == 4 and buckets == 3:
        plan = [
            ([(0, 1)], [(0, 2), (1, 1)]),
            ([(0, 2), (1, 1)], [(0, 3)]),
            ([(0, 3)], [(1, 2), (2, 1)]),
            ([(1, 2)], [(1, 3)]),
            ([(1, 3), (2, 1)], [(2, 2)]),
            ([(2, 2)], [(2, 3)]),
            ([(2, 3)], []),
        ]
    else:
        plan = []
        for b in range(buckets):
            for slot in range(1, n):
                source = held[b][-1]
                held[b].append(hop(source, slot))
    if plan:
        moving[0, 1] = hop(tokens[0], 1)

    def passing(kernel, last):
        if kernel >= len(plan):
            return [last]
        arrived, next_hops = plan[kernel]
        fresh = [b for b, slot in next_hops if slot == 1]
        held_on = [(b, slot - 1) for b, slot in next_hops if slot > 1 and (b, slot - 1) not in arrived]
        values = [moving.pop(k) for k in arrived] + [held[b][slot] for b, slot in held_on]
        passed = gate(values + [own[b - 1][3] for b in fresh], [last])
        for k, value in zip(arrived, passed):
            held[k[0]].append(value)
        for (b, slot), value in zip(held_on, passed[len(arrived) :]):
            held[b][slot] = value
        starts = dict(zip(fresh, passed[len(values) :]))
        for b, slot in next_hops:
            moving[b, slot] = hop(starts[b] if slot == 1 else held[b][slot - 1], slot)
        return passed[:1]

    after = [vecs, b_in]
    for b in range(buckets):
        own.append(run_own(b, after))
        after = passing(b, own[b][0])
    for b in range(buckets):
        attn, lse = run_far(b, after)
        attns.append(attn)
        lses.append(lse)
        after = passing(buckets + 2 * b, lse)
        mids.append(run_mid(b, out, after))
        out = [mids[b][0]]
        after = passing(buckets + 2 * b + 1, mids[b][9])
    column = lambda i: [m[i] for m in mids]
    kept, sent = wgrad_call(
        places, devices, column(5), column(7), column(4), column(6), attns, column(8), column(9)
    )

    final_rows = HEADS // 4 * (6 * hd + 16)
    final_rows += -final_rows % (16 * lax.axis_size("batch") // 2)

    board = Board(places)
    big = board.start(sum_over_devices(kept, sent, groups))
    waiting = [sent]
    mine, returns = [], []
    sums = None
    for b in range(buckets):
        g, delta, branch = mids[b][2], mids[b][3], mids[b][1]
        args = (own[b][0], g, lses[b], delta, w_kv, b_kv, wq, branch)
        dx = {}
        last = final_rows if b + 1 == buckets else 0
        cut = max(1, n // 2) if b >= SPLIT_FROM else 0
        pieces = lambda i, dx=dx, cut=cut: (dx[0], i) if i < n - max(cut, 1) else (dx[1], i - (n - cut))
        if cut:
            there = held[b][n - 1 : cut - 1 : -1]
            dx[0], dq, sums = back_call(b, cut, n - 1, places, me, lengths, there, *args, None, sums, 0, waiting)
            returns.append(board.start(send_back(pieces, n)))
            waiting = board.tick([sums])
            there = held[b][cut - 1 :: -1]
            dx[1], own_part, sums = back_call(b, 0, cut - 1, places, me, lengths, there, *args, dq, sums, last, waiting)
            if not last:
                waiting = board.tick([sums])
        else:
            dx[0], own_part, sums = back_call(b, 0, n - 1, places, me, lengths, held[b][::-1], *args, None, sums, last, waiting)
            returns.append(board.start(send_back(pieces, n)))
            waiting = board.tick([sums])
        mine.append(own_part)
    small = sum_over_devices(*sums, groups, n > 1)
    small_first = Process(small)
    after = [sums[1]]
    whole, grads, done = [], None, set()
    alone = 2
    landed = lambda: [r.result for r in returns if r.result is not None]
    after = board.tick(after + landed())[:1] if board.active else after
    board.active.append(small_first)
    while board.active:
        sent = board.tick(landed() + after, [small_first] if alone > 0 else None)
        alone, after = alone - 1, sent[:1]
        ready = [b for b in range(buckets) if b not in done and returns[b].result is not None]
        if grads is None and big.result is not None:
            grads = big_call(places, *big.result, ff, sent)
            after = [grads[3]]
        elif ready:
            b = ready[0]
            whole = [tokens_call(b, buckets, mine[b], returns[b].result, whole, sent)]
            done.add(b)
            after = whole
    for b in range(buckets):
        if b not in done:
            whole = [tokens_call(b, buckets, mine[b], returns[b].result, whole, [])]
    grad_wq, grad_wk, grad_wv, bias = small_call(places, *small_first.result)
    grad_w_outer, grad_w_inner, grad_w_out, v = grads
    return (
        out[0], whole[0], grad_wq, grad_wk, grad_wv, grad_w_out, bias[0], bias[1], v[7],
        v[5], v[6], v[0], v[1], v[2], v[3],
        grad_w_inner, v[8 : 8 + ff // d].reshape(ff), grad_w_outer, v[4],
    )


def solution(mesh):
    rows = P("batch", "blk", None)
    in_specs = (rows, P("batch")) + (P(),) * 17 + (rows,)
    out_specs = (rows, rows) + (P(),) * 17
    return jax.shard_map(on_device, mesh=mesh, in_specs=in_specs, out_specs=out_specs, check_vma=False)
```

```python
import functools
import math

import jax
import jax.numpy as jnp
from jax import lax
from jax.experimental import pallas as pl
from jax.experimental.pallas import tpu as pltpu
from jax.sharding import PartitionSpec as P

HEADS = 8
F32 = jnp.float32
BF16 = jnp.bfloat16
FAR = -1e30
EPS = 1e-05
SPLIT_FROM = 0
LOG2E = math.log2(math.e)
LN2 = math.log(2.0)
GELU_C = math.sqrt(2.0 / math.pi)
GELU_K = 0.044715

VM = pl.BlockSpec(memory_space=pltpu.VMEM)
SM = pl.BlockSpec(memory_space=pltpu.SMEM)
ANY = pl.BlockSpec(memory_space=pl.ANY)
S = jax.ShapeDtypeStruct


def dot(a, b, dims):
    return lax.dot_general(a, b, (dims, ((), ())), preferred_element_type=F32)


def nn(a, b):
    return dot(a, b, ((1,), (0,)))


def nt(a, b):
    return dot(a, b, ((1,), (1,)))


def tn(a, b):
    return dot(a, b, ((0,), (0,)))


def params(mib=56):
    return pltpu.CompilerParams(vmem_limit_bytes=mib * 2**20)


def cost(flops, bytes_accessed):
    return pl.CostEstimate(flops=int(flops), bytes_accessed=int(bytes_accessed), transcendentals=0)


def head_size(features):
    return features // HEADS


def set_bias(bias, slot, me, length):
    rows = bias.shape[0]
    first = (me - slot) * rows
    partial = (slot == 0) | (first + rows > length)

    @pl.when(partial)
    def _():
        c = first + lax.broadcasted_iota(jnp.int32, bias.shape, 0)
        p = me * rows + lax.broadcasted_iota(jnp.int32, bias.shape, 1)
        bias[...] = jnp.where(c <= jnp.minimum(p, length - 1), 0.0, FAR)

    @pl.when(jnp.logical_not(partial))
    def _():
        bias[...] = jnp.zeros(bias.shape, F32)


def project_pair(w_kv, b_kv, x):
    kv = (nt(w_kv, x) + b_kv).astype(BF16)
    hd = kv.shape[0] // 4
    return [kv[:hd], kv[hd : 2 * hd]], [kv[2 * hd : 3 * hd], kv[3 * hd :]]


def attend_slot(x, q, w_kv, b_kv, bias, top_s, acc_s):
    pairs = w_kv.shape[0]
    rows = x.shape[0]

    def body(step, carry):
        for j in range(2):
            one_pair(step * 2 + j)
        return carry

    def one_pair(pair):
        ks, vs = project_pair(w_kv[pair], b_kv[pair], x[...])
        for i in range(2):
            h = pair * 2 + i
            logits = tn(ks[i], q[h]) + bias[...]
            old = top_s[h]
            top = jnp.maximum(jnp.max(logits, axis=0, keepdims=True), old)
            weights = jnp.exp2(logits - top).astype(BF16)
            v_one = jnp.concatenate([vs[i], jnp.ones((16, rows), BF16)], axis=0)
            acc_s[h] = nn(v_one, weights) + jnp.exp2(old - top) * acc_s[h]
            top_s[h] = top

    lax.fori_loop(0, pairs // 2, body, 0)


def own_kernel(bucket, ahead, me_ref, len_ref, x, wq, bq, w_kv, b_kv, *refs):
    more = refs[0]
    refs = refs[len(refs) - 4 - (ahead > 0) :]
    q_o, top_o, acc_o = refs[:3]
    bias = refs[-1]
    me = me_ref[0]
    length = len_ref[bucket]
    rows = x.shape[1]
    scale = head_size(x.shape[2]) ** -0.5 * LOG2E
    pairs = w_kv.shape[0]
    hd = q_o.shape[1]
    if ahead:
        refs[3][...] = more[0]

    def body(pair, carry):
        q = ((nt(wq[pair], x[0]) + bq[pair]) * scale).astype(BF16)
        q_o[2 * pair] = q[:hd]
        q_o[2 * pair + 1] = q[hd:]
        return carry

    lax.fori_loop(0, pairs, body, 0)
    top_o[...] = jnp.full(top_o.shape, FAR, F32)
    acc_o[...] = jnp.zeros(acc_o.shape, F32)

    @pl.when(me * rows < length)
    def _():
        set_bias(bias, 0, me, length)
        attend_slot(x.at[0], q_o, w_kv, b_kv, bias, top_o, acc_o)


def own_call(bucket, me, lengths, tokens, wq, bq, w_kv, b_kv, ahead, after):
    _, rows, d = tokens.shape
    hd = head_size(d)
    shapes = [S((HEADS, hd, rows), BF16), S((HEADS, 1, rows), F32), S((HEADS, hd + 16, rows), F32)]
    one = lambda b: pl.BlockSpec((1, rows, d), lambda i: (b, 0, 0))
    extra = [one(ahead)] if ahead else []
    shapes += [S((rows, d), BF16)] * len(extra)
    return pl.pallas_call(
        functools.partial(own_kernel, bucket, ahead),
        grid=(1,),
        out_shape=tuple(shapes),
        in_specs=[SM, SM, one(bucket)] + [VM] * 4 + extra + [ANY] * len(after),
        out_specs=(VM,) * len(shapes),
        scratch_shapes=[pltpu.VMEM((rows, rows), F32)],
        compiler_params=params(),
        cost_estimate=cost(8e9, 4e6),
        name=f"attend_own_{bucket}",
    )(me, lengths, tokens, wq, bq, w_kv, b_kv, *([tokens] if ahead else []), *after)


def far_kernel(bucket, count, me_ref, len_ref, *refs):
    xs = refs[:count]
    q, top_i, acc_i, w_kv, b_kv = refs[count : count + 5]
    out_o, lse_o, x_s, top_s, acc_s, bias = refs[len(refs) - 6 :]
    me = me_ref[0]
    length = len_ref[bucket]
    rows = xs[0].shape[0]
    hd = out_o.shape[1]
    top_s[...] = top_i[...]
    acc_s[...] = acc_i[...]
    for i in range(count):

        @pl.when(me > i)
        def _(i=i):
            x_s[i] = xs[i][...]

    def body(slot, carry):
        first = (me - slot) * rows

        @pl.when(first < length)
        def _():
            set_bias(bias, slot, me, length)
            attend_slot(x_s.at[slot - 1], q, w_kv, b_kv, bias, top_s, acc_s)

        return carry

    lax.fori_loop(1, jnp.minimum(me, count) + 1, body, 0)

    def finish(h, carry):
        total = acc_s[h, hd : hd + 1]
        out_o[h] = (acc_s[h, :hd] / total).astype(BF16)
        lse_o[h] = top_s[h] + jnp.log2(total)
        return carry

    lax.fori_loop(0, HEADS, finish, 0)


def far_call(bucket, me, lengths, xs, q, top, acc, w_kv, b_kv, after):
    rows, d = xs[0].shape
    hd = head_size(d)
    shapes = ((HEADS, hd, rows), (HEADS, 1, rows), (HEADS, hd + 16, rows))
    operands = [me, lengths, *xs, q, top, acc, w_kv, b_kv]
    specs = [SM, SM] + [VM] * (len(xs) + 5)
    out_shape = [S(shapes[0], BF16), S(shapes[1], F32)]
    return pl.pallas_call(
        functools.partial(far_kernel, bucket, len(xs)),
        grid=(1,),
        out_shape=tuple(out_shape),
        in_specs=specs + [ANY] * len(after),
        out_specs=(VM,) * len(out_shape),
        scratch_shapes=[
            pltpu.VMEM((len(xs), rows, d), BF16),
            pltpu.VMEM(shapes[1], F32),
            pltpu.VMEM(shapes[2], F32),
            pltpu.VMEM((rows, rows), F32),
        ],
        compiler_params=params(),
        cost_estimate=cost(18e9, 5e6),
        name=f"attend_far_{bucket}",
    )(*operands, *after)


def norm_stats(v):
    centered = v - jnp.mean(v, axis=-1, keepdims=True)
    r = lax.rsqrt(jnp.mean(centered * centered, axis=-1, keepdims=True) + EPS)
    return centered * r, r


def norm_grad(n, r, gain, upstream):
    gu = gain * upstream
    return r * (gu - jnp.mean(gu, axis=-1, keepdims=True) - n * jnp.mean(gu * n, axis=-1, keepdims=True))


def over_rows(v):
    return jnp.sum(v.astype(F32), axis=0, keepdims=True)


def mid_kernel(bucket, me_ref, len_ref, attn, x, cot, w_out, w_inner, w_outer, vecs, b_inner, *refs):
    (out_o, branch_o, g_o, delta_o, normed_o, active_o, ghid_o, gtwo_o, gb_o, sums_o,
     pre_s, n1_s, r1_s, dual_s, slope_s, acc_s,
     inner_s, outer_s, cot_s, normed_s, active_s, ghid_s, gtwo_s, sems) = refs[len(refs) - 24 :]
    copies_in = [
        pltpu.make_async_copy(a, b, sems.at[i])
        for i, (a, b) in enumerate([(w_inner, inner_s), (w_outer, outer_s), (cot.at[bucket], cot_s)])
    ]
    for copy in copies_in:
        copy.start()
    w_inner, w_outer, cot = inner_s, outer_s, cot_s
    copies_out = [
        pltpu.make_async_copy(a, b, sems.at[3 + i])
        for i, (a, b) in enumerate([(normed_s, normed_o), (active_s, active_o), (gtwo_s, gtwo_o), (ghid_s, ghid_o)])
    ]
    me = me_ref[0]
    length = len_ref[bucket]
    _, rows, d = out_o.shape
    ff = active_s.shape[1]
    up_step = min(512, ff)
    down_step = min(512, ff)
    block = min(256, rows)
    b_out, gain1, shift1, gain2, shift2, gain_f, shift_f, b_outer = (vecs[i : i + 1] for i in range(8))
    attn_t = attn[...].reshape(d, rows)
    pre_s[...] = tn(attn_t, w_out[...])

    def over_blocks(work):
        def body(i, carry):
            work(pl.ds(pl.multiple_of(i * block, block), block), i * block)
            return carry

        lax.fori_loop(0, rows // block, body, 0)

    def first_norm(at, _):
        pre = x[0, at].astype(F32) + (pre_s[at] + b_out)
        n1, r1 = norm_stats(pre)
        pre_s[at] = pre
        n1_s[at] = n1
        r1_s[at] = r1
        normed_s[at] = (n1 * gain1 + shift1).astype(BF16)

    over_blocks(first_norm)
    copies_out[0].start()
    copies_in[0].wait()
    copies_in[1].wait()
    acc_s[...] = jnp.zeros(acc_s.shape, F32)

    def lift(i):
        f = pl.ds(pl.multiple_of(i * up_step, up_step), up_step)
        return nn(normed_s[...], w_inner[:, f]) + b_inner[:, f]


    def up(i, carry):
        f = pl.ds(pl.multiple_of(i * up_step, up_step), up_step)
        h = lift(i)
        square = h * h
        t = jnp.tanh(h * (GELU_C + (GELU_C * GELU_K) * square))
        half = 0.5 + 0.5 * t
        active = (h * half).astype(BF16)
        active_s[:, f] = active
        slope_s[:, f] = half + (0.5 * h) * (1.0 - t * t) * (GELU_C + (3.0 * GELU_C * GELU_K) * square)
        acc_s[...] += nn(active, w_outer[f, :])
        return carry

    lax.fori_loop(0, ff // up_step, up, 0)
    copies_out[1].start()
    sums_o[...] = jnp.zeros(sums_o.shape, F32)
    copies_in[2].wait()

    def last_norms(at, start):
        branch_two = acc_s[at] + b_outer
        normed = n1_s[at] * gain1 + shift1
        n2, r2 = norm_stats(normed + branch_two)
        nf, rf = norm_stats(pre_s[at] + branch_two)
        out_o[0, at] = ((n2 * gain2 + shift2) + (nf * gain_f + shift_f)).astype(BF16)
        p = me * rows + start + lax.broadcasted_iota(jnp.int32, (block, 1), 0)
        g_out = jnp.where(p < length, cot[at].astype(F32), 0.0)
        g_dual = norm_grad(nf, rf, gain_f, g_out)
        g_two = norm_grad(n2, r2, gain2, g_out)
        g_branch_two = (g_two + g_dual).astype(BF16)
        gtwo_s[at] = g_branch_two
        dual_s[at] = g_dual
        acc_s[at] = g_two
        sums_o[0:1] += over_rows(g_out * n2)
        sums_o[1:2] += over_rows(g_out)
        sums_o[2:3] += over_rows(g_out * nf)
        sums_o[4:5] += over_rows(g_branch_two)

    over_blocks(last_norms)
    copies_out[2].start()
    sums_o[3:4] = sums_o[1:2]

    @pl.when(me * rows < length)
    def _():
        def down(i, carry):
            f = pl.ds(pl.multiple_of(i * down_step, down_step), down_step)
            g_hidden = (nt(gtwo_s[...], w_outer[f, :]) * slope_s[:, f]).astype(BF16)
            ghid_s[:, f] = g_hidden
            sums_o[pl.ds(8 + i, 1)] = over_rows(g_hidden)
            acc_s[...] += nt(g_hidden, w_inner[:, f])
            return carry

        lax.fori_loop(0, ff // down_step, down, 0)
        copies_out[3].start()

        def first_back(at, _):
            g_normed = acc_s[at]
            n1 = n1_s[at]
            g_branch = norm_grad(n1, r1_s[at], gain1, g_normed) + dual_s[at]
            branch_o[at] = g_branch
            g_b = g_branch.astype(BF16)
            gb_o[at] = g_b
            sums_o[5:6] += over_rows(g_normed * n1)
            sums_o[6:7] += over_rows(g_normed)
            sums_o[7:8] += over_rows(g_b)

        over_blocks(first_back)
        g_o[...] = nt(w_out[...], gb_o[...]).astype(BF16).reshape(g_o.shape)

        def head_delta(h, carry):
            delta_o[h] = jnp.sum(g_o[h].astype(F32) * attn[h].astype(F32), axis=0, keepdims=True)
            return carry

        lax.fori_loop(0, HEADS, head_delta, 0)

    @pl.when(me * rows >= length)
    def _():
        for ref in (branch_o, g_o, delta_o, ghid_s, gb_o):
            ref[...] = jnp.zeros(ref.shape, ref.dtype)
        copies_out[3].start()

    for copy in copies_out:
        copy.wait()


def mid_call(bucket, me, lengths, attn, tokens, cotangent, w_out, w_inner, w_outer, vecs, b_inner, out, after):
    buckets, rows, d = tokens.shape
    ff = w_inner.shape[1]
    hd = head_size(d)
    one = pl.BlockSpec((1, rows, d), lambda i: (bucket, 0, 0))
    return pl.pallas_call(
        functools.partial(mid_kernel, bucket),
        grid=(1,),
        out_shape=(
            S((buckets, rows, d), BF16),
            S((rows, d), F32),
            S((HEADS, hd, rows), BF16),
            S((HEADS, 1, rows), F32),
            S((rows, d), BF16),
            S((rows, ff), BF16),
            S((rows, ff), BF16),
            S((rows, d), BF16),
            S((rows, d), BF16),
            S((16, d), F32),
        ),
        in_specs=[SM, SM, VM, one, ANY, VM, ANY, ANY, VM, VM] + [ANY] * (len(out) + len(after)),
        out_specs=(one, VM, VM, VM, ANY, ANY, ANY, ANY, VM, VM),
        input_output_aliases={10: 0} if out else {},
        scratch_shapes=[
            pltpu.VMEM((rows, d), F32),
            pltpu.VMEM((rows, d), F32),
            pltpu.VMEM((rows, 1), F32),
            pltpu.VMEM((rows, d), F32),
            pltpu.VMEM((rows, ff), F32),
            pltpu.VMEM((rows, d), F32),
            pltpu.VMEM((d, ff), BF16),
            pltpu.VMEM((ff, d), BF16),
            pltpu.VMEM((rows, d), BF16),
            pltpu.VMEM((rows, d), BF16),
            pltpu.VMEM((rows, ff), BF16),
            pltpu.VMEM((rows, ff), BF16),
            pltpu.VMEM((rows, d), BF16),
            pltpu.SemaphoreType.DMA((7,)),
        ],
        compiler_params=params(),
        cost_estimate=cost(12e9, 14e6),
        name=f"feed_forward_{bucket}",
    )(me, lengths, attn, tokens, cotangent, w_out, w_inner, w_outer, vecs, b_inner, *out, *after)


def wgrad_job(step, half, core):
    return step % half + jnp.where(step < half, 1 - core, core) * half


def rows_of(refs):
    return jnp.concatenate([r[...] for r in refs], axis=0)


def wgrad_kernel(buckets, count, half, places, *refs):
    groups = [refs[i * buckets : (i + 1) * buckets] for i in range(7)]
    active, g_two, normed, g_hidden, attn, g_b, sums = groups
    kept_o, sent_o = refs[7 * buckets :]
    step = pl.program_id(0)
    job = wgrad_job(step, half, places[0])

    def put(value):
        @pl.when(step < half)
        def _():
            sent_o[...] = value

        @pl.when(step >= half)
        def _():
            kept_o[...] = value

    @pl.when(job < count)
    def _():
        put(tn(rows_of(active), rows_of(g_two)).astype(BF16))

    @pl.when((job >= count) & (job < 2 * count))
    def _():
        put(tn(rows_of(normed), rows_of(g_hidden)).astype(BF16))

    @pl.when(job == 2 * count)
    def _():
        put(sum(nn(a[...], g[...]) for a, g in zip(attn, g_b)).astype(BF16))

    @pl.when(job > 2 * count)
    def _():
        put(jnp.zeros(kept_o.shape, BF16))

    @pl.when(job == 2 * count + 1)
    def _():
        value = sum(s[...] for s in sums).astype(BF16)

        @pl.when(step < half)
        def _():
            sent_o[:16] = value

        @pl.when(step >= half)
        def _():
            kept_o[:16] = value


def wgrad_call(places, devices, active, g_two, normed, g_hidden, attn, g_b, sums):
    buckets = len(active)
    rows, ff = active[0].shape
    d = g_two[0].shape[1]
    count = ff // d
    half = count + 1
    while 2 * half * d % (16 * devices):
        half += 1
    clip = lambda v, top: jnp.minimum(jnp.maximum(v, 0), top)
    job = lambda j, p: wgrad_job(j, half, p[0])
    full = pl.BlockSpec((rows, d), lambda j, p: (0, 0))
    tall = pl.BlockSpec((d, rows), lambda j, p: (0, 0))
    active_spec = pl.BlockSpec((rows, d), lambda j, p: (0, clip(job(j, p), count - 1)))
    hid_spec = pl.BlockSpec((rows, d), lambda j, p: (0, clip(job(j, p) - count, count - 1)))
    attn2 = [a.reshape(d, rows) for a in attn]
    return pl.pallas_call(
        functools.partial(wgrad_kernel, buckets, count, half),
        grid_spec=pltpu.PrefetchScalarGridSpec(
            num_scalar_prefetch=1,
            grid=(2 * half,),
            in_specs=[active_spec] * buckets + [full] * buckets + [full] * buckets + [hid_spec] * buckets
            + [tall] * buckets + [full] * buckets + [pl.BlockSpec((16, d), lambda j, p: (0, 0))] * buckets,
            out_specs=(
                pl.BlockSpec((d, d), lambda j, p: (jnp.maximum(j - half, 0), 0)),
                pl.BlockSpec((d, d), lambda j, p: (jnp.minimum(j, half - 1), 0)),
            ),
        ),
        out_shape=(S((half * d, d), BF16),) * 2,
        compiler_params=params(),
        cost_estimate=cost(buckets * 5e9, 20e6),
        name="weight_gradients",
    )(places, *active, *g_two, *normed, *g_hidden, *attn2, *g_b, *sums)


def attend_back(x, q, g, w_kv, b_kv, lse, delta, bias, dq_s, kv_s, dkv_s):
    pairs, width, d = w_kv.shape
    hd = width // 4
    rows = x.shape[0]
    block = 2 * width

    def project(i, carry):
        at = pl.ds(pl.multiple_of(i * block, block), block)
        w = w_kv[pl.ds(2 * i, 2)].reshape(block, d)
        kv_s[at] = (nt(w, x[...]) + b_kv[pl.ds(2 * i, 2)].reshape(block, 1)).astype(BF16)
        return carry

    lax.fori_loop(0, pairs // 2, project, 0)

    def body(step, carry):
        for j in range(2):
            one_pair(step * 2 + j)
        return carry

    def one_pair(pair):
        base = pl.multiple_of(pair * width, width)
        for i in range(2):
            h = pair * 2 + i
            at_k = pl.ds(base + i * hd, hd)
            at_v = pl.ds(base + (2 + i) * hd, hd)
            k = kv_s[at_k]
            q_t, g_t = q[h], g[h]
            probs = jnp.exp2(tn(k, q_t) + bias[...] - lse[h])
            g_probs = tn(kv_s[at_v], g_t)
            g_logits = (probs * (g_probs - delta[h])).astype(BF16)
            dkv_s[at_v] = nt(g_t, probs.astype(BF16)).astype(BF16)
            dkv_s[at_k] = (nt(q_t, g_logits) * LN2).astype(BF16)
            dq_s[h] += nn(k, g_logits)

    lax.fori_loop(0, pairs // 2, body, 0)


def back_kernel(bucket, low, high, fresh, first, final, places, me_ref, len_ref, *refs):
    count = high - low + 1
    refs = list(refs)
    take = lambda n: [refs.pop(0) for _ in range(n)]
    xs = take(count)
    q, g, lse, delta, w_kv, b_kv = take(6)
    sems = refs.pop()
    wq, branch = take(2) if low == 0 else (None, None)
    dq_i = None if fresh else take(1)[0]
    sums_i = None if first else take(1)[0]
    x_s, kv_s, dkv_s, dq_s, dx_s, bias, *late = refs[len(refs) - 6 - (low == 0) - (not first) :]
    refs = refs[: len(refs) - 6 - len(late)]
    refs = refs[len(refs) - 2 - final - (high > 0) :]
    dx_o = refs.pop(0) if high > 0 else None
    last_o, *sums_o = refs
    me = me_ref[0]
    length = len_ref[bucket]
    rows, d = xs[0].shape
    hd = g.shape[1]
    live = me * rows < length
    dq_s[...] = jnp.zeros(dq_s.shape, F32) if fresh else dq_i[...]
    rows_in = [
        pltpu.make_async_copy(xs[i], x_s.at[pl.ds(i * rows, rows)], sems.at[i]) for i in range(count)
    ]
    late_in = [
        pltpu.make_async_copy(source, to, sems.at[count + j])
        for j, (source, to) in enumerate(zip([branch] * (low == 0) + [sums_i] * (not first), late))
    ]
    for copy in rows_in + late_in:
        copy.start()

    def take_rows(i):
        for j in range(count):

            @pl.when(i == j)
            def _(j=j):
                rows_in[j].wait()

    def dx_out(i):
        return pltpu.make_async_copy(dx_s.at[i], dx_o.at[i], sems.at[count + 2 + i])

    def body(i, carry):
        slot = high - i
        at = pl.ds(pl.multiple_of(i * rows, rows), rows)
        active = live & (me >= slot)
        take_rows(i)

        @pl.when(active)
        def _():
            set_bias(bias, slot, me, length)
            attend_back(x_s.at[at], q, g, w_kv, b_kv, lse, delta, bias, dq_s, kv_s, dkv_s.at[:, at])

        @pl.when(active & (slot > 0))
        def _():
            dx_s[i] = tn(dkv_s[:, at], w_kv[...].reshape(2 * d, d)).astype(BF16)

        @pl.when(jnp.logical_not(active))
        def _():
            dkv_s[:, at] = jnp.zeros((2 * d, rows), BF16)

        @pl.when(jnp.logical_not(active) & (slot > 0))
        def _():
            dx_s[i] = jnp.zeros((rows, d), BF16)

        @pl.when(slot > 0)
        def _():
            dx_out(i).start()

        return carry

    lax.fori_loop(0, count, body, 0)
    pairs = HEADS // 2
    dq = (dq_s[...] * hd**-0.5).astype(BF16).reshape(d, rows)
    here = slice((count - 1) * rows, count * rows)
    for copy in late_in:
        copy.wait()
    if low == 0:
        last_o[...] = late[0][...]

        @pl.when(live)
        def _():
            last_o[...] += tn(dkv_s[:, here], w_kv[...].reshape(2 * d, d)) + tn(dq, wq[...])
    else:
        last_o[...] = dq_s[...]

    half = HEADS // 4
    ones = jnp.ones((8, count * rows), BF16)

    def add(pair, carry):
        at = pl.ds(pl.multiple_of(pair * 4 * hd, 4 * hd), 4 * hd)
        dkv = dkv_s[at, :]
        parts = [None, nn(dkv, x_s[...]), None]
        bias_sums = [nt(ones, dkv), jnp.zeros((8, d - 4 * hd), F32)]
        if low == 0:
            dq_pair = (dq_s[pl.ds(2 * pair, 2)] * hd**-0.5).astype(BF16).reshape(2 * hd, rows)
            parts[0] = nn(dq_pair, x_s[here])
            bias_sums[1:] = [nt(ones[:, :rows], dq_pair), jnp.zeros((8, d - 6 * hd), F32)]
        else:
            parts[0] = jnp.zeros((2 * hd, d), F32)
        parts[2] = jnp.concatenate([jnp.concatenate(bias_sums, axis=1), jnp.zeros((8, d), F32)])
        value = jnp.concatenate(parts, axis=0)
        if not first:
            value = value + late[-1][pair].astype(F32)
        value = value.astype(BF16)
        if final:
            kept = pair // half == places[0]
            to = pl.ds(pl.multiple_of((pair % half) * 6 * hd, 6 * hd), 6 * hd)
            to_bias = pl.ds(pl.multiple_of(half * 6 * hd + (pair % half) * 16, 16), 16)

            def put(ref):
                ref[to] = value[: 6 * hd]
                ref[to_bias] = value[6 * hd :]

            @pl.when(kept)
            def _():
                put(sums_o[0])

            @pl.when(jnp.logical_not(kept))
            def _():
                put(sums_o[1])
        else:
            sums_o[0][pair] = value
        return carry

    if final:
        used = half * (6 * hd + 16)
        for ref in sums_o:
            if used < ref.shape[0]:
                ref[used:] = jnp.zeros((ref.shape[0] - used, d), BF16)
    lax.fori_loop(0, pairs, add, 0)
    for i in range(count - (low == 0)):
        dx_out(i).wait()


def back_call(
    bucket, low, high, places, me, lengths, xs, q, g, lse, delta, w_kv, b_kv, wq, branch, dq, sums, final, after
):
    rows, d = xs[0].shape
    hd = head_size(d)
    own = low == 0
    fresh = dq is None
    far = high - max(low, 1) + 1
    operands = [places, me, lengths, *xs, q, g, lse, delta, w_kv, b_kv]
    specs = [SM] * 3 + [ANY] * len(xs) + [VM] * 6
    late = []
    if own:
        operands += [wq.reshape(d, d), branch]
        specs += [VM, ANY]
        late.append(branch)
    if not fresh:
        operands.append(dq)
        specs.append(VM)
    if sums is not None:
        operands.append(sums)
        specs.append(ANY)
        late.append(sums)
    sums_shape = (HEADS // 2, 6 * hd + 16, d)
    out_shape = [S((far, rows, d), BF16)] if far else []
    out_shape += [S((rows, d), F32) if own else S((HEADS, hd, rows), F32)]
    out_shape += [S((final, d), BF16)] * 2 if final else [S(sums_shape, BF16)]
    outs = pl.pallas_call(
        functools.partial(back_kernel, bucket, low, high, fresh, sums is None, final > 0),
        grid=(1,),
        out_shape=tuple(out_shape),
        in_specs=specs + [ANY] * len(after),
        out_specs=((ANY,) if far else ()) + (VM,) * (len(out_shape) - (far > 0)),
        scratch_shapes=[
            pltpu.VMEM((len(xs) * rows, d), BF16),
            pltpu.VMEM((2 * d, rows), BF16),
            pltpu.VMEM((2 * d, len(xs) * rows), BF16),
            pltpu.VMEM((HEADS, hd, rows), F32),
            pltpu.VMEM((max(far, 1), rows, d), BF16),
            pltpu.VMEM((rows, rows), F32),
            *[pltpu.VMEM(a.shape, a.dtype) for a in late],
            pltpu.SemaphoreType.DMA((2 * len(xs) + 2,)),
        ],
        compiler_params=params(36),
        cost_estimate=cost(10e9 * len(xs), 14e6),
        name=f"attend_back_{bucket}_{high}",
    )(*operands, *after)
    last = len(out_shape) - (3 if final else 2)
    return (outs[0] if far else None), outs[last], (outs[last + 1 :] if final else outs[-1])


def step_call(name, places, jobs, after):
    operands, specs, shapes, bodies = [places], [SM], [], []
    for job_in, job_specs, job_out, body in jobs:
        bodies.append((len(job_in), len(job_out), body))
        operands += job_in
        specs += job_specs
        shapes += job_out
    first_out = len(operands) + len(after)

    def kernel(places_ref, *refs):
        at_in, at_out = 0, first_out - 1
        for n_in, n_out, body in bodies:
            body(places_ref, *refs[at_in : at_in + n_in], *refs[at_out : at_out + n_out])
            at_in += n_in
            at_out += n_out

    outs = pl.pallas_call(
        kernel,
        grid=(1,),
        out_shape=tuple(shapes),
        in_specs=specs + [ANY] * len(after),
        out_specs=(VM,) * len(shapes),
        compiler_params=params(16),
        cost_estimate=cost(2e9, 4e6),
        name=name,
    )(*operands, *after)
    found = []
    for _, n_out, _ in bodies:
        found.append(outs[:n_out])
        outs = outs[n_out:]
    return found


def gate(arrays, after):
    outs = pl.pallas_call(
        lambda *refs: None,
        out_shape=tuple(S(a.shape, a.dtype) for a in arrays),
        in_specs=[ANY] * (len(arrays) + len(after)),
        out_specs=(ANY,) * len(arrays),
        input_output_aliases={i: i for i in range(len(arrays))},
        name="gate",
    )(*arrays, *after)
    return list(outs)


class Group:
    def __init__(self, index, axis, low, high):
        self.index, self.axis, self.low, self.count = index, axis, low, 1 << (high - low)
        self.place = (lax.axis_index(axis) >> low) & (self.count - 1)

    def swap(self, value, mask):
        size = lax.axis_size(self.axis)
        return lax.ppermute(value, self.axis, [(i, i ^ (mask << self.low)) for i in range(size)])


def part_rows(place, mask, size):
    return pl.ds(pl.multiple_of((place ^ mask) * size, size), size)


def total(kept, got, at):
    values = [r[at].astype(F32) for r in [kept, *got]]
    while len(values) > 1:
        values = [a + b for a, b in zip(values[::2], values[1::2])]
    return values[0].astype(BF16)


def split_job(kept, got, group):
    rows, d = kept.shape
    count = group.count if group else 1
    size = rows // count

    def body(places, kept, *refs):
        arrived, outs = refs[: len(got)], refs[len(got) :]
        for m in range(count):
            at = part_rows(places[group.index], m, size) if group else slice(None)
            outs[m][...] = total(kept, arrived, at)

    return [kept, *got], [VM] * (1 + len(got)), [S((size, d), BF16)] * count, body


def join_job(part, got, group):
    size, d = part.shape

    def body(places, *refs):
        for m in range(group.count):
            refs[-1][part_rows(places[group.index], m, size)] = refs[m][...]

    return [part, *got], [VM] * (1 + len(got)), [S((size * group.count, d), BF16)], body


def message_job(dx, at, carry):
    _, rows, d = dx.shape
    more = [] if carry is None else [carry]

    def body(places, dx, *refs):
        if more:
            refs[-1][...] = (dx[0].astype(F32) + refs[0][...].astype(F32)).astype(BF16)
        else:
            refs[-1][...] = dx[0]

    specs = [pl.BlockSpec((1, rows, d), lambda i: (at, 0, 0))] + [VM] * len(more)
    return [dx, *more], specs, [S((rows, d), BF16)], body


def sum_over_devices(kept, sent, groups, full=False):
    first, *rest = groups
    got = [first.swap(sent, 1)]
    scatter = rest[:-1] if full else rest
    for group in scatter:
        kept, *shards = yield split_job(kept, got, group)
        got = [group.swap(s, m + 1) for m, s in enumerate(shards)]
    (part,) = yield split_job(kept, got, None)
    if full and rest:
        got = [rest[-1].swap(part, m) for m in range(1, rest[-1].count)]
        (part,) = yield split_job(part, got, None)
    for group in reversed(scatter):
        got = [group.swap(part, m) for m in range(1, group.count)]
        (part,) = yield join_job(part, got, group)
    return part, first.swap(part, 1)


def send_back(pieces, n):
    carry = None
    for i, slot in enumerate(range(n - 1, 0, -1)):
        (message,) = yield message_job(*pieces(i), carry)
        carry = lax.ppermute(message, "blk", [(j, j - 1) for j in range(slot, n)])
    return carry


class Process:
    def __init__(self, steps):
        self.steps, self.result = steps, None
        self.job = next(steps)

    def advance(self, outs):
        try:
            self.job = self.steps.send(outs)
        except StopIteration as end:
            self.job, self.result = None, end.value


class Board:
    def __init__(self, places):
        self.places, self.active, self.ticks = places, [], 0

    def start(self, steps):
        self.active.append(Process(steps))
        return self.active[-1]

    def tick(self, after, only=None):
        self.ticks += 1
        now = self.active if only is None else only
        outs = step_call(f"step_{self.ticks}", self.places, [p.job for p in now], after)
        for p, o in zip(list(now), outs):
            p.advance(o)
        self.active = [p for p in self.active if p.job is not None]
        return [o for group in outs for o in group]


def big_kernel(ff, places, mine, got, *refs):
    outer_o, inner_o, out_o, vec_o = refs[len(refs) - 4 :]
    half, d = mine.shape
    count = ff // d
    for own_half in range(2):

        @pl.when(places[0] == own_half)
        def _(own_half=own_half):
            for i in range(2 * half // d):
                src = mine if i // (half // d) == own_half else got
                at = (i % (half // d)) * d
                value = src[at : at + d]
                if i < count:
                    outer_o[i * d : i * d + d] = value.astype(F32)
                elif i < 2 * count:
                    inner_o[:, (i - count) * d : (i - count) * d + d] = value.astype(F32)
                elif i == 2 * count:
                    out_o[...] = value.astype(F32)
                elif i == 2 * count + 1:
                    vec_o[...] = value[:16].astype(F32)


def big_call(places, mine, got, ff, after):
    d = mine.shape[1]
    shapes = (S((ff, d), F32), S((d, ff), F32), S((d, d), F32), S((16, d), F32))
    return pl.pallas_call(
        functools.partial(big_kernel, ff),
        grid=(1,),
        out_shape=shapes,
        in_specs=[SM, VM, VM] + [ANY] * len(after),
        out_specs=(VM,) * 4,
        compiler_params=params(24),
        cost_estimate=cost(5e9, 14e6),
        name="feed_forward_sums",
    )(places, mine, got, *after)


def small_kernel(places, mine, got, *refs):
    weights, bias_o = refs[len(refs) - 4 : len(refs) - 1], refs[-1]
    d = weights[0].shape[0]
    hd = head_size(d)
    half = HEADS // 4
    bias_o[...] = jnp.zeros(bias_o.shape, F32)
    for own_half in range(2):

        @pl.when(places[0] == own_half)
        def _(own_half=own_half):
            for pair in range(HEADS // 2):
                src = mine if pair // half == own_half else got
                at = (pair % half) * 6 * hd
                at_bias = half * 6 * hd + (pair % half) * 16
                lanes = slice(2 * hd * pair, 2 * hd * pair + 2 * hd)
                for k in range(3):
                    rows = src[at + 2 * hd * k : at + 2 * hd * k + 2 * hd].astype(F32)
                    weights[k][:, lanes] = rows.T
                bias = src[at_bias : at_bias + 16].astype(F32)
                bias_o[0:1, lanes] = bias[:1, 4 * hd : 6 * hd]
                bias_o[1:2, lanes] = bias[:1, 2 * hd : 4 * hd]


def small_call(places, mine, got):
    d = mine.shape[1]
    return pl.pallas_call(
        small_kernel,
        grid=(1,),
        out_shape=(S((d, d), F32),) * 3 + (S((8, d), F32),),
        in_specs=[SM, VM, VM],
        out_specs=(VM,) * 4,
        compiler_params=params(16),
        cost_estimate=cost(2e9, 5e6),
        name="attention_sums",
    )(places, mine, got)


def tokens_kernel(mine, carry, *refs):
    refs[-1][0] = mine[...] + carry[...].astype(F32)


def tokens_call(bucket, buckets, mine, carry, whole, after):
    rows, d = mine.shape
    return pl.pallas_call(
        tokens_kernel,
        grid=(1,),
        out_shape=S((buckets, rows, d), F32),
        in_specs=[VM, VM] + [ANY] * (len(whole) + len(after)),
        out_specs=pl.BlockSpec((1, rows, d), lambda i: (bucket, 0, 0)),
        input_output_aliases={2: 0} if whole else {},
        compiler_params=params(16),
        cost_estimate=cost(2e9, 3e6),
        name=f"token_gradients_{bucket}",
    )(mine, carry, *whole, *after)


def on_device(
    tokens, lengths, w_query, w_key, w_value, w_out, b_query, b_value, b_out, norm1_gain, norm1_bias,
    norm2_gain, norm2_bias, final_gain, final_bias, w_inner, b_inner, w_outer, b_outer, cotangent,
):
    buckets, rows, d = tokens.shape
    ff = w_inner.shape[1]
    hd = head_size(d)
    pairs = HEADS // 2
    n = lax.axis_size("blk")
    me = lax.axis_index("blk").astype(jnp.int32).reshape(1)
    bits = lambda axis: (lax.axis_size(axis) - 1).bit_length()
    groups = [Group(0, "batch", 0, 1), Group(1, "batch", 1, bits("batch")), Group(2, "blk", 0, bits("blk"))]
    places = jnp.stack([g.place for g in groups]).astype(jnp.int32)
    devices = math.prod(g.count for g in groups)
    groups = [groups[0]] + [g for g in groups[1:] if g.count > 1]

    paired = lambda w: w.T.reshape(pairs, 2 * hd, d)
    wq = paired(w_query)
    bq = b_query.reshape(pairs, 2 * hd, 1)
    w_kv = jnp.concatenate([paired(w_key), paired(w_value)], axis=1)
    b_v = b_value.reshape(pairs, 2 * hd, 1)
    b_kv = jnp.concatenate([jnp.zeros_like(b_v), b_v], axis=1)
    vecs = jnp.stack([b_out, norm1_gain, norm1_bias, norm2_gain, norm2_bias, final_gain, final_bias, b_outer])
    b_in = b_inner.reshape(1, ff)

    def hop(value, slot):
        return lax.ppermute(value, "blk", [(i, i + 1) for i in range(slot - 1, n - 1)])

    run_own = lambda b, after: own_call(b, me, lengths, tokens, wq, bq, w_kv, b_kv, (b + 1) % buckets, after)
    run_far = lambda b, after: far_call(b, me, lengths, held[b][1:], own[b][0], own[b][1], own[b][2], w_kv, b_kv, after)
    run_mid = lambda b, out, after: mid_call(
        b, me, lengths, attns[b], tokens, cotangent, w_out, w_inner, w_outer, vecs, b_in, out, after
    )
    held = [[tokens[b]] for b in range(buckets)]
    own, mids, attns, lses, out = [], [], [], [], []
    moving = {}
    if n == 4 and buckets == 3:
        plan = [
            ([(0, 1)], [(0, 2), (1, 1)]),
            ([(0, 2), (1, 1)], [(0, 3)]),
            ([(0, 3)], [(1, 2), (2, 1)]),
            ([(1, 2)], [(1, 3)]),
            ([(1, 3), (2, 1)], [(2, 2)]),
            ([(2, 2)], [(2, 3)]),
            ([(2, 3)], []),
        ]
    else:
        plan = []
        for b in range(buckets):
            for slot in range(1, n):
                source = held[b][-1]
                held[b].append(hop(source, slot))
    if plan:
        moving[0, 1] = hop(tokens[0], 1)

    def passing(kernel, last):
        if kernel >= len(plan):
            return [last]
        arrived, next_hops = plan[kernel]
        fresh = [b for b, slot in next_hops if slot == 1]
        held_on = [(b, slot - 1) for b, slot in next_hops if slot > 1 and (b, slot - 1) not in arrived]
        values = [moving.pop(k) for k in arrived] + [held[b][slot] for b, slot in held_on]
        passed = gate(values + [own[b - 1][3] for b in fresh], [last])
        for k, value in zip(arrived, passed):
            held[k[0]].append(value)
        for (b, slot), value in zip(held_on, passed[len(arrived) :]):
            held[b][slot] = value
        starts = dict(zip(fresh, passed[len(values) :]))
        for b, slot in next_hops:
            moving[b, slot] = hop(starts[b] if slot == 1 else held[b][slot - 1], slot)
        return passed[:1]

    after = [vecs, b_in]
    for b in range(buckets):
        own.append(run_own(b, after))
        after = passing(b, own[b][0])
    for b in range(buckets):
        attn, lse = run_far(b, after)
        attns.append(attn)
        lses.append(lse)
        after = passing(buckets + 2 * b, lse)
        mids.append(run_mid(b, out, after))
        out = [mids[b][0]]
        after = passing(buckets + 2 * b + 1, mids[b][9])
    column = lambda i: [m[i] for m in mids]
    kept, sent = wgrad_call(
        places, devices, column(5), column(7), column(4), column(6), attns, column(8), column(9)
    )

    final_rows = HEADS // 4 * (6 * hd + 16)
    final_rows += -final_rows % (16 * lax.axis_size("batch") // 2)

    board = Board(places)
    big = board.start(sum_over_devices(kept, sent, groups))
    waiting = [sent]
    mine, returns = [], []
    resting = lambda: [p for p in board.active if p is not big] if board.ticks == 1 else None
    sums = None
    for b in range(buckets):
        g, delta, branch = mids[b][2], mids[b][3], mids[b][1]
        args = (own[b][0], g, lses[b], delta, w_kv, b_kv, wq, branch)
        dx = {}
        last = final_rows if b + 1 == buckets else 0
        cut = max(1, n // 2) if b >= SPLIT_FROM else 0
        pieces = lambda i, dx=dx, cut=cut: (dx[0], i) if i < n - max(cut, 1) else (dx[1], i - (n - cut))
        if cut:
            there = held[b][n - 1 : cut - 1 : -1]
            dx[0], dq, sums = back_call(b, cut, n - 1, places, me, lengths, there, *args, None, sums, 0, waiting)
            returns.append(board.start(send_back(pieces, n)))
            waiting = board.tick([sums], resting())
            there = held[b][cut - 1 :: -1]
            dx[1], own_part, sums = back_call(b, 0, cut - 1, places, me, lengths, there, *args, dq, sums, last, waiting)
            if not last:
                waiting = board.tick([sums], resting())
        else:
            dx[0], own_part, sums = back_call(b, 0, n - 1, places, me, lengths, held[b][::-1], *args, None, sums, last, waiting)
            returns.append(board.start(send_back(pieces, n)))
            waiting = board.tick([sums])
        mine.append(own_part)
    after = [sums[1]]
    whole, grads, done = [], None, set()
    alone = 2
    landed = lambda: [r.result for r in returns if r.result is not None]
    if board.active:
        after = board.tick(after + landed())[:1]
    small_first = Process(sum_over_devices(*gate(list(sums), after), groups, n > 1))
    board.active.append(small_first)
    while board.active:
        sent = board.tick(landed() + after, [small_first] if alone > 0 else None)
        alone, after = alone - 1, sent[:1]
        ready = [b for b in range(buckets) if b not in done and returns[b].result is not None]
        if grads is None and big.result is not None:
            grads = big_call(places, *big.result, ff, sent)
            after = [grads[3]]
        elif ready:
            b = ready[0]
            whole = [tokens_call(b, buckets, mine[b], returns[b].result, whole, sent)]
            done.add(b)
            after = whole
    for b in range(buckets):
        if b not in done:
            whole = [tokens_call(b, buckets, mine[b], returns[b].result, whole, [])]
    grad_wq, grad_wk, grad_wv, bias = small_call(places, *small_first.result)
    grad_w_outer, grad_w_inner, grad_w_out, v = grads
    return (
        out[0], whole[0], grad_wq, grad_wk, grad_wv, grad_w_out, bias[0], bias[1], v[7],
        v[5], v[6], v[0], v[1], v[2], v[3],
        grad_w_inner, v[8 : 8 + ff // d].reshape(ff), grad_w_outer, v[4],
    )


def solution(mesh):
    rows = P("batch", "blk", None)
    in_specs = (rows, P("batch")) + (P(),) * 17 + (rows,)
    out_specs = (rows, rows) + (P(),) * 17
    return jax.shard_map(on_device, mesh=mesh, in_specs=in_specs, out_specs=out_specs, check_vma=False)
```

```python
import functools
import math

import jax
import jax.numpy as jnp
from jax import lax
from jax.experimental import pallas as pl
from jax.experimental.pallas import tpu as pltpu
from jax.sharding import PartitionSpec as P

HEADS = 8
F32 = jnp.float32
BF16 = jnp.bfloat16
FAR = -1e30
EPS = 1e-05
SPLIT_FROM = 0
LOG2E = math.log2(math.e)
LN2 = math.log(2.0)
GELU_C = math.sqrt(2.0 / math.pi)
GELU_K = 0.044715

VM = pl.BlockSpec(memory_space=pltpu.VMEM)
SM = pl.BlockSpec(memory_space=pltpu.SMEM)
ANY = pl.BlockSpec(memory_space=pl.ANY)
S = jax.ShapeDtypeStruct


def dot(a, b, dims):
    return lax.dot_general(a, b, (dims, ((), ())), preferred_element_type=F32)


def nn(a, b):
    return dot(a, b, ((1,), (0,)))


def nt(a, b):
    return dot(a, b, ((1,), (1,)))


def tn(a, b):
    return dot(a, b, ((0,), (0,)))


def params(mib=56):
    return pltpu.CompilerParams(vmem_limit_bytes=mib * 2**20)


def cost(flops, bytes_accessed):
    return pl.CostEstimate(flops=int(flops), bytes_accessed=int(bytes_accessed), transcendentals=0)


def head_size(features):
    return features // HEADS


def set_bias(bias, slot, me, length):
    rows = bias.shape[0]
    first = (me - slot) * rows
    partial = (slot == 0) | (first + rows > length)

    @pl.when(partial)
    def _():
        c = first + lax.broadcasted_iota(jnp.int32, bias.shape, 0)
        p = me * rows + lax.broadcasted_iota(jnp.int32, bias.shape, 1)
        bias[...] = jnp.where(c <= jnp.minimum(p, length - 1), 0.0, FAR)

    @pl.when(jnp.logical_not(partial))
    def _():
        bias[...] = jnp.zeros(bias.shape, F32)


def project_pair(w_kv, b_kv, x):
    kv = (nt(w_kv, x) + b_kv).astype(BF16)
    hd = kv.shape[0] // 4
    return [kv[:hd], kv[hd : 2 * hd]], [kv[2 * hd : 3 * hd], kv[3 * hd :]]


def attend_slot(x, q, w_kv, b_kv, bias, top_s, acc_s):
    pairs = w_kv.shape[0]
    rows = x.shape[0]

    def body(step, carry):
        for j in range(2):
            one_pair(step * 2 + j)
        return carry

    def one_pair(pair):
        ks, vs = project_pair(w_kv[pair], b_kv[pair], x[...])
        for i in range(2):
            h = pair * 2 + i
            logits = tn(ks[i], q[h]) + bias[...]
            old = top_s[h]
            top = jnp.maximum(jnp.max(logits, axis=0, keepdims=True), old)
            weights = jnp.exp2(logits - top).astype(BF16)
            v_one = jnp.concatenate([vs[i], jnp.ones((16, rows), BF16)], axis=0)
            acc_s[h] = nn(v_one, weights) + jnp.exp2(old - top) * acc_s[h]
            top_s[h] = top

    lax.fori_loop(0, pairs // 2, body, 0)


def own_kernel(bucket, ahead, me_ref, len_ref, x, wq, bq, w_kv, b_kv, *refs):
    more = refs[0]
    refs = refs[len(refs) - 4 - (ahead > 0) :]
    q_o, top_o, acc_o = refs[:3]
    bias = refs[-1]
    me = me_ref[0]
    length = len_ref[bucket]
    rows = x.shape[1]
    scale = head_size(x.shape[2]) ** -0.5 * LOG2E
    pairs = w_kv.shape[0]
    hd = q_o.shape[1]
    if ahead:
        refs[3][...] = more[0]

    def body(pair, carry):
        q = ((nt(wq[pair], x[0]) + bq[pair]) * scale).astype(BF16)
        q_o[2 * pair] = q[:hd]
        q_o[2 * pair + 1] = q[hd:]
        return carry

    lax.fori_loop(0, pairs, body, 0)
    top_o[...] = jnp.full(top_o.shape, FAR, F32)
    acc_o[...] = jnp.zeros(acc_o.shape, F32)

    @pl.when(me * rows < length)
    def _():
        set_bias(bias, 0, me, length)
        attend_slot(x.at[0], q_o, w_kv, b_kv, bias, top_o, acc_o)


def own_call(bucket, me, lengths, tokens, wq, bq, w_kv, b_kv, ahead, after):
    _, rows, d = tokens.shape
    hd = head_size(d)
    shapes = [S((HEADS, hd, rows), BF16), S((HEADS, 1, rows), F32), S((HEADS, hd + 16, rows), F32)]
    one = lambda b: pl.BlockSpec((1, rows, d), lambda i: (b, 0, 0))
    extra = [one(ahead)] if ahead else []
    shapes += [S((rows, d), BF16)] * len(extra)
    return pl.pallas_call(
        functools.partial(own_kernel, bucket, ahead),
        grid=(1,),
        out_shape=tuple(shapes),
        in_specs=[SM, SM, one(bucket)] + [VM] * 4 + extra + [ANY] * len(after),
        out_specs=(VM,) * len(shapes),
        scratch_shapes=[pltpu.VMEM((rows, rows), F32)],
        compiler_params=params(),
        cost_estimate=cost(8e9, 4e6),
        name=f"attend_own_{bucket}",
    )(me, lengths, tokens, wq, bq, w_kv, b_kv, *([tokens] if ahead else []), *after)


def far_kernel(bucket, count, first_slot, final, me_ref, len_ref, *refs):
    xs = refs[:count]
    q, top_i, acc_i, w_kv, b_kv = refs[count : count + 5]
    out_o, lse_o, x_s, top_s, acc_s, bias = refs[len(refs) - 6 :]
    me = me_ref[0]
    length = len_ref[bucket]
    rows = xs[0].shape[0]
    hd = acc_s.shape[1] - 16
    top_s[...] = top_i[...]
    acc_s[...] = acc_i[...]
    for i in range(count):

        @pl.when(me >= first_slot + i)
        def _(i=i):
            x_s[i] = xs[i][...]

    def body(slot, carry):
        first = (me - slot) * rows

        @pl.when(first < length)
        def _():
            set_bias(bias, slot, me, length)
            attend_slot(x_s.at[slot - first_slot], q, w_kv, b_kv, bias, top_s, acc_s)

        return carry

    lax.fori_loop(first_slot, jnp.minimum(me, first_slot + count - 1) + 1, body, 0)
    if not final:
        out_o[...] = top_s[...]
        lse_o[...] = acc_s[...]
        return

    def finish(h, carry):
        total = acc_s[h, hd : hd + 1]
        out_o[h] = (acc_s[h, :hd] / total).astype(BF16)
        lse_o[h] = top_s[h] + jnp.log2(total)
        return carry

    lax.fori_loop(0, HEADS, finish, 0)


def far_call(bucket, me, lengths, xs, q, top, acc, w_kv, b_kv, after, first_slot=1, final=True):
    rows, d = xs[0].shape
    hd = head_size(d)
    shapes = ((HEADS, hd, rows), (HEADS, 1, rows), (HEADS, hd + 16, rows))
    operands = [me, lengths, *xs, q, top, acc, w_kv, b_kv]
    specs = [SM, SM] + [VM] * (len(xs) + 5)
    out_shape = [S(shapes[0], BF16), S(shapes[1], F32)] if final else [S(shapes[1], F32), S(shapes[2], F32)]
    return pl.pallas_call(
        functools.partial(far_kernel, bucket, len(xs), first_slot, final),
        grid=(1,),
        out_shape=tuple(out_shape),
        in_specs=specs + [ANY] * len(after),
        out_specs=(VM,) * len(out_shape),
        scratch_shapes=[
            pltpu.VMEM((len(xs), rows, d), BF16),
            pltpu.VMEM(shapes[1], F32),
            pltpu.VMEM(shapes[2], F32),
            pltpu.VMEM((rows, rows), F32),
        ],
        compiler_params=params(),
        cost_estimate=cost(18e9, 5e6),
        name=f"attend_far_{bucket}_{first_slot}",
    )(*operands, *after)


def norm_stats(v):
    centered = v - jnp.mean(v, axis=-1, keepdims=True)
    r = lax.rsqrt(jnp.mean(centered * centered, axis=-1, keepdims=True) + EPS)
    return centered * r, r


def norm_grad(n, r, gain, upstream):
    gu = gain * upstream
    return r * (gu - jnp.mean(gu, axis=-1, keepdims=True) - n * jnp.mean(gu * n, axis=-1, keepdims=True))


def over_rows(v):
    return jnp.sum(v.astype(F32), axis=0, keepdims=True)


def mid_kernel(bucket, me_ref, len_ref, attn, x, cot, w_out, w_inner, w_outer, vecs, b_inner, *refs):
    (out_o, branch_o, g_o, delta_o, normed_o, active_o, ghid_o, gtwo_o, gb_o, sums_o,
     pre_s, n1_s, r1_s, dual_s, slope_s, acc_s,
     inner_s, outer_s, cot_s, normed_s, active_s, ghid_s, gtwo_s, sems) = refs[len(refs) - 24 :]
    copies_in = [
        pltpu.make_async_copy(a, b, sems.at[i])
        for i, (a, b) in enumerate([(w_inner, inner_s), (w_outer, outer_s), (cot.at[bucket], cot_s)])
    ]
    for copy in copies_in:
        copy.start()
    w_inner, w_outer, cot = inner_s, outer_s, cot_s
    copies_out = [
        pltpu.make_async_copy(a, b, sems.at[3 + i])
        for i, (a, b) in enumerate([(normed_s, normed_o), (active_s, active_o), (gtwo_s, gtwo_o), (ghid_s, ghid_o)])
    ]
    me = me_ref[0]
    length = len_ref[bucket]
    _, rows, d = out_o.shape
    ff = active_s.shape[1]
    up_step = min(512, ff)
    down_step = min(512, ff)
    block = min(256, rows)
    b_out, gain1, shift1, gain2, shift2, gain_f, shift_f, b_outer = (vecs[i : i + 1] for i in range(8))
    attn_t = attn[...].reshape(d, rows)
    pre_s[...] = tn(attn_t, w_out[...])

    def over_blocks(work):
        def body(i, carry):
            work(pl.ds(pl.multiple_of(i * block, block), block), i * block)
            return carry

        lax.fori_loop(0, rows // block, body, 0)

    def first_norm(at, _):
        pre = x[0, at].astype(F32) + (pre_s[at] + b_out)
        n1, r1 = norm_stats(pre)
        pre_s[at] = pre
        n1_s[at] = n1
        r1_s[at] = r1
        normed_s[at] = (n1 * gain1 + shift1).astype(BF16)

    over_blocks(first_norm)
    copies_out[0].start()
    copies_in[0].wait()
    copies_in[1].wait()
    acc_s[...] = jnp.zeros(acc_s.shape, F32)

    def lift(i):
        f = pl.ds(pl.multiple_of(i * up_step, up_step), up_step)
        return nn(normed_s[...], w_inner[:, f]) + b_inner[:, f]


    def up(i, carry):
        f = pl.ds(pl.multiple_of(i * up_step, up_step), up_step)
        h = lift(i)
        square = h * h
        t = jnp.tanh(h * (GELU_C + (GELU_C * GELU_K) * square))
        half = 0.5 + 0.5 * t
        active = (h * half).astype(BF16)
        active_s[:, f] = active
        slope_s[:, f] = half + (0.5 * h) * (1.0 - t * t) * (GELU_C + (3.0 * GELU_C * GELU_K) * square)
        acc_s[...] += nn(active, w_outer[f, :])
        return carry

    lax.fori_loop(0, ff // up_step, up, 0)
    copies_out[1].start()
    sums_o[...] = jnp.zeros(sums_o.shape, F32)
    copies_in[2].wait()

    def last_norms(at, start):
        branch_two = acc_s[at] + b_outer
        normed = n1_s[at] * gain1 + shift1
        n2, r2 = norm_stats(normed + branch_two)
        nf, rf = norm_stats(pre_s[at] + branch_two)
        out_o[0, at] = ((n2 * gain2 + shift2) + (nf * gain_f + shift_f)).astype(BF16)
        p = me * rows + start + lax.broadcasted_iota(jnp.int32, (block, 1), 0)
        g_out = jnp.where(p < length, cot[at].astype(F32), 0.0)
        g_dual = norm_grad(nf, rf, gain_f, g_out)
        g_two = norm_grad(n2, r2, gain2, g_out)
        g_branch_two = (g_two + g_dual).astype(BF16)
        gtwo_s[at] = g_branch_two
        dual_s[at] = g_dual
        acc_s[at] = g_two
        sums_o[0:1] += over_rows(g_out * n2)
        sums_o[1:2] += over_rows(g_out)
        sums_o[2:3] += over_rows(g_out * nf)
        sums_o[4:5] += over_rows(g_branch_two)

    over_blocks(last_norms)
    copies_out[2].start()
    sums_o[3:4] = sums_o[1:2]

    @pl.when(me * rows < length)
    def _():
        def down(i, carry):
            f = pl.ds(pl.multiple_of(i * down_step, down_step), down_step)
            g_hidden = (nt(gtwo_s[...], w_outer[f, :]) * slope_s[:, f]).astype(BF16)
            ghid_s[:, f] = g_hidden
            sums_o[pl.ds(8 + i, 1)] = over_rows(g_hidden)
            acc_s[...] += nt(g_hidden, w_inner[:, f])
            return carry

        lax.fori_loop(0, ff // down_step, down, 0)
        copies_out[3].start()

        def first_back(at, _):
            g_normed = acc_s[at]
            n1 = n1_s[at]
            g_branch = norm_grad(n1, r1_s[at], gain1, g_normed) + dual_s[at]
            branch_o[at] = g_branch
            g_b = g_branch.astype(BF16)
            gb_o[at] = g_b
            sums_o[5:6] += over_rows(g_normed * n1)
            sums_o[6:7] += over_rows(g_normed)
            sums_o[7:8] += over_rows(g_b)

        over_blocks(first_back)
        g_o[...] = nt(w_out[...], gb_o[...]).astype(BF16).reshape(g_o.shape)

        def head_delta(h, carry):
            delta_o[h] = jnp.sum(g_o[h].astype(F32) * attn[h].astype(F32), axis=0, keepdims=True)
            return carry

        lax.fori_loop(0, HEADS, head_delta, 0)

    @pl.when(me * rows >= length)
    def _():
        for ref in (branch_o, g_o, delta_o, ghid_s, gb_o):
            ref[...] = jnp.zeros(ref.shape, ref.dtype)
        copies_out[3].start()

    for copy in copies_out:
        copy.wait()


def mid_call(bucket, me, lengths, attn, tokens, cotangent, w_out, w_inner, w_outer, vecs, b_inner, out, after):
    buckets, rows, d = tokens.shape
    ff = w_inner.shape[1]
    hd = head_size(d)
    one = pl.BlockSpec((1, rows, d), lambda i: (bucket, 0, 0))
    return pl.pallas_call(
        functools.partial(mid_kernel, bucket),
        grid=(1,),
        out_shape=(
            S((buckets, rows, d), BF16),
            S((rows, d), F32),
            S((HEADS, hd, rows), BF16),
            S((HEADS, 1, rows), F32),
            S((rows, d), BF16),
            S((rows, ff), BF16),
            S((rows, ff), BF16),
            S((rows, d), BF16),
            S((rows, d), BF16),
            S((16, d), F32),
        ),
        in_specs=[SM, SM, VM, one, ANY, VM, ANY, ANY, VM, VM] + [ANY] * (len(out) + len(after)),
        out_specs=(one, VM, VM, VM, ANY, ANY, ANY, ANY, VM, VM),
        input_output_aliases={10: 0} if out else {},
        scratch_shapes=[
            pltpu.VMEM((rows, d), F32),
            pltpu.VMEM((rows, d), F32),
            pltpu.VMEM((rows, 1), F32),
            pltpu.VMEM((rows, d), F32),
            pltpu.VMEM((rows, ff), F32),
            pltpu.VMEM((rows, d), F32),
            pltpu.VMEM((d, ff), BF16),
            pltpu.VMEM((ff, d), BF16),
            pltpu.VMEM((rows, d), BF16),
            pltpu.VMEM((rows, d), BF16),
            pltpu.VMEM((rows, ff), BF16),
            pltpu.VMEM((rows, ff), BF16),
            pltpu.VMEM((rows, d), BF16),
            pltpu.SemaphoreType.DMA((7,)),
        ],
        compiler_params=params(),
        cost_estimate=cost(12e9, 14e6),
        name=f"feed_forward_{bucket}",
    )(me, lengths, attn, tokens, cotangent, w_out, w_inner, w_outer, vecs, b_inner, *out, *after)


def wgrad_job(step, half, core):
    return step % half + jnp.where(step < half, 1 - core, core) * half


def rows_of(refs):
    return jnp.concatenate([r[...] for r in refs], axis=0)


def wgrad_kernel(buckets, count, half, places, *refs):
    groups = [refs[i * buckets : (i + 1) * buckets] for i in range(7)]
    active, g_two, normed, g_hidden, attn, g_b, sums = groups
    kept_o, sent_o = refs[7 * buckets :]
    step = pl.program_id(0)
    job = wgrad_job(step, half, places[0])

    def put(value):
        @pl.when(step < half)
        def _():
            sent_o[...] = value

        @pl.when(step >= half)
        def _():
            kept_o[...] = value

    @pl.when(job < count)
    def _():
        put(tn(rows_of(active), rows_of(g_two)).astype(BF16))

    @pl.when((job >= count) & (job < 2 * count))
    def _():
        put(tn(rows_of(normed), rows_of(g_hidden)).astype(BF16))

    @pl.when(job == 2 * count)
    def _():
        put(sum(nn(a[...], g[...]) for a, g in zip(attn, g_b)).astype(BF16))

    @pl.when(job > 2 * count)
    def _():
        put(jnp.zeros(kept_o.shape, BF16))

    @pl.when(job == 2 * count + 1)
    def _():
        value = sum(s[...] for s in sums).astype(BF16)

        @pl.when(step < half)
        def _():
            sent_o[:16] = value

        @pl.when(step >= half)
        def _():
            kept_o[:16] = value


def wgrad_call(places, devices, active, g_two, normed, g_hidden, attn, g_b, sums):
    buckets = len(active)
    rows, ff = active[0].shape
    d = g_two[0].shape[1]
    count = ff // d
    half = count + 1
    while 2 * half * d % (16 * devices):
        half += 1
    clip = lambda v, top: jnp.minimum(jnp.maximum(v, 0), top)
    job = lambda j, p: wgrad_job(j, half, p[0])
    full = pl.BlockSpec((rows, d), lambda j, p: (0, 0))
    tall = pl.BlockSpec((d, rows), lambda j, p: (0, 0))
    active_spec = pl.BlockSpec((rows, d), lambda j, p: (0, clip(job(j, p), count - 1)))
    hid_spec = pl.BlockSpec((rows, d), lambda j, p: (0, clip(job(j, p) - count, count - 1)))
    attn2 = [a.reshape(d, rows) for a in attn]
    return pl.pallas_call(
        functools.partial(wgrad_kernel, buckets, count, half),
        grid_spec=pltpu.PrefetchScalarGridSpec(
            num_scalar_prefetch=1,
            grid=(2 * half,),
            in_specs=[active_spec] * buckets + [full] * buckets + [full] * buckets + [hid_spec] * buckets
            + [tall] * buckets + [full] * buckets + [pl.BlockSpec((16, d), lambda j, p: (0, 0))] * buckets,
            out_specs=(
                pl.BlockSpec((d, d), lambda j, p: (jnp.maximum(j - half, 0), 0)),
                pl.BlockSpec((d, d), lambda j, p: (jnp.minimum(j, half - 1), 0)),
            ),
        ),
        out_shape=(S((half * d, d), BF16),) * 2,
        compiler_params=params(),
        cost_estimate=cost(buckets * 5e9, 20e6),
        name="weight_gradients",
    )(places, *active, *g_two, *normed, *g_hidden, *attn2, *g_b, *sums)


def attend_back(x, q, g, w_kv, b_kv, lse, delta, bias, dq_s, kv_s, dkv_s):
    pairs, width, d = w_kv.shape
    hd = width // 4
    rows = x.shape[0]
    block = 2 * width

    def project(i, carry):
        at = pl.ds(pl.multiple_of(i * block, block), block)
        w = w_kv[pl.ds(2 * i, 2)].reshape(block, d)
        kv_s[at] = (nt(w, x[...]) + b_kv[pl.ds(2 * i, 2)].reshape(block, 1)).astype(BF16)
        return carry

    lax.fori_loop(0, pairs // 2, project, 0)

    def body(step, carry):
        for j in range(2):
            one_pair(step * 2 + j)
        return carry

    def one_pair(pair):
        base = pl.multiple_of(pair * width, width)
        for i in range(2):
            h = pair * 2 + i
            at_k = pl.ds(base + i * hd, hd)
            at_v = pl.ds(base + (2 + i) * hd, hd)
            k = kv_s[at_k]
            q_t, g_t = q[h], g[h]
            probs = jnp.exp2(tn(k, q_t) + bias[...] - lse[h])
            g_probs = tn(kv_s[at_v], g_t)
            g_logits = (probs * (g_probs - delta[h])).astype(BF16)
            dkv_s[at_v] = nt(g_t, probs.astype(BF16)).astype(BF16)
            dkv_s[at_k] = (nt(q_t, g_logits) * LN2).astype(BF16)
            dq_s[h] += nn(k, g_logits)

    lax.fori_loop(0, pairs // 2, body, 0)


def back_kernel(bucket, low, high, fresh, first, final, places, me_ref, len_ref, *refs):
    count = high - low + 1
    refs = list(refs)
    take = lambda n: [refs.pop(0) for _ in range(n)]
    xs = take(count)
    q, g, lse, delta, w_kv, b_kv = take(6)
    sems = refs.pop()
    wq, branch = take(2) if low == 0 else (None, None)
    dq_i = None if fresh else take(1)[0]
    sums_i = None if first else take(1)[0]
    x_s, kv_s, dkv_s, dq_s, dx_s, bias, *late = refs[len(refs) - 6 - (low == 0) - (not first) :]
    refs = refs[: len(refs) - 6 - len(late)]
    refs = refs[len(refs) - 2 - final - (high > 0) :]
    dx_o = refs.pop(0) if high > 0 else None
    last_o, *sums_o = refs
    me = me_ref[0]
    length = len_ref[bucket]
    rows, d = xs[0].shape
    hd = g.shape[1]
    live = me * rows < length
    dq_s[...] = jnp.zeros(dq_s.shape, F32) if fresh else dq_i[...]
    rows_in = [
        pltpu.make_async_copy(xs[i], x_s.at[pl.ds(i * rows, rows)], sems.at[i]) for i in range(count)
    ]
    late_in = [
        pltpu.make_async_copy(source, to, sems.at[count + j])
        for j, (source, to) in enumerate(zip([branch] * (low == 0) + [sums_i] * (not first), late))
    ]
    for copy in rows_in + late_in:
        copy.start()

    def take_rows(i):
        for j in range(count):

            @pl.when(i == j)
            def _(j=j):
                rows_in[j].wait()

    def dx_out(i):
        return pltpu.make_async_copy(dx_s.at[i], dx_o.at[i], sems.at[count + 2 + i])

    def body(i, carry):
        slot = high - i
        at = pl.ds(pl.multiple_of(i * rows, rows), rows)
        active = live & (me >= slot)
        take_rows(i)

        @pl.when(active)
        def _():
            set_bias(bias, slot, me, length)
            attend_back(x_s.at[at], q, g, w_kv, b_kv, lse, delta, bias, dq_s, kv_s, dkv_s.at[:, at])

        @pl.when(active & (slot > 0))
        def _():
            dx_s[i] = tn(dkv_s[:, at], w_kv[...].reshape(2 * d, d)).astype(BF16)

        @pl.when(jnp.logical_not(active))
        def _():
            dkv_s[:, at] = jnp.zeros((2 * d, rows), BF16)

        @pl.when(jnp.logical_not(active) & (slot > 0))
        def _():
            dx_s[i] = jnp.zeros((rows, d), BF16)

        @pl.when(slot > 0)
        def _():
            dx_out(i).start()

        return carry

    lax.fori_loop(0, count, body, 0)
    pairs = HEADS // 2
    dq = (dq_s[...] * hd**-0.5).astype(BF16).reshape(d, rows)
    here = slice((count - 1) * rows, count * rows)
    for copy in late_in:
        copy.wait()
    if low == 0:
        last_o[...] = late[0][...]

        @pl.when(live)
        def _():
            last_o[...] += tn(dkv_s[:, here], w_kv[...].reshape(2 * d, d)) + tn(dq, wq[...])
    else:
        last_o[...] = dq_s[...]

    half = HEADS // 4
    ones = jnp.ones((8, count * rows), BF16)

    def add(pair, carry):
        at = pl.ds(pl.multiple_of(pair * 4 * hd, 4 * hd), 4 * hd)
        dkv = dkv_s[at, :]
        parts = [None, nn(dkv, x_s[...]), None]
        bias_sums = [nt(ones, dkv), jnp.zeros((8, d - 4 * hd), F32)]
        if low == 0:
            dq_pair = (dq_s[pl.ds(2 * pair, 2)] * hd**-0.5).astype(BF16).reshape(2 * hd, rows)
            parts[0] = nn(dq_pair, x_s[here])
            bias_sums[1:] = [nt(ones[:, :rows], dq_pair), jnp.zeros((8, d - 6 * hd), F32)]
        else:
            parts[0] = jnp.zeros((2 * hd, d), F32)
        parts[2] = jnp.concatenate([jnp.concatenate(bias_sums, axis=1), jnp.zeros((8, d), F32)])
        value = jnp.concatenate(parts, axis=0)
        if not first:
            value = value + late[-1][pair].astype(F32)
        value = value.astype(BF16)
        if final:
            kept = pair // half == places[0]
            to = pl.ds(pl.multiple_of((pair % half) * 6 * hd, 6 * hd), 6 * hd)
            to_bias = pl.ds(pl.multiple_of(half * 6 * hd + (pair % half) * 16, 16), 16)

            def put(ref):
                ref[to] = value[: 6 * hd]
                ref[to_bias] = value[6 * hd :]

            @pl.when(kept)
            def _():
                put(sums_o[0])

            @pl.when(jnp.logical_not(kept))
            def _():
                put(sums_o[1])
        else:
            sums_o[0][pair] = value
        return carry

    if final:
        used = half * (6 * hd + 16)
        for ref in sums_o:
            if used < ref.shape[0]:
                ref[used:] = jnp.zeros((ref.shape[0] - used, d), BF16)
    lax.fori_loop(0, pairs, add, 0)
    for i in range(count - (low == 0)):
        dx_out(i).wait()


def back_call(
    bucket, low, high, places, me, lengths, xs, q, g, lse, delta, w_kv, b_kv, wq, branch, dq, sums, final, after
):
    rows, d = xs[0].shape
    hd = head_size(d)
    own = low == 0
    fresh = dq is None
    far = high - max(low, 1) + 1
    operands = [places, me, lengths, *xs, q, g, lse, delta, w_kv, b_kv]
    specs = [SM] * 3 + [ANY] * len(xs) + [VM] * 6
    late = []
    if own:
        operands += [wq.reshape(d, d), branch]
        specs += [VM, ANY]
        late.append(branch)
    if not fresh:
        operands.append(dq)
        specs.append(VM)
    if sums is not None:
        operands.append(sums)
        specs.append(ANY)
        late.append(sums)
    sums_shape = (HEADS // 2, 6 * hd + 16, d)
    out_shape = [S((far, rows, d), BF16)] if far else []
    out_shape += [S((rows, d), F32) if own else S((HEADS, hd, rows), F32)]
    out_shape += [S((final, d), BF16)] * 2 if final else [S(sums_shape, BF16)]
    outs = pl.pallas_call(
        functools.partial(back_kernel, bucket, low, high, fresh, sums is None, final > 0),
        grid=(1,),
        out_shape=tuple(out_shape),
        in_specs=specs + [ANY] * len(after),
        out_specs=((ANY,) if far else ()) + (VM,) * (len(out_shape) - (far > 0)),
        scratch_shapes=[
            pltpu.VMEM((len(xs) * rows, d), BF16),
            pltpu.VMEM((2 * d, rows), BF16),
            pltpu.VMEM((2 * d, len(xs) * rows), BF16),
            pltpu.VMEM((HEADS, hd, rows), F32),
            pltpu.VMEM((max(far, 1), rows, d), BF16),
            pltpu.VMEM((rows, rows), F32),
            *[pltpu.VMEM(a.shape, a.dtype) for a in late],
            pltpu.SemaphoreType.DMA((2 * len(xs) + 2,)),
        ],
        compiler_params=params(36),
        cost_estimate=cost(10e9 * len(xs), 14e6),
        name=f"attend_back_{bucket}_{high}",
    )(*operands, *after)
    last = len(out_shape) - (3 if final else 2)
    return (outs[0] if far else None), outs[last], (outs[last + 1 :] if final else outs[-1])


def step_call(name, places, jobs, after):
    operands, specs, shapes, bodies = [places], [SM], [], []
    for job_in, job_specs, job_out, body in jobs:
        bodies.append((len(job_in), len(job_out), body))
        operands += job_in
        specs += job_specs
        shapes += job_out
    first_out = len(operands) + len(after)

    def kernel(places_ref, *refs):
        at_in, at_out = 0, first_out - 1
        for n_in, n_out, body in bodies:
            body(places_ref, *refs[at_in : at_in + n_in], *refs[at_out : at_out + n_out])
            at_in += n_in
            at_out += n_out

    outs = pl.pallas_call(
        kernel,
        grid=(1,),
        out_shape=tuple(shapes),
        in_specs=specs + [ANY] * len(after),
        out_specs=(VM,) * len(shapes),
        compiler_params=params(16),
        cost_estimate=cost(2e9, 4e6),
        name=name,
    )(*operands, *after)
    found = []
    for _, n_out, _ in bodies:
        found.append(outs[:n_out])
        outs = outs[n_out:]
    return found


def gate(arrays, after):
    outs = pl.pallas_call(
        lambda *refs: None,
        out_shape=tuple(S(a.shape, a.dtype) for a in arrays),
        in_specs=[ANY] * (len(arrays) + len(after)),
        out_specs=(ANY,) * len(arrays),
        input_output_aliases={i: i for i in range(len(arrays))},
        name="gate",
    )(*arrays, *after)
    return list(outs)


class Group:
    def __init__(self, index, axis, low, high):
        self.index, self.axis, self.low, self.count = index, axis, low, 1 << (high - low)
        self.place = (lax.axis_index(axis) >> low) & (self.count - 1)

    def swap(self, value, mask):
        size = lax.axis_size(self.axis)
        return lax.ppermute(value, self.axis, [(i, i ^ (mask << self.low)) for i in range(size)])


def part_rows(place, mask, size):
    return pl.ds(pl.multiple_of((place ^ mask) * size, size), size)


def total(kept, got, at):
    values = [r[at].astype(F32) for r in [kept, *got]]
    while len(values) > 1:
        values = [a + b for a, b in zip(values[::2], values[1::2])]
    return values[0].astype(BF16)


def split_job(kept, got, group):
    rows, d = kept.shape
    count = group.count if group else 1
    size = rows // count

    def body(places, kept, *refs):
        arrived, outs = refs[: len(got)], refs[len(got) :]
        for m in range(count):
            at = part_rows(places[group.index], m, size) if group else slice(None)
            outs[m][...] = total(kept, arrived, at)

    return [kept, *got], [VM] * (1 + len(got)), [S((size, d), BF16)] * count, body


def join_job(part, got, group):
    size, d = part.shape

    def body(places, *refs):
        for m in range(group.count):
            refs[-1][part_rows(places[group.index], m, size)] = refs[m][...]

    return [part, *got], [VM] * (1 + len(got)), [S((size * group.count, d), BF16)], body


def message_job(dx, at, carry):
    _, rows, d = dx.shape
    more = [] if carry is None else [carry]

    def body(places, dx, *refs):
        if more:
            refs[-1][...] = (dx[0].astype(F32) + refs[0][...].astype(F32)).astype(BF16)
        else:
            refs[-1][...] = dx[0]

    specs = [pl.BlockSpec((1, rows, d), lambda i: (at, 0, 0))] + [VM] * len(more)
    return [dx, *more], specs, [S((rows, d), BF16)], body


def sum_over_devices(kept, sent, groups, full=False):
    first, *rest = groups
    got = [first.swap(sent, 1)]
    scatter = rest[:-1] if full else rest
    for group in scatter:
        kept, *shards = yield split_job(kept, got, group)
        got = [group.swap(s, m + 1) for m, s in enumerate(shards)]
    (part,) = yield split_job(kept, got, None)
    if full and rest:
        got = [rest[-1].swap(part, m) for m in range(1, rest[-1].count)]
        (part,) = yield split_job(part, got, None)
    for group in reversed(scatter):
        got = [group.swap(part, m) for m in range(1, group.count)]
        (part,) = yield join_job(part, got, group)
    return part, first.swap(part, 1)


def send_back(pieces, n):
    carry = None
    for i, slot in enumerate(range(n - 1, 0, -1)):
        (message,) = yield message_job(*pieces(i), carry)
        carry = lax.ppermute(message, "blk", [(j, j - 1) for j in range(slot, n)])
    return carry


class Process:
    def __init__(self, steps):
        self.steps, self.result = steps, None
        self.job = next(steps)

    def advance(self, outs):
        try:
            self.job = self.steps.send(outs)
        except StopIteration as end:
            self.job, self.result = None, end.value


class Board:
    def __init__(self, places):
        self.places, self.active, self.ticks = places, [], 0

    def start(self, steps):
        self.active.append(Process(steps))
        return self.active[-1]

    def tick(self, after, only=None):
        self.ticks += 1
        now = self.active if only is None else only
        outs = step_call(f"step_{self.ticks}", self.places, [p.job for p in now], after)
        for p, o in zip(list(now), outs):
            p.advance(o)
        self.active = [p for p in self.active if p.job is not None]
        return [o for group in outs for o in group]


def big_kernel(ff, places, mine, got, *refs):
    outer_o, inner_o, out_o, vec_o = refs[len(refs) - 4 :]
    half, d = mine.shape
    count = ff // d
    for own_half in range(2):

        @pl.when(places[0] == own_half)
        def _(own_half=own_half):
            for i in range(2 * half // d):
                src = mine if i // (half // d) == own_half else got
                at = (i % (half // d)) * d
                value = src[at : at + d]
                if i < count:
                    outer_o[i * d : i * d + d] = value.astype(F32)
                elif i < 2 * count:
                    inner_o[:, (i - count) * d : (i - count) * d + d] = value.astype(F32)
                elif i == 2 * count:
                    out_o[...] = value.astype(F32)
                elif i == 2 * count + 1:
                    vec_o[...] = value[:16].astype(F32)


def big_call(places, mine, got, ff, after):
    d = mine.shape[1]
    shapes = (S((ff, d), F32), S((d, ff), F32), S((d, d), F32), S((16, d), F32))
    return pl.pallas_call(
        functools.partial(big_kernel, ff),
        grid=(1,),
        out_shape=shapes,
        in_specs=[SM, VM, VM] + [ANY] * len(after),
        out_specs=(VM,) * 4,
        compiler_params=params(24),
        cost_estimate=cost(5e9, 14e6),
        name="feed_forward_sums",
    )(places, mine, got, *after)


def small_kernel(places, mine, got, *refs):
    weights, bias_o = refs[len(refs) - 4 : len(refs) - 1], refs[-1]
    d = weights[0].shape[0]
    hd = head_size(d)
    half = HEADS // 4
    bias_o[...] = jnp.zeros(bias_o.shape, F32)
    for own_half in range(2):

        @pl.when(places[0] == own_half)
        def _(own_half=own_half):
            for pair in range(HEADS // 2):
                src = mine if pair // half == own_half else got
                at = (pair % half) * 6 * hd
                at_bias = half * 6 * hd + (pair % half) * 16
                lanes = slice(2 * hd * pair, 2 * hd * pair + 2 * hd)
                for k in range(3):
                    rows = src[at + 2 * hd * k : at + 2 * hd * k + 2 * hd].astype(F32)
                    weights[k][:, lanes] = rows.T
                bias = src[at_bias : at_bias + 16].astype(F32)
                bias_o[0:1, lanes] = bias[:1, 4 * hd : 6 * hd]
                bias_o[1:2, lanes] = bias[:1, 2 * hd : 4 * hd]


def small_call(places, mine, got):
    d = mine.shape[1]
    return pl.pallas_call(
        small_kernel,
        grid=(1,),
        out_shape=(S((d, d), F32),) * 3 + (S((8, d), F32),),
        in_specs=[SM, VM, VM],
        out_specs=(VM,) * 4,
        compiler_params=params(16),
        cost_estimate=cost(2e9, 5e6),
        name="attention_sums",
    )(places, mine, got)


def tokens_kernel(mine, carry, *refs):
    refs[-1][0] = mine[...] + carry[...].astype(F32)


def tokens_call(bucket, buckets, mine, carry, whole, after):
    rows, d = mine.shape
    return pl.pallas_call(
        tokens_kernel,
        grid=(1,),
        out_shape=S((buckets, rows, d), F32),
        in_specs=[VM, VM] + [ANY] * (len(whole) + len(after)),
        out_specs=pl.BlockSpec((1, rows, d), lambda i: (bucket, 0, 0)),
        input_output_aliases={2: 0} if whole else {},
        compiler_params=params(16),
        cost_estimate=cost(2e9, 3e6),
        name=f"token_gradients_{bucket}",
    )(mine, carry, *whole, *after)


def on_device(
    tokens, lengths, w_query, w_key, w_value, w_out, b_query, b_value, b_out, norm1_gain, norm1_bias,
    norm2_gain, norm2_bias, final_gain, final_bias, w_inner, b_inner, w_outer, b_outer, cotangent,
):
    buckets, rows, d = tokens.shape
    ff = w_inner.shape[1]
    hd = head_size(d)
    pairs = HEADS // 2
    n = lax.axis_size("blk")
    me = lax.axis_index("blk").astype(jnp.int32).reshape(1)
    bits = lambda axis: (lax.axis_size(axis) - 1).bit_length()
    groups = [Group(0, "batch", 0, 1), Group(1, "batch", 1, bits("batch")), Group(2, "blk", 0, bits("blk"))]
    places = jnp.stack([g.place for g in groups]).astype(jnp.int32)
    devices = math.prod(g.count for g in groups)
    groups = [groups[0]] + [g for g in groups[1:] if g.count > 1]

    paired = lambda w: w.T.reshape(pairs, 2 * hd, d)
    wq = paired(w_query)
    bq = b_query.reshape(pairs, 2 * hd, 1)
    w_kv = jnp.concatenate([paired(w_key), paired(w_value)], axis=1)
    b_v = b_value.reshape(pairs, 2 * hd, 1)
    b_kv = jnp.concatenate([jnp.zeros_like(b_v), b_v], axis=1)
    vecs = jnp.stack([b_out, norm1_gain, norm1_bias, norm2_gain, norm2_bias, final_gain, final_bias, b_outer])
    b_in = b_inner.reshape(1, ff)

    def hop(value, slot):
        return lax.ppermute(value, "blk", [(i, i + 1) for i in range(slot - 1, n - 1)])

    run_own = lambda b, after: own_call(b, me, lengths, tokens, wq, bq, w_kv, b_kv, (b + 1) % buckets, after)
    run_far = lambda b, after: far_call(b, me, lengths, held[b][1:], own[b][0], own[b][1], own[b][2], w_kv, b_kv, after)
    run_mid = lambda b, out, after: mid_call(
        b, me, lengths, attns[b], tokens, cotangent, w_out, w_inner, w_outer, vecs, b_in, out, after
    )
    held = [[tokens[b]] for b in range(buckets)]
    own, mids, attns, lses, out = [], [], [], [], []
    moving = {}
    if n == 4 and buckets == 3:
        plan = [
            ([(0, 1)], [(0, 2), (1, 1)]),
            ([], []),
            ([(0, 2), (1, 1)], [(0, 3), (1, 2)]),
            ([(0, 3)], [(2, 1)]),
            ([(1, 2)], [(1, 3)]),
            ([(1, 3), (2, 1)], [(2, 2)]),
            ([(2, 2)], [(2, 3)]),
            ([(2, 3)], []),
        ]
    else:
        plan = []
        for b in range(buckets):
            for slot in range(1, n):
                source = held[b][-1]
                held[b].append(hop(source, slot))
    if plan:
        moving[0, 1] = hop(tokens[0], 1)

    def passing(kernel, last):
        if kernel >= len(plan):
            return [last]
        arrived, next_hops = plan[kernel]
        if not arrived:
            return [last]
        fresh = [b for b, slot in next_hops if slot == 1]
        held_on = [(b, slot - 1) for b, slot in next_hops if slot > 1 and (b, slot - 1) not in arrived]
        values = [moving.pop(k) for k in arrived] + [held[b][slot] for b, slot in held_on]
        passed = gate(values + [own[b - 1][3] for b in fresh], [last])
        for k, value in zip(arrived, passed):
            held[k[0]].append(value)
        for (b, slot), value in zip(held_on, passed[len(arrived) :]):
            held[b][slot] = value
        starts = dict(zip(fresh, passed[len(values) :]))
        for b, slot in next_hops:
            moving[b, slot] = hop(starts[b] if slot == 1 else held[b][slot - 1], slot)
        return passed[:1]

    after = [vecs, b_in]
    for b in range(buckets):
        own.append(run_own(b, after))
        after = passing(b, own[b][0])
    extra = 0
    if plan:
        early = far_call(0, me, lengths, held[0][1:3], *own[0][:3], w_kv, b_kv, after, 1, False)
        own[0] = (own[0][0], *early)
        after = passing(buckets, early[0])
        extra = 1
    for b in range(buckets):
        if b == 0 and plan:
            attn, lse = far_call(0, me, lengths, held[0][3:], *own[0][:3], w_kv, b_kv, after, 3, True)
        else:
            attn, lse = run_far(b, after)
        attns.append(attn)
        lses.append(lse)
        after = passing(buckets + extra + 2 * b, lse)
        mids.append(run_mid(b, out, after))
        out = [mids[b][0]]
        after = passing(buckets + extra + 2 * b + 1, mids[b][9])
    column = lambda i: [m[i] for m in mids]
    kept, sent = wgrad_call(
        places, devices, column(5), column(7), column(4), column(6), attns, column(8), column(9)
    )

    final_rows = HEADS // 4 * (6 * hd + 16)
    final_rows += -final_rows % (16 * lax.axis_size("batch") // 2)

    board = Board(places)
    big = board.start(sum_over_devices(kept, sent, groups))
    waiting = [sent]
    mine, returns = [], []
    resting = lambda: [p for p in board.active if p is not big] if board.ticks == 1 else None
    sums = None
    for b in range(buckets):
        g, delta, branch = mids[b][2], mids[b][3], mids[b][1]
        args = (own[b][0], g, lses[b], delta, w_kv, b_kv, wq, branch)
        dx = {}
        last = final_rows if b + 1 == buckets else 0
        cut = max(1, n // 2) if b >= SPLIT_FROM else 0
        pieces = lambda i, dx=dx, cut=cut: (dx[0], i) if i < n - max(cut, 1) else (dx[1], i - (n - cut))
        if cut:
            there = held[b][n - 1 : cut - 1 : -1]
            dx[0], dq, sums = back_call(b, cut, n - 1, places, me, lengths, there, *args, None, sums, 0, waiting)
            returns.append(board.start(send_back(pieces, n)))
            waiting = board.tick([sums], resting())
            there = held[b][cut - 1 :: -1]
            dx[1], own_part, sums = back_call(b, 0, cut - 1, places, me, lengths, there, *args, dq, sums, last, waiting)
            if not last:
                waiting = board.tick([sums], resting())
        else:
            dx[0], own_part, sums = back_call(b, 0, n - 1, places, me, lengths, held[b][::-1], *args, None, sums, last, waiting)
            returns.append(board.start(send_back(pieces, n)))
            waiting = board.tick([sums])
        mine.append(own_part)
    after = [sums[1]]
    whole, grads, done = [], None, set()
    alone = 2
    landed = lambda: [r.result for r in returns if r.result is not None]
    if board.active:
        after = board.tick(after + landed())[:1]
    small_first = Process(sum_over_devices(*gate(list(sums), after), groups, n > 1))
    board.active.append(small_first)
    while board.active:
        sent = board.tick(landed() + after, [small_first] if alone > 0 else None)
        alone, after = alone - 1, sent[:1]
        ready = [b for b in range(buckets) if b not in done and returns[b].result is not None]
        if grads is None and big.result is not None:
            grads = big_call(places, *big.result, ff, sent)
            after = [grads[3]]
        elif ready:
            b = ready[0]
            whole = [tokens_call(b, buckets, mine[b], returns[b].result, whole, sent)]
            done.add(b)
            after = whole
    for b in range(buckets):
        if b not in done:
            whole = [tokens_call(b, buckets, mine[b], returns[b].result, whole, [])]
    grad_wq, grad_wk, grad_wv, bias = small_call(places, *small_first.result)
    grad_w_outer, grad_w_inner, grad_w_out, v = grads
    return (
        out[0], whole[0], grad_wq, grad_wk, grad_wv, grad_w_out, bias[0], bias[1], v[7],
        v[5], v[6], v[0], v[1], v[2], v[3],
        grad_w_inner, v[8 : 8 + ff // d].reshape(ff), grad_w_outer, v[4],
    )


def solution(mesh):
    rows = P("batch", "blk", None)
    in_specs = (rows, P("batch")) + (P(),) * 17 + (rows,)
    out_specs = (rows, rows) + (P(),) * 17
    return jax.shard_map(on_device, mesh=mesh, in_specs=in_specs, out_specs=out_specs, check_vma=False)
```

```python
import functools
import math

import jax
import jax.numpy as jnp
from jax import lax
from jax.experimental import pallas as pl
from jax.experimental.pallas import tpu as pltpu
from jax.sharding import PartitionSpec as P

HEADS = 8
F32 = jnp.float32
BF16 = jnp.bfloat16
FAR = -1e30
EPS = 1e-05
SPLIT_FROM = 0
LOG2E = math.log2(math.e)
LN2 = math.log(2.0)
GELU_C = math.sqrt(2.0 / math.pi)
GELU_K = 0.044715

VM = pl.BlockSpec(memory_space=pltpu.VMEM)
SM = pl.BlockSpec(memory_space=pltpu.SMEM)
ANY = pl.BlockSpec(memory_space=pl.ANY)
S = jax.ShapeDtypeStruct


def dot(a, b, dims):
    return lax.dot_general(a, b, (dims, ((), ())), preferred_element_type=F32)


def nn(a, b):
    return dot(a, b, ((1,), (0,)))


def nt(a, b):
    return dot(a, b, ((1,), (1,)))


def tn(a, b):
    return dot(a, b, ((0,), (0,)))


def params(mib=56):
    return pltpu.CompilerParams(vmem_limit_bytes=mib * 2**20)


def cost(flops, bytes_accessed):
    return pl.CostEstimate(flops=int(flops), bytes_accessed=int(bytes_accessed), transcendentals=0)


def head_size(features):
    return features // HEADS


def set_bias(bias, slot, me, length):
    rows = bias.shape[0]
    first = (me - slot) * rows
    partial = (slot == 0) | (first + rows > length)

    @pl.when(partial)
    def _():
        c = first + lax.broadcasted_iota(jnp.int32, bias.shape, 0)
        p = me * rows + lax.broadcasted_iota(jnp.int32, bias.shape, 1)
        bias[...] = jnp.where(c <= jnp.minimum(p, length - 1), 0.0, FAR)

    @pl.when(jnp.logical_not(partial))
    def _():
        bias[...] = jnp.zeros(bias.shape, F32)


def project_pair(w_kv, b_kv, x):
    kv = (nt(w_kv, x) + b_kv).astype(BF16)
    hd = kv.shape[0] // 4
    return [kv[:hd], kv[hd : 2 * hd]], [kv[2 * hd : 3 * hd], kv[3 * hd :]]


def attend_slot(x, q, w_kv, b_kv, bias, top_s, acc_s):
    pairs = w_kv.shape[0]
    rows = x.shape[0]

    def body(step, carry):
        for j in range(2):
            one_pair(step * 2 + j)
        return carry

    def one_pair(pair):
        ks, vs = project_pair(w_kv[pair], b_kv[pair], x[...])
        for i in range(2):
            h = pair * 2 + i
            logits = tn(ks[i], q[h]) + bias[...]
            old = top_s[h]
            top = jnp.maximum(jnp.max(logits, axis=0, keepdims=True), old)
            weights = jnp.exp2(logits - top).astype(BF16)
            v_one = jnp.concatenate([vs[i], jnp.ones((16, rows), BF16)], axis=0)
            acc_s[h] = nn(v_one, weights) + jnp.exp2(old - top) * acc_s[h]
            top_s[h] = top

    lax.fori_loop(0, pairs // 2, body, 0)


def own_kernel(bucket, ahead, me_ref, len_ref, x, wq, bq, w_kv, b_kv, *refs):
    more = refs[0]
    refs = refs[len(refs) - 4 - (ahead > 0) :]
    q_o, top_o, acc_o = refs[:3]
    bias = refs[-1]
    me = me_ref[0]
    length = len_ref[bucket]
    rows = x.shape[1]
    scale = head_size(x.shape[2]) ** -0.5 * LOG2E
    pairs = w_kv.shape[0]
    hd = q_o.shape[1]
    if ahead:
        refs[3][...] = more[0]

    def body(pair, carry):
        q = ((nt(wq[pair], x[0]) + bq[pair]) * scale).astype(BF16)
        q_o[2 * pair] = q[:hd]
        q_o[2 * pair + 1] = q[hd:]
        return carry

    lax.fori_loop(0, pairs, body, 0)
    top_o[...] = jnp.full(top_o.shape, FAR, F32)
    acc_o[...] = jnp.zeros(acc_o.shape, F32)

    @pl.when(me * rows < length)
    def _():
        set_bias(bias, 0, me, length)
        attend_slot(x.at[0], q_o, w_kv, b_kv, bias, top_o, acc_o)


def own_call(bucket, me, lengths, tokens, wq, bq, w_kv, b_kv, ahead, after):
    _, rows, d = tokens.shape
    hd = head_size(d)
    shapes = [S((HEADS, hd, rows), BF16), S((HEADS, 1, rows), F32), S((HEADS, hd + 16, rows), F32)]
    one = lambda b: pl.BlockSpec((1, rows, d), lambda i: (b, 0, 0))
    extra = [one(ahead)] if ahead else []
    shapes += [S((rows, d), BF16)] * len(extra)
    return pl.pallas_call(
        functools.partial(own_kernel, bucket, ahead),
        grid=(1,),
        out_shape=tuple(shapes),
        in_specs=[SM, SM, one(bucket)] + [VM] * 4 + extra + [ANY] * len(after),
        out_specs=(VM,) * len(shapes),
        scratch_shapes=[pltpu.VMEM((rows, rows), F32)],
        compiler_params=params(),
        cost_estimate=cost(8e9, 4e6),
        name=f"attend_own_{bucket}",
    )(me, lengths, tokens, wq, bq, w_kv, b_kv, *([tokens] if ahead else []), *after)


def far_kernel(bucket, count, first_slot, final, me_ref, len_ref, *refs):
    xs = refs[:count]
    q, top_i, acc_i, w_kv, b_kv = refs[count : count + 5]
    out_o, lse_o, x_s, top_s, acc_s, bias = refs[len(refs) - 6 :]
    me = me_ref[0]
    length = len_ref[bucket]
    rows = xs[0].shape[0]
    hd = acc_s.shape[1] - 16
    top_s[...] = top_i[...]
    acc_s[...] = acc_i[...]
    for i in range(count):

        @pl.when(me >= first_slot + i)
        def _(i=i):
            x_s[i] = xs[i][...]

    def body(slot, carry):
        first = (me - slot) * rows

        @pl.when(first < length)
        def _():
            set_bias(bias, slot, me, length)
            attend_slot(x_s.at[slot - first_slot], q, w_kv, b_kv, bias, top_s, acc_s)

        return carry

    lax.fori_loop(first_slot, jnp.minimum(me, first_slot + count - 1) + 1, body, 0)
    if not final:
        out_o[...] = top_s[...]
        lse_o[...] = acc_s[...]
        return

    def finish(h, carry):
        total = acc_s[h, hd : hd + 1]
        out_o[h] = (acc_s[h, :hd] / total).astype(BF16)
        lse_o[h] = top_s[h] + jnp.log2(total)
        return carry

    lax.fori_loop(0, HEADS, finish, 0)


def far_call(bucket, me, lengths, xs, q, top, acc, w_kv, b_kv, after, first_slot=1, final=True):
    rows, d = xs[0].shape
    hd = head_size(d)
    shapes = ((HEADS, hd, rows), (HEADS, 1, rows), (HEADS, hd + 16, rows))
    operands = [me, lengths, *xs, q, top, acc, w_kv, b_kv]
    specs = [SM, SM] + [VM] * (len(xs) + 5)
    out_shape = [S(shapes[0], BF16), S(shapes[1], F32)] if final else [S(shapes[1], F32), S(shapes[2], F32)]
    return pl.pallas_call(
        functools.partial(far_kernel, bucket, len(xs), first_slot, final),
        grid=(1,),
        out_shape=tuple(out_shape),
        in_specs=specs + [ANY] * len(after),
        out_specs=(VM,) * len(out_shape),
        scratch_shapes=[
            pltpu.VMEM((len(xs), rows, d), BF16),
            pltpu.VMEM(shapes[1], F32),
            pltpu.VMEM(shapes[2], F32),
            pltpu.VMEM((rows, rows), F32),
        ],
        compiler_params=params(),
        cost_estimate=cost(18e9, 5e6),
        name=f"attend_far_{bucket}_{first_slot}",
    )(*operands, *after)


def norm_stats(v):
    centered = v - jnp.mean(v, axis=-1, keepdims=True)
    r = lax.rsqrt(jnp.mean(centered * centered, axis=-1, keepdims=True) + EPS)
    return centered * r, r


def norm_grad(n, r, gain, upstream):
    gu = gain * upstream
    return r * (gu - jnp.mean(gu, axis=-1, keepdims=True) - n * jnp.mean(gu * n, axis=-1, keepdims=True))


def over_rows(v):
    return jnp.sum(v.astype(F32), axis=0, keepdims=True)


def mid_kernel(bucket, me_ref, len_ref, attn, x, cot, w_out, w_inner, w_outer, vecs, b_inner, *refs):
    (out_o, branch_o, g_o, delta_o, normed_o, active_o, ghid_o, gtwo_o, gb_o, sums_o,
     pre_s, n1_s, r1_s, dual_s, slope_s, acc_s,
     inner_s, outer_s, cot_s, normed_s, active_s, ghid_s, gtwo_s, sems) = refs[len(refs) - 24 :]
    copies_in = [
        pltpu.make_async_copy(a, b, sems.at[i])
        for i, (a, b) in enumerate([(w_inner, inner_s), (w_outer, outer_s), (cot.at[bucket], cot_s)])
    ]
    for copy in copies_in:
        copy.start()
    w_inner, w_outer, cot = inner_s, outer_s, cot_s
    copies_out = [
        pltpu.make_async_copy(a, b, sems.at[3 + i])
        for i, (a, b) in enumerate([(normed_s, normed_o), (active_s, active_o), (gtwo_s, gtwo_o), (ghid_s, ghid_o)])
    ]
    me = me_ref[0]
    length = len_ref[bucket]
    _, rows, d = out_o.shape
    ff = active_s.shape[1]
    up_step = min(512, ff)
    down_step = min(512, ff)
    block = min(512, rows)
    b_out, gain1, shift1, gain2, shift2, gain_f, shift_f, b_outer = (vecs[i : i + 1] for i in range(8))
    attn_t = attn[...].reshape(d, rows)
    pre_s[...] = tn(attn_t, w_out[...])

    def over_blocks(work):
        def body(i, carry):
            work(pl.ds(pl.multiple_of(i * block, block), block), i * block)
            return carry

        lax.fori_loop(0, rows // block, body, 0)

    def first_norm(at, _):
        pre = x[0, at].astype(F32) + (pre_s[at] + b_out)
        n1, r1 = norm_stats(pre)
        pre_s[at] = pre
        n1_s[at] = n1
        r1_s[at] = r1
        normed_s[at] = (n1 * gain1 + shift1).astype(BF16)

    over_blocks(first_norm)
    copies_out[0].start()
    copies_in[0].wait()
    copies_in[1].wait()
    acc_s[...] = jnp.zeros(acc_s.shape, F32)

    def lift(i):
        f = slice(i * up_step, i * up_step + up_step)
        return nn(normed_s[...], w_inner[:, f]) + b_inner[:, f]


    def up(i, carry):
        f = slice(i * up_step, i * up_step + up_step)
        h = lift(i)
        square = h * h
        t = jnp.tanh(h * (GELU_C + (GELU_C * GELU_K) * square))
        half = 0.5 + 0.5 * t
        active = (h * half).astype(BF16)
        active_s[:, f] = active
        slope_s[:, f] = half + (0.5 * h) * (1.0 - t * t) * (GELU_C + (3.0 * GELU_C * GELU_K) * square)
        acc_s[...] += nn(active, w_outer[f, :])
        return carry

    for i in range(ff // up_step):
        up(i, 0)
    copies_out[1].start()
    sums_o[...] = jnp.zeros(sums_o.shape, F32)
    copies_in[2].wait()

    def last_norms(at, start):
        branch_two = acc_s[at] + b_outer
        normed = n1_s[at] * gain1 + shift1
        n2, r2 = norm_stats(normed + branch_two)
        nf, rf = norm_stats(pre_s[at] + branch_two)
        out_o[0, at] = ((n2 * gain2 + shift2) + (nf * gain_f + shift_f)).astype(BF16)
        p = me * rows + start + lax.broadcasted_iota(jnp.int32, (block, 1), 0)
        g_out = jnp.where(p < length, cot[at].astype(F32), 0.0)
        g_dual = norm_grad(nf, rf, gain_f, g_out)
        g_two = norm_grad(n2, r2, gain2, g_out)
        g_branch_two = (g_two + g_dual).astype(BF16)
        gtwo_s[at] = g_branch_two
        dual_s[at] = g_dual
        acc_s[at] = g_two
        sums_o[0:1] += over_rows(g_out * n2)
        sums_o[1:2] += over_rows(g_out)
        sums_o[2:3] += over_rows(g_out * nf)
        sums_o[4:5] += over_rows(g_branch_two)

    over_blocks(last_norms)
    copies_out[2].start()
    sums_o[3:4] = sums_o[1:2]

    @pl.when(me * rows < length)
    def _():
        def down(i, carry):
            f = pl.ds(pl.multiple_of(i * down_step, down_step), down_step)
            g_hidden = (nt(gtwo_s[...], w_outer[f, :]) * slope_s[:, f]).astype(BF16)
            ghid_s[:, f] = g_hidden
            sums_o[pl.ds(8 + i, 1)] = over_rows(g_hidden)
            acc_s[...] += nt(g_hidden, w_inner[:, f])
            return carry

        lax.fori_loop(0, ff // down_step, down, 0)
        copies_out[3].start()

        def first_back(at, _):
            g_normed = acc_s[at]
            n1 = n1_s[at]
            g_branch = norm_grad(n1, r1_s[at], gain1, g_normed) + dual_s[at]
            branch_o[at] = g_branch
            g_b = g_branch.astype(BF16)
            gb_o[at] = g_b
            sums_o[5:6] += over_rows(g_normed * n1)
            sums_o[6:7] += over_rows(g_normed)
            sums_o[7:8] += over_rows(g_b)

        over_blocks(first_back)
        g_o[...] = nt(w_out[...], gb_o[...]).astype(BF16).reshape(g_o.shape)

        def head_delta(h, carry):
            delta_o[h] = jnp.sum(g_o[h].astype(F32) * attn[h].astype(F32), axis=0, keepdims=True)
            return carry

        lax.fori_loop(0, HEADS, head_delta, 0)

    @pl.when(me * rows >= length)
    def _():
        for ref in (branch_o, g_o, delta_o, ghid_s, gb_o):
            ref[...] = jnp.zeros(ref.shape, ref.dtype)
        copies_out[3].start()

    for copy in copies_out:
        copy.wait()


def mid_call(bucket, me, lengths, attn, tokens, cotangent, w_out, w_inner, w_outer, vecs, b_inner, out, after):
    buckets, rows, d = tokens.shape
    ff = w_inner.shape[1]
    hd = head_size(d)
    one = pl.BlockSpec((1, rows, d), lambda i: (bucket, 0, 0))
    return pl.pallas_call(
        functools.partial(mid_kernel, bucket),
        grid=(1,),
        out_shape=(
            S((buckets, rows, d), BF16),
            S((rows, d), F32),
            S((HEADS, hd, rows), BF16),
            S((HEADS, 1, rows), F32),
            S((rows, d), BF16),
            S((rows, ff), BF16),
            S((rows, ff), BF16),
            S((rows, d), BF16),
            S((rows, d), BF16),
            S((16, d), F32),
        ),
        in_specs=[SM, SM, VM, one, ANY, VM, ANY, ANY, VM, VM] + [ANY] * (len(out) + len(after)),
        out_specs=(one, VM, VM, VM, ANY, ANY, ANY, ANY, VM, VM),
        input_output_aliases={10: 0} if out else {},
        scratch_shapes=[
            pltpu.VMEM((rows, d), F32),
            pltpu.VMEM((rows, d), F32),
            pltpu.VMEM((rows, 1), F32),
            pltpu.VMEM((rows, d), F32),
            pltpu.VMEM((rows, ff), F32),
            pltpu.VMEM((rows, d), F32),
            pltpu.VMEM((d, ff), BF16),
            pltpu.VMEM((ff, d), BF16),
            pltpu.VMEM((rows, d), BF16),
            pltpu.VMEM((rows, d), BF16),
            pltpu.VMEM((rows, ff), BF16),
            pltpu.VMEM((rows, ff), BF16),
            pltpu.VMEM((rows, d), BF16),
            pltpu.SemaphoreType.DMA((7,)),
        ],
        compiler_params=params(),
        cost_estimate=cost(12e9, 14e6),
        name=f"feed_forward_{bucket}",
    )(me, lengths, attn, tokens, cotangent, w_out, w_inner, w_outer, vecs, b_inner, *out, *after)


def wgrad_job(step, half, core):
    return step % half + jnp.where(step < half, 1 - core, core) * half


def rows_of(refs):
    return jnp.concatenate([r[...] for r in refs], axis=0)


def wgrad_kernel(buckets, count, half, places, *refs):
    groups = [refs[i * buckets : (i + 1) * buckets] for i in range(7)]
    active, g_two, normed, g_hidden, attn, g_b, sums = groups
    kept_o, sent_o = refs[7 * buckets :]
    step = pl.program_id(0)
    job = wgrad_job(step, half, places[0])

    def put(value):
        @pl.when(step < half)
        def _():
            sent_o[...] = value

        @pl.when(step >= half)
        def _():
            kept_o[...] = value

    @pl.when(job < count)
    def _():
        put(tn(rows_of(active), rows_of(g_two)).astype(BF16))

    @pl.when((job >= count) & (job < 2 * count))
    def _():
        put(tn(rows_of(normed), rows_of(g_hidden)).astype(BF16))

    @pl.when(job == 2 * count)
    def _():
        put(sum(nn(a[...], g[...]) for a, g in zip(attn, g_b)).astype(BF16))

    @pl.when(job > 2 * count)
    def _():
        put(jnp.zeros(kept_o.shape, BF16))

    @pl.when(job == 2 * count + 1)
    def _():
        value = sum(s[...] for s in sums).astype(BF16)

        @pl.when(step < half)
        def _():
            sent_o[:16] = value

        @pl.when(step >= half)
        def _():
            kept_o[:16] = value


def wgrad_call(places, devices, active, g_two, normed, g_hidden, attn, g_b, sums):
    buckets = len(active)
    rows, ff = active[0].shape
    d = g_two[0].shape[1]
    count = ff // d
    half = count + 1
    while 2 * half * d % (16 * devices):
        half += 1
    clip = lambda v, top: jnp.minimum(jnp.maximum(v, 0), top)
    job = lambda j, p: wgrad_job(j, half, p[0])
    full = pl.BlockSpec((rows, d), lambda j, p: (0, 0))
    tall = pl.BlockSpec((d, rows), lambda j, p: (0, 0))
    active_spec = pl.BlockSpec((rows, d), lambda j, p: (0, clip(job(j, p), count - 1)))
    hid_spec = pl.BlockSpec((rows, d), lambda j, p: (0, clip(job(j, p) - count, count - 1)))
    attn2 = [a.reshape(d, rows) for a in attn]
    return pl.pallas_call(
        functools.partial(wgrad_kernel, buckets, count, half),
        grid_spec=pltpu.PrefetchScalarGridSpec(
            num_scalar_prefetch=1,
            grid=(2 * half,),
            in_specs=[active_spec] * buckets + [full] * buckets + [full] * buckets + [hid_spec] * buckets
            + [tall] * buckets + [full] * buckets + [pl.BlockSpec((16, d), lambda j, p: (0, 0))] * buckets,
            out_specs=(
                pl.BlockSpec((d, d), lambda j, p: (jnp.maximum(j - half, 0), 0)),
                pl.BlockSpec((d, d), lambda j, p: (jnp.minimum(j, half - 1), 0)),
            ),
        ),
        out_shape=(S((half * d, d), BF16),) * 2,
        compiler_params=params(),
        cost_estimate=cost(buckets * 5e9, 20e6),
        name="weight_gradients",
    )(places, *active, *g_two, *normed, *g_hidden, *attn2, *g_b, *sums)


def attend_back(x, q, g, w_kv, b_kv, lse, delta, bias, dq_s, kv_s, dkv_s):
    pairs, width, d = w_kv.shape
    hd = width // 4
    rows = x.shape[0]
    block = 2 * width

    def project(i, carry):
        at = pl.ds(pl.multiple_of(i * block, block), block)
        w = w_kv[pl.ds(2 * i, 2)].reshape(block, d)
        kv_s[at] = (nt(w, x[...]) + b_kv[pl.ds(2 * i, 2)].reshape(block, 1)).astype(BF16)
        return carry

    lax.fori_loop(0, pairs // 2, project, 0)

    def body(step, carry):
        for j in range(2):
            one_pair(step * 2 + j)
        return carry

    def one_pair(pair):
        base = pl.multiple_of(pair * width, width)
        for i in range(2):
            h = pair * 2 + i
            at_k = pl.ds(base + i * hd, hd)
            at_v = pl.ds(base + (2 + i) * hd, hd)
            k = kv_s[at_k]
            q_t, g_t = q[h], g[h]
            probs = jnp.exp2(tn(k, q_t) + bias[...] - lse[h])
            g_probs = tn(kv_s[at_v], g_t)
            g_logits = (probs * (g_probs - delta[h])).astype(BF16)
            dkv_s[at_v] = nt(g_t, probs.astype(BF16)).astype(BF16)
            dkv_s[at_k] = (nt(q_t, g_logits) * LN2).astype(BF16)
            dq_s[h] += nn(k, g_logits)

    lax.fori_loop(0, pairs // 2, body, 0)


def back_kernel(bucket, low, high, fresh, first, final, places, me_ref, len_ref, *refs):
    count = high - low + 1
    refs = list(refs)
    take = lambda n: [refs.pop(0) for _ in range(n)]
    xs = take(count)
    q, g, lse, delta, w_kv, b_kv = take(6)
    sems = refs.pop()
    wq, branch = take(2) if low == 0 else (None, None)
    dq_i = None if fresh else take(1)[0]
    sums_i = None if first else take(1)[0]
    x_s, kv_s, dkv_s, dq_s, dx_s, bias, *late = refs[len(refs) - 6 - (low == 0) - (not first) :]
    refs = refs[: len(refs) - 6 - len(late)]
    refs = refs[len(refs) - 2 - final - (high > 0) :]
    dx_o = refs.pop(0) if high > 0 else None
    last_o, *sums_o = refs
    me = me_ref[0]
    length = len_ref[bucket]
    rows, d = xs[0].shape
    hd = g.shape[1]
    live = me * rows < length
    dq_s[...] = jnp.zeros(dq_s.shape, F32) if fresh else dq_i[...]
    rows_in = [
        pltpu.make_async_copy(xs[i], x_s.at[pl.ds(i * rows, rows)], sems.at[i]) for i in range(count)
    ]
    late_in = [
        pltpu.make_async_copy(source, to, sems.at[count + j])
        for j, (source, to) in enumerate(zip([branch] * (low == 0) + [sums_i] * (not first), late))
    ]
    for copy in rows_in + late_in:
        copy.start()

    def take_rows(i):
        for j in range(count):

            @pl.when(i == j)
            def _(j=j):
                rows_in[j].wait()

    def dx_out(i):
        return pltpu.make_async_copy(dx_s.at[i], dx_o.at[i], sems.at[count + 2 + i])

    def body(i, carry):
        slot = high - i
        at = pl.ds(pl.multiple_of(i * rows, rows), rows)
        active = live & (me >= slot)
        take_rows(i)

        @pl.when(active)
        def _():
            set_bias(bias, slot, me, length)
            attend_back(x_s.at[at], q, g, w_kv, b_kv, lse, delta, bias, dq_s, kv_s, dkv_s.at[:, at])

        @pl.when(active & (slot > 0))
        def _():
            dx_s[i] = tn(dkv_s[:, at], w_kv[...].reshape(2 * d, d)).astype(BF16)

        @pl.when(jnp.logical_not(active))
        def _():
            dkv_s[:, at] = jnp.zeros((2 * d, rows), BF16)

        @pl.when(jnp.logical_not(active) & (slot > 0))
        def _():
            dx_s[i] = jnp.zeros((rows, d), BF16)

        @pl.when(slot > 0)
        def _():
            dx_out(i).start()

        return carry

    lax.fori_loop(0, count, body, 0)
    pairs = HEADS // 2
    dq = (dq_s[...] * hd**-0.5).astype(BF16).reshape(d, rows)
    here = slice((count - 1) * rows, count * rows)
    for copy in late_in:
        copy.wait()
    if low == 0:
        last_o[...] = late[0][...]

        @pl.when(live)
        def _():
            last_o[...] += tn(dkv_s[:, here], w_kv[...].reshape(2 * d, d)) + tn(dq, wq[...])
    else:
        last_o[...] = dq_s[...]

    half = HEADS // 4
    ones = jnp.ones((8, count * rows), BF16)

    def add(pair, carry):
        at = pl.ds(pl.multiple_of(pair * 4 * hd, 4 * hd), 4 * hd)
        dkv = dkv_s[at, :]
        parts = [None, nn(dkv, x_s[...]), None]
        bias_sums = [nt(ones, dkv), jnp.zeros((8, d - 4 * hd), F32)]
        if low == 0:
            dq_pair = (dq_s[pl.ds(2 * pair, 2)] * hd**-0.5).astype(BF16).reshape(2 * hd, rows)
            parts[0] = nn(dq_pair, x_s[here])
            bias_sums[1:] = [nt(ones[:, :rows], dq_pair), jnp.zeros((8, d - 6 * hd), F32)]
        else:
            parts[0] = jnp.zeros((2 * hd, d), F32)
        parts[2] = jnp.concatenate([jnp.concatenate(bias_sums, axis=1), jnp.zeros((8, d), F32)])
        value = jnp.concatenate(parts, axis=0)
        if not first:
            value = value + late[-1][pair].astype(F32)
        value = value.astype(BF16)
        if final:
            kept = pair // half == places[0]
            to = pl.ds(pl.multiple_of((pair % half) * 6 * hd, 6 * hd), 6 * hd)
            to_bias = pl.ds(pl.multiple_of(half * 6 * hd + (pair % half) * 16, 16), 16)

            def put(ref):
                ref[to] = value[: 6 * hd]
                ref[to_bias] = value[6 * hd :]

            @pl.when(kept)
            def _():
                put(sums_o[0])

            @pl.when(jnp.logical_not(kept))
            def _():
                put(sums_o[1])
        else:
            sums_o[0][pair] = value
        return carry

    if final:
        used = half * (6 * hd + 16)
        for ref in sums_o:
            if used < ref.shape[0]:
                ref[used:] = jnp.zeros((ref.shape[0] - used, d), BF16)
    lax.fori_loop(0, pairs, add, 0)
    for i in range(count - (low == 0)):
        dx_out(i).wait()


def back_call(
    bucket, low, high, places, me, lengths, xs, q, g, lse, delta, w_kv, b_kv, wq, branch, dq, sums, final, after
):
    rows, d = xs[0].shape
    hd = head_size(d)
    own = low == 0
    fresh = dq is None
    far = high - max(low, 1) + 1
    operands = [places, me, lengths, *xs, q, g, lse, delta, w_kv, b_kv]
    specs = [SM] * 3 + [ANY] * len(xs) + [VM] * 6
    late = []
    if own:
        operands += [wq.reshape(d, d), branch]
        specs += [VM, ANY]
        late.append(branch)
    if not fresh:
        operands.append(dq)
        specs.append(VM)
    if sums is not None:
        operands.append(sums)
        specs.append(ANY)
        late.append(sums)
    sums_shape = (HEADS // 2, 6 * hd + 16, d)
    out_shape = [S((far, rows, d), BF16)] if far else []
    out_shape += [S((rows, d), F32) if own else S((HEADS, hd, rows), F32)]
    out_shape += [S((final, d), BF16)] * 2 if final else [S(sums_shape, BF16)]
    outs = pl.pallas_call(
        functools.partial(back_kernel, bucket, low, high, fresh, sums is None, final > 0),
        grid=(1,),
        out_shape=tuple(out_shape),
        in_specs=specs + [ANY] * len(after),
        out_specs=((ANY,) if far else ()) + (VM,) * (len(out_shape) - (far > 0)),
        scratch_shapes=[
            pltpu.VMEM((len(xs) * rows, d), BF16),
            pltpu.VMEM((2 * d, rows), BF16),
            pltpu.VMEM((2 * d, len(xs) * rows), BF16),
            pltpu.VMEM((HEADS, hd, rows), F32),
            pltpu.VMEM((max(far, 1), rows, d), BF16),
            pltpu.VMEM((rows, rows), F32),
            *[pltpu.VMEM(a.shape, a.dtype) for a in late],
            pltpu.SemaphoreType.DMA((2 * len(xs) + 2,)),
        ],
        compiler_params=params(36),
        cost_estimate=cost(10e9 * len(xs), 14e6),
        name=f"attend_back_{bucket}_{high}",
    )(*operands, *after)
    last = len(out_shape) - (3 if final else 2)
    return (outs[0] if far else None), outs[last], (outs[last + 1 :] if final else outs[-1])


def step_call(name, places, jobs, after):
    operands, specs, shapes, bodies = [places], [SM], [], []
    for job_in, job_specs, job_out, body in jobs:
        bodies.append((len(job_in), len(job_out), body))
        operands += job_in
        specs += job_specs
        shapes += job_out
    first_out = len(operands) + len(after)

    def kernel(places_ref, *refs):
        at_in, at_out = 0, first_out - 1
        for n_in, n_out, body in bodies:
            body(places_ref, *refs[at_in : at_in + n_in], *refs[at_out : at_out + n_out])
            at_in += n_in
            at_out += n_out

    outs = pl.pallas_call(
        kernel,
        grid=(1,),
        out_shape=tuple(shapes),
        in_specs=specs + [ANY] * len(after),
        out_specs=(VM,) * len(shapes),
        compiler_params=params(16),
        cost_estimate=cost(2e9, 4e6),
        name=name,
    )(*operands, *after)
    found = []
    for _, n_out, _ in bodies:
        found.append(outs[:n_out])
        outs = outs[n_out:]
    return found


def gate(arrays, after):
    outs = pl.pallas_call(
        lambda *refs: None,
        out_shape=tuple(S(a.shape, a.dtype) for a in arrays),
        in_specs=[ANY] * (len(arrays) + len(after)),
        out_specs=(ANY,) * len(arrays),
        input_output_aliases={i: i for i in range(len(arrays))},
        name="gate",
    )(*arrays, *after)
    return list(outs)


class Group:
    def __init__(self, index, axis, low, high):
        self.index, self.axis, self.low, self.count = index, axis, low, 1 << (high - low)
        self.place = (lax.axis_index(axis) >> low) & (self.count - 1)

    def swap(self, value, mask):
        size = lax.axis_size(self.axis)
        return lax.ppermute(value, self.axis, [(i, i ^ (mask << self.low)) for i in range(size)])


def part_rows(place, mask, size):
    return pl.ds(pl.multiple_of((place ^ mask) * size, size), size)


def total(kept, got, at):
    values = [r[at].astype(F32) for r in [kept, *got]]
    while len(values) > 1:
        values = [a + b for a, b in zip(values[::2], values[1::2])]
    return values[0].astype(BF16)


def split_job(kept, got, group):
    rows, d = kept.shape
    count = group.count if group else 1
    size = rows // count

    def body(places, kept, *refs):
        arrived, outs = refs[: len(got)], refs[len(got) :]
        for m in range(count):
            at = part_rows(places[group.index], m, size) if group else slice(None)
            outs[m][...] = total(kept, arrived, at)

    return [kept, *got], [VM] * (1 + len(got)), [S((size, d), BF16)] * count, body


def join_job(part, got, group):
    size, d = part.shape

    def body(places, *refs):
        for m in range(group.count):
            refs[-1][part_rows(places[group.index], m, size)] = refs[m][...]

    return [part, *got], [VM] * (1 + len(got)), [S((size * group.count, d), BF16)], body


def message_job(dx, at, carry):
    _, rows, d = dx.shape
    more = [] if carry is None else [carry]

    def body(places, dx, *refs):
        if more:
            refs[-1][...] = (dx[0].astype(F32) + refs[0][...].astype(F32)).astype(BF16)
        else:
            refs[-1][...] = dx[0]

    specs = [pl.BlockSpec((1, rows, d), lambda i: (at, 0, 0))] + [VM] * len(more)
    return [dx, *more], specs, [S((rows, d), BF16)], body


def sum_over_devices(kept, sent, groups, full=False):
    first, *rest = groups
    got = [first.swap(sent, 1)]
    scatter = rest[:-1] if full else rest
    for group in scatter:
        kept, *shards = yield split_job(kept, got, group)
        got = [group.swap(s, m + 1) for m, s in enumerate(shards)]
    (part,) = yield split_job(kept, got, None)
    if full and rest:
        got = [rest[-1].swap(part, m) for m in range(1, rest[-1].count)]
        (part,) = yield split_job(part, got, None)
    for group in reversed(scatter):
        got = [group.swap(part, m) for m in range(1, group.count)]
        (part,) = yield join_job(part, got, group)
    return part, first.swap(part, 1)


def send_back(pieces, n):
    carry = None
    for i, slot in enumerate(range(n - 1, 0, -1)):
        (message,) = yield message_job(*pieces(i), carry)
        carry = lax.ppermute(message, "blk", [(j, j - 1) for j in range(slot, n)])
    return carry


class Process:
    def __init__(self, steps):
        self.steps, self.result = steps, None
        self.job = next(steps)

    def advance(self, outs):
        try:
            self.job = self.steps.send(outs)
        except StopIteration as end:
            self.job, self.result = None, end.value


class Board:
    def __init__(self, places):
        self.places, self.active, self.ticks = places, [], 0

    def start(self, steps):
        self.active.append(Process(steps))
        return self.active[-1]

    def tick(self, after, only=None):
        self.ticks += 1
        now = self.active if only is None else only
        outs = step_call(f"step_{self.ticks}", self.places, [p.job for p in now], after)
        for p, o in zip(list(now), outs):
            p.advance(o)
        self.active = [p for p in self.active if p.job is not None]
        return [o for group in outs for o in group]


def big_kernel(ff, places, mine, got, *refs):
    outer_o, inner_o, out_o, vec_o = refs[len(refs) - 4 :]
    half, d = mine.shape
    count = ff // d
    for own_half in range(2):

        @pl.when(places[0] == own_half)
        def _(own_half=own_half):
            for i in range(2 * half // d):
                src = mine if i // (half // d) == own_half else got
                at = (i % (half // d)) * d
                value = src[at : at + d]
                if i < count:
                    outer_o[i * d : i * d + d] = value.astype(F32)
                elif i < 2 * count:
                    inner_o[:, (i - count) * d : (i - count) * d + d] = value.astype(F32)
                elif i == 2 * count:
                    out_o[...] = value.astype(F32)
                elif i == 2 * count + 1:
                    vec_o[...] = value[:16].astype(F32)


def big_call(places, mine, got, ff, after):
    d = mine.shape[1]
    shapes = (S((ff, d), F32), S((d, ff), F32), S((d, d), F32), S((16, d), F32))
    return pl.pallas_call(
        functools.partial(big_kernel, ff),
        grid=(1,),
        out_shape=shapes,
        in_specs=[SM, VM, VM] + [ANY] * len(after),
        out_specs=(VM,) * 4,
        compiler_params=params(24),
        cost_estimate=cost(5e9, 14e6),
        name="feed_forward_sums",
    )(places, mine, got, *after)


def small_kernel(places, mine, got, *refs):
    weights, bias_o = refs[len(refs) - 4 : len(refs) - 1], refs[-1]
    d = weights[0].shape[0]
    hd = head_size(d)
    half = HEADS // 4
    bias_o[...] = jnp.zeros(bias_o.shape, F32)
    for own_half in range(2):

        @pl.when(places[0] == own_half)
        def _(own_half=own_half):
            for pair in range(HEADS // 2):
                src = mine if pair // half == own_half else got
                at = (pair % half) * 6 * hd
                at_bias = half * 6 * hd + (pair % half) * 16
                lanes = slice(2 * hd * pair, 2 * hd * pair + 2 * hd)
                for k in range(3):
                    rows = src[at + 2 * hd * k : at + 2 * hd * k + 2 * hd].astype(F32)
                    weights[k][:, lanes] = rows.T
                bias = src[at_bias : at_bias + 16].astype(F32)
                bias_o[0:1, lanes] = bias[:1, 4 * hd : 6 * hd]
                bias_o[1:2, lanes] = bias[:1, 2 * hd : 4 * hd]


def small_call(places, mine, got):
    d = mine.shape[1]
    return pl.pallas_call(
        small_kernel,
        grid=(1,),
        out_shape=(S((d, d), F32),) * 3 + (S((8, d), F32),),
        in_specs=[SM, VM, VM],
        out_specs=(VM,) * 4,
        compiler_params=params(16),
        cost_estimate=cost(2e9, 5e6),
        name="attention_sums",
    )(places, mine, got)


def tokens_kernel(mine, carry, *refs):
    refs[-1][0] = mine[...] + carry[...].astype(F32)


def tokens_call(bucket, buckets, mine, carry, whole, after):
    rows, d = mine.shape
    return pl.pallas_call(
        tokens_kernel,
        grid=(1,),
        out_shape=S((buckets, rows, d), F32),
        in_specs=[VM, VM] + [ANY] * (len(whole) + len(after)),
        out_specs=pl.BlockSpec((1, rows, d), lambda i: (bucket, 0, 0)),
        input_output_aliases={2: 0} if whole else {},
        compiler_params=params(16),
        cost_estimate=cost(2e9, 3e6),
        name=f"token_gradients_{bucket}",
    )(mine, carry, *whole, *after)


def on_device(
    tokens, lengths, w_query, w_key, w_value, w_out, b_query, b_value, b_out, norm1_gain, norm1_bias,
    norm2_gain, norm2_bias, final_gain, final_bias, w_inner, b_inner, w_outer, b_outer, cotangent,
):
    buckets, rows, d = tokens.shape
    ff = w_inner.shape[1]
    hd = head_size(d)
    pairs = HEADS // 2
    n = lax.axis_size("blk")
    me = lax.axis_index("blk").astype(jnp.int32).reshape(1)
    bits = lambda axis: (lax.axis_size(axis) - 1).bit_length()
    groups = [Group(0, "batch", 0, 1), Group(1, "batch", 1, bits("batch")), Group(2, "blk", 0, bits("blk"))]
    places = jnp.stack([g.place for g in groups]).astype(jnp.int32)
    devices = math.prod(g.count for g in groups)
    groups = [groups[0]] + [g for g in groups[1:] if g.count > 1]

    paired = lambda w: w.T.reshape(pairs, 2 * hd, d)
    wq = paired(w_query)
    bq = b_query.reshape(pairs, 2 * hd, 1)
    w_kv = jnp.concatenate([paired(w_key), paired(w_value)], axis=1)
    b_v = b_value.reshape(pairs, 2 * hd, 1)
    b_kv = jnp.concatenate([jnp.zeros_like(b_v), b_v], axis=1)
    vecs = jnp.stack([b_out, norm1_gain, norm1_bias, norm2_gain, norm2_bias, final_gain, final_bias, b_outer])
    b_in = b_inner.reshape(1, ff)

    def hop(value, slot):
        return lax.ppermute(value, "blk", [(i, i + 1) for i in range(slot - 1, n - 1)])

    run_own = lambda b, after: own_call(b, me, lengths, tokens, wq, bq, w_kv, b_kv, (b + 1) % buckets, after)
    run_far = lambda b, after: far_call(b, me, lengths, held[b][1:], own[b][0], own[b][1], own[b][2], w_kv, b_kv, after)
    run_mid = lambda b, out, after: mid_call(
        b, me, lengths, attns[b], tokens, cotangent, w_out, w_inner, w_outer, vecs, b_in, out, after
    )
    held = [[tokens[b]] for b in range(buckets)]
    own, mids, attns, lses, out = [], [], [], [], []
    moving = {}
    if n == 4 and buckets == 3:
        plan = [
            ([(0, 1)], [(0, 2), (1, 1)]),
            ([], []),
            ([(0, 2), (1, 1)], [(0, 3)]),
            ([(0, 3)], [(1, 2), (2, 1)]),
            ([(1, 2)], [(1, 3)]),
            ([(1, 3), (2, 1)], [(2, 2)]),
            ([(2, 2)], [(2, 3)]),
            ([(2, 3)], []),
        ]
    else:
        plan = []
        for b in range(buckets):
            for slot in range(1, n):
                source = held[b][-1]
                held[b].append(hop(source, slot))
    if plan:
        moving[0, 1] = hop(tokens[0], 1)

    def passing(kernel, last):
        if kernel >= len(plan):
            return [last]
        arrived, next_hops = plan[kernel]
        if not arrived:
            return [last]
        fresh = [b for b, slot in next_hops if slot == 1]
        held_on = [(b, slot - 1) for b, slot in next_hops if slot > 1 and (b, slot - 1) not in arrived]
        values = [moving.pop(k) for k in arrived] + [held[b][slot] for b, slot in held_on]
        passed = gate(values + [own[b - 1][3] for b in fresh], [last])
        for k, value in zip(arrived, passed):
            held[k[0]].append(value)
        for (b, slot), value in zip(held_on, passed[len(arrived) :]):
            held[b][slot] = value
        starts = dict(zip(fresh, passed[len(values) :]))
        for b, slot in next_hops:
            moving[b, slot] = hop(starts[b] if slot == 1 else held[b][slot - 1], slot)
        return passed[:1]

    after = [vecs, b_in]
    for b in range(buckets):
        own.append(run_own(b, after))
        after = passing(b, own[b][0])
    extra = 0
    if plan:
        early = far_call(0, me, lengths, held[0][1:3], *own[0][:3], w_kv, b_kv, after, 1, False)
        own[0] = (own[0][0], *early)
        after = passing(buckets, early[0])
        extra = 1
    for b in range(buckets):
        if b == 0 and plan:
            attn, lse = far_call(0, me, lengths, held[0][3:], *own[0][:3], w_kv, b_kv, after, 3, True)
        else:
            attn, lse = run_far(b, after)
        attns.append(attn)
        lses.append(lse)
        after = passing(buckets + extra + 2 * b, lse)
        mids.append(run_mid(b, out, after))
        out = [mids[b][0]]
        after = passing(buckets + extra + 2 * b + 1, mids[b][9])
    column = lambda i: [m[i] for m in mids]
    kept, sent = wgrad_call(
        places, devices, column(5), column(7), column(4), column(6), attns, column(8), column(9)
    )

    final_rows = HEADS // 4 * (6 * hd + 16)
    final_rows += -final_rows % (16 * lax.axis_size("batch") // 2)

    board = Board(places)
    big = board.start(sum_over_devices(kept, sent, groups))
    waiting = [sent]
    mine, returns = [], []
    resting = lambda: [p for p in board.active if p is not big] if board.ticks == 1 else None
    sums = None
    for b in range(buckets):
        g, delta, branch = mids[b][2], mids[b][3], mids[b][1]
        args = (own[b][0], g, lses[b], delta, w_kv, b_kv, wq, branch)
        dx = {}
        last = final_rows if b + 1 == buckets else 0
        cut = max(1, n // 2) if b >= SPLIT_FROM else 0
        pieces = lambda i, dx=dx, cut=cut: (dx[0], i) if i < n - max(cut, 1) else (dx[1], i - (n - cut))
        if cut:
            there = held[b][n - 1 : cut - 1 : -1]
            dx[0], dq, sums = back_call(b, cut, n - 1, places, me, lengths, there, *args, None, sums, 0, waiting)
            returns.append(board.start(send_back(pieces, n)))
            waiting = board.tick([sums], resting())
            there = held[b][cut - 1 :: -1]
            dx[1], own_part, sums = back_call(b, 0, cut - 1, places, me, lengths, there, *args, dq, sums, last, waiting)
            if not last:
                waiting = board.tick([sums], resting())
        else:
            dx[0], own_part, sums = back_call(b, 0, n - 1, places, me, lengths, held[b][::-1], *args, None, sums, last, waiting)
            returns.append(board.start(send_back(pieces, n)))
            waiting = board.tick([sums])
        mine.append(own_part)
    after = [sums[1]]
    whole, grads, done = [], None, set()
    alone = 2
    landed = lambda: [r.result for r in returns if r.result is not None]
    if board.active:
        after = board.tick(after + landed())[:1]
    small_first = Process(sum_over_devices(*gate(list(sums), after), groups, n > 1))
    board.active.append(small_first)
    while board.active:
        sent = board.tick(landed() + after, [small_first] if alone > 0 else None)
        alone, after = alone - 1, sent[:1]
        ready = [b for b in range(buckets) if b not in done and returns[b].result is not None]
        if grads is None and big.result is not None:
            grads = big_call(places, *big.result, ff, sent)
            after = [grads[3]]
        elif ready:
            b = ready[0]
            whole = [tokens_call(b, buckets, mine[b], returns[b].result, whole, sent)]
            done.add(b)
            after = whole
    for b in range(buckets):
        if b not in done:
            whole = [tokens_call(b, buckets, mine[b], returns[b].result, whole, [])]
    grad_wq, grad_wk, grad_wv, bias = small_call(places, *small_first.result)
    grad_w_outer, grad_w_inner, grad_w_out, v = grads
    return (
        out[0], whole[0], grad_wq, grad_wk, grad_wv, grad_w_out, bias[0], bias[1], v[7],
        v[5], v[6], v[0], v[1], v[2], v[3],
        grad_w_inner, v[8 : 8 + ff // d].reshape(ff), grad_w_outer, v[4],
    )


def solution(mesh):
    rows = P("batch", "blk", None)
    in_specs = (rows, P("batch")) + (P(),) * 17 + (rows,)
    out_specs = (rows, rows) + (P(),) * 17
    return jax.shard_map(on_device, mesh=mesh, in_specs=in_specs, out_specs=out_specs, check_vma=False)
```

```python
import functools
import math

import jax
import jax.numpy as jnp
from jax import lax
from jax.experimental import pallas as pl
from jax.experimental.pallas import tpu as pltpu
from jax.sharding import PartitionSpec as P

HEADS = 8
F32 = jnp.float32
BF16 = jnp.bfloat16
FAR = -1e30
EPS = 1e-05
SPLIT_FROM = 0
LOG2E = math.log2(math.e)
LN2 = math.log(2.0)
GELU_C = math.sqrt(2.0 / math.pi)
GELU_K = 0.044715

VM = pl.BlockSpec(memory_space=pltpu.VMEM)
SM = pl.BlockSpec(memory_space=pltpu.SMEM)
ANY = pl.BlockSpec(memory_space=pl.ANY)
S = jax.ShapeDtypeStruct


def dot(a, b, dims):
    return lax.dot_general(a, b, (dims, ((), ())), preferred_element_type=F32)


def nn(a, b):
    return dot(a, b, ((1,), (0,)))


def nt(a, b):
    return dot(a, b, ((1,), (1,)))


def tn(a, b):
    return dot(a, b, ((0,), (0,)))


def params(mib=56):
    return pltpu.CompilerParams(vmem_limit_bytes=mib * 2**20)


def cost(flops, bytes_accessed):
    return pl.CostEstimate(flops=int(flops), bytes_accessed=int(bytes_accessed), transcendentals=0)


def head_size(features):
    return features // HEADS


def set_bias(bias, slot, me, length):
    rows = bias.shape[0]
    first = (me - slot) * rows
    partial = (slot == 0) | (first + rows > length)

    @pl.when(partial)
    def _():
        c = first + lax.broadcasted_iota(jnp.int32, bias.shape, 0)
        p = me * rows + lax.broadcasted_iota(jnp.int32, bias.shape, 1)
        bias[...] = jnp.where(c <= jnp.minimum(p, length - 1), 0.0, FAR)

    @pl.when(jnp.logical_not(partial))
    def _():
        bias[...] = jnp.zeros(bias.shape, F32)


def project_pair(w_kv, b_kv, x):
    kv = (nt(w_kv, x) + b_kv).astype(BF16)
    hd = kv.shape[0] // 4
    return [kv[:hd], kv[hd : 2 * hd]], [kv[2 * hd : 3 * hd], kv[3 * hd :]]


def attend_slot(x, q, w_kv, b_kv, bias, top_s, acc_s):
    pairs = w_kv.shape[0]
    rows = x.shape[0]

    def body(step, carry):
        for j in range(2):
            one_pair(step * 2 + j)
        return carry

    def one_pair(pair):
        ks, vs = project_pair(w_kv[pair], b_kv[pair], x[...])
        for i in range(2):
            h = pair * 2 + i
            logits = tn(ks[i], q[h]) + bias[...]
            old = top_s[h]
            top = jnp.maximum(jnp.max(logits, axis=0, keepdims=True), old)
            weights = jnp.exp2(logits - top).astype(BF16)
            v_one = jnp.concatenate([vs[i], jnp.ones((16, rows), BF16)], axis=0)
            acc_s[h] = nn(v_one, weights) + jnp.exp2(old - top) * acc_s[h]
            top_s[h] = top

    lax.fori_loop(0, pairs // 2, body, 0)


def own_kernel(bucket, ahead, me_ref, len_ref, x, wq, bq, w_kv, b_kv, *refs):
    more = refs[0]
    refs = refs[len(refs) - 4 - (ahead > 0) :]
    q_o, top_o, acc_o = refs[:3]
    bias = refs[-1]
    me = me_ref[0]
    length = len_ref[bucket]
    rows = x.shape[1]
    scale = head_size(x.shape[2]) ** -0.5 * LOG2E
    pairs = w_kv.shape[0]
    hd = q_o.shape[1]
    if ahead:
        refs[3][...] = more[0]

    def body(pair, carry):
        q = ((nt(wq[pair], x[0]) + bq[pair]) * scale).astype(BF16)
        q_o[2 * pair] = q[:hd]
        q_o[2 * pair + 1] = q[hd:]
        return carry

    lax.fori_loop(0, pairs, body, 0)
    top_o[...] = jnp.full(top_o.shape, FAR, F32)
    acc_o[...] = jnp.zeros(acc_o.shape, F32)

    @pl.when(me * rows < length)
    def _():
        set_bias(bias, 0, me, length)
        attend_slot(x.at[0], q_o, w_kv, b_kv, bias, top_o, acc_o)


def own_call(bucket, me, lengths, tokens, wq, bq, w_kv, b_kv, ahead, after):
    _, rows, d = tokens.shape
    hd = head_size(d)
    shapes = [S((HEADS, hd, rows), BF16), S((HEADS, 1, rows), F32), S((HEADS, hd + 16, rows), F32)]
    one = lambda b: pl.BlockSpec((1, rows, d), lambda i: (b, 0, 0))
    extra = [one(ahead)] if ahead else []
    shapes += [S((rows, d), BF16)] * len(extra)
    return pl.pallas_call(
        functools.partial(own_kernel, bucket, ahead),
        grid=(1,),
        out_shape=tuple(shapes),
        in_specs=[SM, SM, one(bucket)] + [VM] * 4 + extra + [ANY] * len(after),
        out_specs=(VM,) * len(shapes),
        scratch_shapes=[pltpu.VMEM((rows, rows), F32)],
        compiler_params=params(),
        cost_estimate=cost(8e9, 4e6),
        name=f"attend_own_{bucket}",
    )(me, lengths, tokens, wq, bq, w_kv, b_kv, *([tokens] if ahead else []), *after)


def far_kernel(bucket, count, me_ref, len_ref, *refs):
    xs = refs[:count]
    q, top_i, acc_i, w_kv, b_kv = refs[count : count + 5]
    out_o, lse_o, x_s, top_s, acc_s, bias = refs[len(refs) - 6 :]
    me = me_ref[0]
    length = len_ref[bucket]
    rows = xs[0].shape[0]
    hd = out_o.shape[1]
    top_s[...] = top_i[...]
    acc_s[...] = acc_i[...]
    for i in range(count):

        @pl.when(me > i)
        def _(i=i):
            x_s[i] = xs[i][...]

    def body(slot, carry):
        first = (me - slot) * rows

        @pl.when(first < length)
        def _():
            set_bias(bias, slot, me, length)
            attend_slot(x_s.at[slot - 1], q, w_kv, b_kv, bias, top_s, acc_s)

        return carry

    lax.fori_loop(1, jnp.minimum(me, count) + 1, body, 0)

    def finish(h, carry):
        total = acc_s[h, hd : hd + 1]
        out_o[h] = (acc_s[h, :hd] / total).astype(BF16)
        lse_o[h] = top_s[h] + jnp.log2(total)
        return carry

    lax.fori_loop(0, HEADS, finish, 0)


def far_call(bucket, me, lengths, xs, q, top, acc, w_kv, b_kv, after):
    rows, d = xs[0].shape
    hd = head_size(d)
    shapes = ((HEADS, hd, rows), (HEADS, 1, rows), (HEADS, hd + 16, rows))
    operands = [me, lengths, *xs, q, top, acc, w_kv, b_kv]
    specs = [SM, SM] + [VM] * (len(xs) + 5)
    out_shape = [S(shapes[0], BF16), S(shapes[1], F32)]
    return pl.pallas_call(
        functools.partial(far_kernel, bucket, len(xs)),
        grid=(1,),
        out_shape=tuple(out_shape),
        in_specs=specs + [ANY] * len(after),
        out_specs=(VM,) * len(out_shape),
        scratch_shapes=[
            pltpu.VMEM((len(xs), rows, d), BF16),
            pltpu.VMEM(shapes[1], F32),
            pltpu.VMEM(shapes[2], F32),
            pltpu.VMEM((rows, rows), F32),
        ],
        compiler_params=params(),
        cost_estimate=cost(18e9, 5e6),
        name=f"attend_far_{bucket}",
    )(*operands, *after)


def norm_stats(v):
    centered = v - jnp.mean(v, axis=-1, keepdims=True)
    r = lax.rsqrt(jnp.mean(centered * centered, axis=-1, keepdims=True) + EPS)
    return centered * r, r


def norm_grad(n, r, gain, upstream):
    gu = gain * upstream
    return r * (gu - jnp.mean(gu, axis=-1, keepdims=True) - n * jnp.mean(gu * n, axis=-1, keepdims=True))


def over_rows(v):
    return jnp.sum(v.astype(F32), axis=0, keepdims=True)


def mid_kernel(bucket, me_ref, len_ref, attn, x, cot, w_out, w_inner, w_outer, vecs, b_inner, *refs):
    (out_o, branch_o, g_o, delta_o, normed_o, active_o, ghid_o, gtwo_o, gb_o, sums_o,
     pre_s, n1_s, r1_s, dual_s, slope_s, acc_s,
     inner_s, outer_s, cot_s, normed_s, active_s, ghid_s, gtwo_s, sems) = refs[len(refs) - 24 :]
    copies_in = [
        pltpu.make_async_copy(a, b, sems.at[i])
        for i, (a, b) in enumerate([(w_inner, inner_s), (w_outer, outer_s), (cot.at[bucket], cot_s)])
    ]
    for copy in copies_in:
        copy.start()
    w_inner, w_outer, cot = inner_s, outer_s, cot_s
    copies_out = [
        pltpu.make_async_copy(a, b, sems.at[3 + i])
        for i, (a, b) in enumerate([(normed_s, normed_o), (active_s, active_o), (gtwo_s, gtwo_o), (ghid_s, ghid_o)])
    ]
    me = me_ref[0]
    length = len_ref[bucket]
    _, rows, d = out_o.shape
    ff = active_s.shape[1]
    up_step = min(512, ff)
    down_step = min(512, ff)
    block = min(512, rows)
    b_out, gain1, shift1, gain2, shift2, gain_f, shift_f, b_outer = (vecs[i : i + 1] for i in range(8))
    attn_t = attn[...].reshape(d, rows)
    pre_s[...] = tn(attn_t, w_out[...])

    def over_blocks(work):
        def body(i, carry):
            work(pl.ds(pl.multiple_of(i * block, block), block), i * block)
            return carry

        lax.fori_loop(0, rows // block, body, 0)

    def first_norm(at, _):
        pre = x[0, at].astype(F32) + (pre_s[at] + b_out)
        n1, r1 = norm_stats(pre)
        pre_s[at] = pre
        n1_s[at] = n1
        r1_s[at] = r1
        normed_s[at] = (n1 * gain1 + shift1).astype(BF16)

    over_blocks(first_norm)
    copies_out[0].start()
    copies_in[0].wait()
    copies_in[1].wait()
    acc_s[...] = jnp.zeros(acc_s.shape, F32)

    def lift(i):
        f = slice(i * up_step, i * up_step + up_step)
        return nn(normed_s[...], w_inner[:, f]) + b_inner[:, f]


    def up(i, carry):
        f = slice(i * up_step, i * up_step + up_step)
        h = lift(i)
        square = h * h
        t = jnp.tanh(h * (GELU_C + (GELU_C * GELU_K) * square))
        half = 0.5 + 0.5 * t
        active = (h * half).astype(BF16)
        active_s[:, f] = active
        slope_s[:, f] = half + (0.5 * h) * (1.0 - t * t) * (GELU_C + (3.0 * GELU_C * GELU_K) * square)
        acc_s[...] += nn(active, w_outer[f, :])
        return carry

    for i in range(ff // up_step):
        up(i, 0)
    copies_out[1].start()
    sums_o[...] = jnp.zeros(sums_o.shape, F32)
    copies_in[2].wait()

    def last_norms(at, start):
        branch_two = acc_s[at] + b_outer
        normed = n1_s[at] * gain1 + shift1
        n2, r2 = norm_stats(normed + branch_two)
        nf, rf = norm_stats(pre_s[at] + branch_two)
        out_o[0, at] = ((n2 * gain2 + shift2) + (nf * gain_f + shift_f)).astype(BF16)
        p = me * rows + start + lax.broadcasted_iota(jnp.int32, (block, 1), 0)
        g_out = jnp.where(p < length, cot[at].astype(F32), 0.0)
        g_dual = norm_grad(nf, rf, gain_f, g_out)
        g_two = norm_grad(n2, r2, gain2, g_out)
        g_branch_two = (g_two + g_dual).astype(BF16)
        gtwo_s[at] = g_branch_two
        dual_s[at] = g_dual
        acc_s[at] = g_two
        sums_o[0:1] += over_rows(g_out * n2)
        sums_o[1:2] += over_rows(g_out)
        sums_o[2:3] += over_rows(g_out * nf)
        sums_o[4:5] += over_rows(g_branch_two)

    over_blocks(last_norms)
    copies_out[2].start()
    sums_o[3:4] = sums_o[1:2]

    @pl.when(me * rows < length)
    def _():
        def down(i, carry):
            f = pl.ds(pl.multiple_of(i * down_step, down_step), down_step)
            g_hidden = (nt(gtwo_s[...], w_outer[f, :]) * slope_s[:, f]).astype(BF16)
            ghid_s[:, f] = g_hidden
            sums_o[pl.ds(8 + i, 1)] = over_rows(g_hidden)
            acc_s[...] += nt(g_hidden, w_inner[:, f])
            return carry

        lax.fori_loop(0, ff // down_step, down, 0)
        copies_out[3].start()

        def first_back(at, _):
            g_normed = acc_s[at]
            n1 = n1_s[at]
            g_branch = norm_grad(n1, r1_s[at], gain1, g_normed) + dual_s[at]
            branch_o[at] = g_branch
            g_b = g_branch.astype(BF16)
            gb_o[at] = g_b
            sums_o[5:6] += over_rows(g_normed * n1)
            sums_o[6:7] += over_rows(g_normed)
            sums_o[7:8] += over_rows(g_b)

        over_blocks(first_back)
        g_o[...] = nt(w_out[...], gb_o[...]).astype(BF16).reshape(g_o.shape)

        def head_delta(h, carry):
            delta_o[h] = jnp.sum(g_o[h].astype(F32) * attn[h].astype(F32), axis=0, keepdims=True)
            return carry

        lax.fori_loop(0, HEADS, head_delta, 0)

    @pl.when(me * rows >= length)
    def _():
        for ref in (branch_o, g_o, delta_o, ghid_s, gb_o):
            ref[...] = jnp.zeros(ref.shape, ref.dtype)
        copies_out[3].start()

    for copy in copies_out:
        copy.wait()


def mid_call(bucket, me, lengths, attn, tokens, cotangent, w_out, w_inner, w_outer, vecs, b_inner, out, after):
    buckets, rows, d = tokens.shape
    ff = w_inner.shape[1]
    hd = head_size(d)
    one = pl.BlockSpec((1, rows, d), lambda i: (bucket, 0, 0))
    return pl.pallas_call(
        functools.partial(mid_kernel, bucket),
        grid=(1,),
        out_shape=(
            S((buckets, rows, d), BF16),
            S((rows, d), F32),
            S((HEADS, hd, rows), BF16),
            S((HEADS, 1, rows), F32),
            S((rows, d), BF16),
            S((rows, ff), BF16),
            S((rows, ff), BF16),
            S((rows, d), BF16),
            S((rows, d), BF16),
            S((16, d), F32),
        ),
        in_specs=[SM, SM, VM, one, ANY, VM, ANY, ANY, VM, VM] + [ANY] * (len(out) + len(after)),
        out_specs=(one, VM, VM, VM, ANY, ANY, ANY, ANY, VM, VM),
        input_output_aliases={10: 0} if out else {},
        scratch_shapes=[
            pltpu.VMEM((rows, d), F32),
            pltpu.VMEM((rows, d), F32),
            pltpu.VMEM((rows, 1), F32),
            pltpu.VMEM((rows, d), F32),
            pltpu.VMEM((rows, ff), F32),
            pltpu.VMEM((rows, d), F32),
            pltpu.VMEM((d, ff), BF16),
            pltpu.VMEM((ff, d), BF16),
            pltpu.VMEM((rows, d), BF16),
            pltpu.VMEM((rows, d), BF16),
            pltpu.VMEM((rows, ff), BF16),
            pltpu.VMEM((rows, ff), BF16),
            pltpu.VMEM((rows, d), BF16),
            pltpu.SemaphoreType.DMA((7,)),
        ],
        compiler_params=params(),
        cost_estimate=cost(12e9, 14e6),
        name=f"feed_forward_{bucket}",
    )(me, lengths, attn, tokens, cotangent, w_out, w_inner, w_outer, vecs, b_inner, *out, *after)


def wgrad_job(step, half, core):
    return step % half + jnp.where(step < half, 1 - core, core) * half


def rows_of(refs):
    return jnp.concatenate([r[...] for r in refs], axis=0)


def wgrad_kernel(buckets, count, half, places, *refs):
    groups = [refs[i * buckets : (i + 1) * buckets] for i in range(7)]
    active, g_two, normed, g_hidden, attn, g_b, sums = groups
    kept_o, sent_o = refs[7 * buckets :]
    step = pl.program_id(0)
    job = wgrad_job(step, half, places[0])

    def put(value):
        @pl.when(step < half)
        def _():
            sent_o[...] = value

        @pl.when(step >= half)
        def _():
            kept_o[...] = value

    @pl.when(job < count)
    def _():
        put(tn(rows_of(active), rows_of(g_two)).astype(BF16))

    @pl.when((job >= count) & (job < 2 * count))
    def _():
        put(tn(rows_of(normed), rows_of(g_hidden)).astype(BF16))

    @pl.when(job == 2 * count)
    def _():
        put(sum(nn(a[...], g[...]) for a, g in zip(attn, g_b)).astype(BF16))

    @pl.when(job > 2 * count)
    def _():
        put(jnp.zeros(kept_o.shape, BF16))

    @pl.when(job == 2 * count + 1)
    def _():
        value = sum(s[...] for s in sums).astype(BF16)

        @pl.when(step < half)
        def _():
            sent_o[:16] = value

        @pl.when(step >= half)
        def _():
            kept_o[:16] = value


def wgrad_call(places, devices, active, g_two, normed, g_hidden, attn, g_b, sums):
    buckets = len(active)
    rows, ff = active[0].shape
    d = g_two[0].shape[1]
    count = ff // d
    half = count + 1
    while 2 * half * d % (16 * devices):
        half += 1
    clip = lambda v, top: jnp.minimum(jnp.maximum(v, 0), top)
    job = lambda j, p: wgrad_job(j, half, p[0])
    full = pl.BlockSpec((rows, d), lambda j, p: (0, 0))
    tall = pl.BlockSpec((d, rows), lambda j, p: (0, 0))
    active_spec = pl.BlockSpec((rows, d), lambda j, p: (0, clip(job(j, p), count - 1)))
    hid_spec = pl.BlockSpec((rows, d), lambda j, p: (0, clip(job(j, p) - count, count - 1)))
    attn2 = [a.reshape(d, rows) for a in attn]
    return pl.pallas_call(
        functools.partial(wgrad_kernel, buckets, count, half),
        grid_spec=pltpu.PrefetchScalarGridSpec(
            num_scalar_prefetch=1,
            grid=(2 * half,),
            in_specs=[active_spec] * buckets + [full] * buckets + [full] * buckets + [hid_spec] * buckets
            + [tall] * buckets + [full] * buckets + [pl.BlockSpec((16, d), lambda j, p: (0, 0))] * buckets,
            out_specs=(
                pl.BlockSpec((d, d), lambda j, p: (jnp.maximum(j - half, 0), 0)),
                pl.BlockSpec((d, d), lambda j, p: (jnp.minimum(j, half - 1), 0)),
            ),
        ),
        out_shape=(S((half * d, d), BF16),) * 2,
        compiler_params=params(),
        cost_estimate=cost(buckets * 5e9, 20e6),
        name="weight_gradients",
    )(places, *active, *g_two, *normed, *g_hidden, *attn2, *g_b, *sums)


def attend_back(x, q, g, w_kv, b_kv, lse, delta, bias, dq_s, kv_s, dkv_s):
    pairs, width, d = w_kv.shape
    hd = width // 4
    rows = x.shape[0]
    block = 2 * width

    def project(i, carry):
        at = pl.ds(pl.multiple_of(i * block, block), block)
        w = w_kv[pl.ds(2 * i, 2)].reshape(block, d)
        kv_s[at] = (nt(w, x[...]) + b_kv[pl.ds(2 * i, 2)].reshape(block, 1)).astype(BF16)
        return carry

    lax.fori_loop(0, pairs // 2, project, 0)

    def body(step, carry):
        for j in range(2):
            one_pair(step * 2 + j)
        return carry

    def one_pair(pair):
        base = pl.multiple_of(pair * width, width)
        for i in range(2):
            h = pair * 2 + i
            at_k = pl.ds(base + i * hd, hd)
            at_v = pl.ds(base + (2 + i) * hd, hd)
            k = kv_s[at_k]
            q_t, g_t = q[h], g[h]
            probs = jnp.exp2(tn(k, q_t) + bias[...] - lse[h])
            g_probs = tn(kv_s[at_v], g_t)
            g_logits = (probs * (g_probs - delta[h])).astype(BF16)
            dkv_s[at_v] = nt(g_t, probs.astype(BF16)).astype(BF16)
            dkv_s[at_k] = (nt(q_t, g_logits) * LN2).astype(BF16)
            dq_s[h] += nn(k, g_logits)

    lax.fori_loop(0, pairs // 2, body, 0)


def back_kernel(bucket, low, high, fresh, first, final, places, me_ref, len_ref, *refs):
    count = high - low + 1
    refs = list(refs)
    take = lambda n: [refs.pop(0) for _ in range(n)]
    xs = take(count)
    q, g, lse, delta, w_kv, b_kv = take(6)
    sems = refs.pop()
    wq, branch = take(2) if low == 0 else (None, None)
    dq_i = None if fresh else take(1)[0]
    sums_i = None if first else take(1)[0]
    x_s, kv_s, dkv_s, dq_s, dx_s, bias, *late = refs[len(refs) - 6 - (low == 0) - (not first) :]
    refs = refs[: len(refs) - 6 - len(late)]
    refs = refs[len(refs) - 2 - final - (high > 0) :]
    dx_o = refs.pop(0) if high > 0 else None
    last_o, *sums_o = refs
    me = me_ref[0]
    length = len_ref[bucket]
    rows, d = xs[0].shape
    hd = g.shape[1]
    live = me * rows < length
    dq_s[...] = jnp.zeros(dq_s.shape, F32) if fresh else dq_i[...]
    rows_in = [
        pltpu.make_async_copy(xs[i], x_s.at[pl.ds(i * rows, rows)], sems.at[i]) for i in range(count)
    ]
    late_in = [
        pltpu.make_async_copy(source, to, sems.at[count + j])
        for j, (source, to) in enumerate(zip([branch] * (low == 0) + [sums_i] * (not first), late))
    ]
    for copy in rows_in + late_in:
        copy.start()

    def take_rows(i):
        for j in range(count):

            @pl.when(i == j)
            def _(j=j):
                rows_in[j].wait()

    def dx_out(i):
        return pltpu.make_async_copy(dx_s.at[i], dx_o.at[i], sems.at[count + 2 + i])

    def body(i, carry):
        slot = high - i
        at = pl.ds(pl.multiple_of(i * rows, rows), rows)
        active = live & (me >= slot)
        take_rows(i)

        @pl.when(active)
        def _():
            set_bias(bias, slot, me, length)
            attend_back(x_s.at[at], q, g, w_kv, b_kv, lse, delta, bias, dq_s, kv_s, dkv_s.at[:, at])

        @pl.when(active & (slot > 0))
        def _():
            dx_s[i] = tn(dkv_s[:, at], w_kv[...].reshape(2 * d, d)).astype(BF16)

        @pl.when(jnp.logical_not(active))
        def _():
            dkv_s[:, at] = jnp.zeros((2 * d, rows), BF16)

        @pl.when(jnp.logical_not(active) & (slot > 0))
        def _():
            dx_s[i] = jnp.zeros((rows, d), BF16)

        @pl.when(slot > 0)
        def _():
            dx_out(i).start()

        return carry

    lax.fori_loop(0, count, body, 0)
    pairs = HEADS // 2
    dq = (dq_s[...] * hd**-0.5).astype(BF16).reshape(d, rows)
    here = slice((count - 1) * rows, count * rows)
    for copy in late_in:
        copy.wait()
    if low == 0:
        last_o[...] = late[0][...]

        @pl.when(live)
        def _():
            last_o[...] += tn(dkv_s[:, here], w_kv[...].reshape(2 * d, d)) + tn(dq, wq[...])
    else:
        last_o[...] = dq_s[...]

    half = HEADS // 4
    ones = jnp.ones((8, count * rows), BF16)

    def add(pair, carry):
        at = pl.ds(pl.multiple_of(pair * 4 * hd, 4 * hd), 4 * hd)
        dkv = dkv_s[at, :]
        parts = [None, nn(dkv, x_s[...]), None]
        bias_sums = [nt(ones, dkv), jnp.zeros((8, d - 4 * hd), F32)]
        if low == 0:
            dq_pair = (dq_s[pl.ds(2 * pair, 2)] * hd**-0.5).astype(BF16).reshape(2 * hd, rows)
            parts[0] = nn(dq_pair, x_s[here])
            bias_sums[1:] = [nt(ones[:, :rows], dq_pair), jnp.zeros((8, d - 6 * hd), F32)]
        else:
            parts[0] = jnp.zeros((2 * hd, d), F32)
        parts[2] = jnp.concatenate([jnp.concatenate(bias_sums, axis=1), jnp.zeros((8, d), F32)])
        value = jnp.concatenate(parts, axis=0)
        if not first:
            value = value + late[-1][pair].astype(F32)
        value = value.astype(BF16)
        if final:
            kept = pair // half == places[0]
            to = pl.ds(pl.multiple_of((pair % half) * 6 * hd, 6 * hd), 6 * hd)
            to_bias = pl.ds(pl.multiple_of(half * 6 * hd + (pair % half) * 16, 16), 16)

            def put(ref):
                ref[to] = value[: 6 * hd]
                ref[to_bias] = value[6 * hd :]

            @pl.when(kept)
            def _():
                put(sums_o[0])

            @pl.when(jnp.logical_not(kept))
            def _():
                put(sums_o[1])
        else:
            sums_o[0][pair] = value
        return carry

    if final:
        used = half * (6 * hd + 16)
        for ref in sums_o:
            if used < ref.shape[0]:
                ref[used:] = jnp.zeros((ref.shape[0] - used, d), BF16)
    lax.fori_loop(0, pairs, add, 0)
    for i in range(count - (low == 0)):
        dx_out(i).wait()


def back_call(
    bucket, low, high, places, me, lengths, xs, q, g, lse, delta, w_kv, b_kv, wq, branch, dq, sums, final, after
):
    rows, d = xs[0].shape
    hd = head_size(d)
    own = low == 0
    fresh = dq is None
    far = high - max(low, 1) + 1
    operands = [places, me, lengths, *xs, q, g, lse, delta, w_kv, b_kv]
    specs = [SM] * 3 + [ANY] * len(xs) + [VM] * 6
    late = []
    if own:
        operands += [wq.reshape(d, d), branch]
        specs += [VM, ANY]
        late.append(branch)
    if not fresh:
        operands.append(dq)
        specs.append(VM)
    if sums is not None:
        operands.append(sums)
        specs.append(ANY)
        late.append(sums)
    sums_shape = (HEADS // 2, 6 * hd + 16, d)
    out_shape = [S((far, rows, d), BF16)] if far else []
    out_shape += [S((rows, d), F32) if own else S((HEADS, hd, rows), F32)]
    out_shape += [S((final, d), BF16)] * 2 if final else [S(sums_shape, BF16)]
    outs = pl.pallas_call(
        functools.partial(back_kernel, bucket, low, high, fresh, sums is None, final > 0),
        grid=(1,),
        out_shape=tuple(out_shape),
        in_specs=specs + [ANY] * len(after),
        out_specs=((ANY,) if far else ()) + (VM,) * (len(out_shape) - (far > 0)),
        scratch_shapes=[
            pltpu.VMEM((len(xs) * rows, d), BF16),
            pltpu.VMEM((2 * d, rows), BF16),
            pltpu.VMEM((2 * d, len(xs) * rows), BF16),
            pltpu.VMEM((HEADS, hd, rows), F32),
            pltpu.VMEM((max(far, 1), rows, d), BF16),
            pltpu.VMEM((rows, rows), F32),
            *[pltpu.VMEM(a.shape, a.dtype) for a in late],
            pltpu.SemaphoreType.DMA((2 * len(xs) + 2,)),
        ],
        compiler_params=params(36),
        cost_estimate=cost(10e9 * len(xs), 14e6),
        name=f"attend_back_{bucket}_{high}",
    )(*operands, *after)
    last = len(out_shape) - (3 if final else 2)
    return (outs[0] if far else None), outs[last], (outs[last + 1 :] if final else outs[-1])


def step_call(name, places, jobs, after):
    operands, specs, shapes, bodies = [places], [SM], [], []
    for job_in, job_specs, job_out, body in jobs:
        bodies.append((len(job_in), len(job_out), body))
        operands += job_in
        specs += job_specs
        shapes += job_out
    first_out = len(operands) + len(after)

    def kernel(places_ref, *refs):
        at_in, at_out = 0, first_out - 1
        for n_in, n_out, body in bodies:
            body(places_ref, *refs[at_in : at_in + n_in], *refs[at_out : at_out + n_out])
            at_in += n_in
            at_out += n_out

    outs = pl.pallas_call(
        kernel,
        grid=(1,),
        out_shape=tuple(shapes),
        in_specs=specs + [ANY] * len(after),
        out_specs=(VM,) * len(shapes),
        compiler_params=params(16),
        cost_estimate=cost(2e9, 4e6),
        name=name,
    )(*operands, *after)
    found = []
    for _, n_out, _ in bodies:
        found.append(outs[:n_out])
        outs = outs[n_out:]
    return found


def gate(arrays, after):
    outs = pl.pallas_call(
        lambda *refs: None,
        out_shape=tuple(S(a.shape, a.dtype) for a in arrays),
        in_specs=[ANY] * (len(arrays) + len(after)),
        out_specs=(ANY,) * len(arrays),
        input_output_aliases={i: i for i in range(len(arrays))},
        name="gate",
    )(*arrays, *after)
    return list(outs)


class Group:
    def __init__(self, index, axis, low, high):
        self.index, self.axis, self.low, self.count = index, axis, low, 1 << (high - low)
        self.place = (lax.axis_index(axis) >> low) & (self.count - 1)

    def swap(self, value, mask):
        size = lax.axis_size(self.axis)
        return lax.ppermute(value, self.axis, [(i, i ^ (mask << self.low)) for i in range(size)])


def part_rows(place, mask, size):
    return pl.ds(pl.multiple_of((place ^ mask) * size, size), size)


def total(kept, got, at):
    values = [r[at].astype(F32) for r in [kept, *got]]
    while len(values) > 1:
        values = [a + b for a, b in zip(values[::2], values[1::2])]
    return values[0].astype(BF16)


def split_job(kept, got, group):
    rows, d = kept.shape
    count = group.count if group else 1
    size = rows // count

    def body(places, kept, *refs):
        arrived, outs = refs[: len(got)], refs[len(got) :]
        for m in range(count):
            at = part_rows(places[group.index], m, size) if group else slice(None)
            outs[m][...] = total(kept, arrived, at)

    return [kept, *got], [VM] * (1 + len(got)), [S((size, d), BF16)] * count, body


def join_job(part, got, group):
    size, d = part.shape

    def body(places, *refs):
        for m in range(group.count):
            refs[-1][part_rows(places[group.index], m, size)] = refs[m][...]

    return [part, *got], [VM] * (1 + len(got)), [S((size * group.count, d), BF16)], body


def message_job(dx, at, carry):
    _, rows, d = dx.shape
    more = [] if carry is None else [carry]

    def body(places, dx, *refs):
        if more:
            refs[-1][...] = (dx[0].astype(F32) + refs[0][...].astype(F32)).astype(BF16)
        else:
            refs[-1][...] = dx[0]

    specs = [pl.BlockSpec((1, rows, d), lambda i: (at, 0, 0))] + [VM] * len(more)
    return [dx, *more], specs, [S((rows, d), BF16)], body


def sum_over_devices(kept, sent, groups, full=False):
    first, *rest = groups
    got = [first.swap(sent, 1)]
    scatter = rest[:-1] if full else rest
    for group in scatter:
        kept, *shards = yield split_job(kept, got, group)
        got = [group.swap(s, m + 1) for m, s in enumerate(shards)]
    (part,) = yield split_job(kept, got, None)
    if full and rest:
        got = [rest[-1].swap(part, m) for m in range(1, rest[-1].count)]
        (part,) = yield split_job(part, got, None)
    for group in reversed(scatter):
        got = [group.swap(part, m) for m in range(1, group.count)]
        (part,) = yield join_job(part, got, group)
    return part, first.swap(part, 1)


def send_back(pieces, n):
    carry = None
    for i, slot in enumerate(range(n - 1, 0, -1)):
        (message,) = yield message_job(*pieces(i), carry)
        carry = lax.ppermute(message, "blk", [(j, j - 1) for j in range(slot, n)])
    return carry


class Process:
    def __init__(self, steps):
        self.steps, self.result = steps, None
        self.job = next(steps)

    def advance(self, outs):
        try:
            self.job = self.steps.send(outs)
        except StopIteration as end:
            self.job, self.result = None, end.value


class Board:
    def __init__(self, places):
        self.places, self.active, self.ticks = places, [], 0

    def start(self, steps):
        self.active.append(Process(steps))
        return self.active[-1]

    def tick(self, after, only=None):
        self.ticks += 1
        now = self.active if only is None else only
        outs = step_call(f"step_{self.ticks}", self.places, [p.job for p in now], after)
        for p, o in zip(list(now), outs):
            p.advance(o)
        self.active = [p for p in self.active if p.job is not None]
        return [o for group in outs for o in group]


def big_kernel(ff, places, mine, got, *refs):
    outer_o, inner_o, out_o, vec_o = refs[len(refs) - 4 :]
    half, d = mine.shape
    count = ff // d
    for own_half in range(2):

        @pl.when(places[0] == own_half)
        def _(own_half=own_half):
            for i in range(2 * half // d):
                src = mine if i // (half // d) == own_half else got
                at = (i % (half // d)) * d
                value = src[at : at + d]
                if i < count:
                    outer_o[i * d : i * d + d] = value.astype(F32)
                elif i < 2 * count:
                    inner_o[:, (i - count) * d : (i - count) * d + d] = value.astype(F32)
                elif i == 2 * count:
                    out_o[...] = value.astype(F32)
                elif i == 2 * count + 1:
                    vec_o[...] = value[:16].astype(F32)


def big_call(places, mine, got, ff, after):
    d = mine.shape[1]
    shapes = (S((ff, d), F32), S((d, ff), F32), S((d, d), F32), S((16, d), F32))
    return pl.pallas_call(
        functools.partial(big_kernel, ff),
        grid=(1,),
        out_shape=shapes,
        in_specs=[SM, VM, VM] + [ANY] * len(after),
        out_specs=(VM,) * 4,
        compiler_params=params(24),
        cost_estimate=cost(5e9, 14e6),
        name="feed_forward_sums",
    )(places, mine, got, *after)


def small_kernel(places, mine, got, *refs):
    weights, bias_o = refs[len(refs) - 4 : len(refs) - 1], refs[-1]
    d = weights[0].shape[0]
    hd = head_size(d)
    half = HEADS // 4
    bias_o[...] = jnp.zeros(bias_o.shape, F32)
    for own_half in range(2):

        @pl.when(places[0] == own_half)
        def _(own_half=own_half):
            for pair in range(HEADS // 2):
                src = mine if pair // half == own_half else got
                at = (pair % half) * 6 * hd
                at_bias = half * 6 * hd + (pair % half) * 16
                lanes = slice(2 * hd * pair, 2 * hd * pair + 2 * hd)
                for k in range(3):
                    rows = src[at + 2 * hd * k : at + 2 * hd * k + 2 * hd].astype(F32)
                    weights[k][:, lanes] = rows.T
                bias = src[at_bias : at_bias + 16].astype(F32)
                bias_o[0:1, lanes] = bias[:1, 4 * hd : 6 * hd]
                bias_o[1:2, lanes] = bias[:1, 2 * hd : 4 * hd]


def small_call(places, mine, got):
    d = mine.shape[1]
    return pl.pallas_call(
        small_kernel,
        grid=(1,),
        out_shape=(S((d, d), F32),) * 3 + (S((8, d), F32),),
        in_specs=[SM, VM, VM],
        out_specs=(VM,) * 4,
        compiler_params=params(16),
        cost_estimate=cost(2e9, 5e6),
        name="attention_sums",
    )(places, mine, got)


def tokens_kernel(mine, carry, *refs):
    refs[-1][0] = mine[...] + carry[...].astype(F32)


def tokens_call(bucket, buckets, mine, carry, whole, after):
    rows, d = mine.shape
    return pl.pallas_call(
        tokens_kernel,
        grid=(1,),
        out_shape=S((buckets, rows, d), F32),
        in_specs=[VM, VM] + [ANY] * (len(whole) + len(after)),
        out_specs=pl.BlockSpec((1, rows, d), lambda i: (bucket, 0, 0)),
        input_output_aliases={2: 0} if whole else {},
        compiler_params=params(16),
        cost_estimate=cost(2e9, 3e6),
        name=f"token_gradients_{bucket}",
    )(mine, carry, *whole, *after)


def on_device(
    tokens, lengths, w_query, w_key, w_value, w_out, b_query, b_value, b_out, norm1_gain, norm1_bias,
    norm2_gain, norm2_bias, final_gain, final_bias, w_inner, b_inner, w_outer, b_outer, cotangent,
):
    buckets, rows, d = tokens.shape
    ff = w_inner.shape[1]
    hd = head_size(d)
    pairs = HEADS // 2
    n = lax.axis_size("blk")
    me = lax.axis_index("blk").astype(jnp.int32).reshape(1)
    bits = lambda axis: (lax.axis_size(axis) - 1).bit_length()
    groups = [Group(0, "batch", 0, 1), Group(1, "batch", 1, bits("batch")), Group(2, "blk", 0, bits("blk"))]
    places = jnp.stack([g.place for g in groups]).astype(jnp.int32)
    devices = math.prod(g.count for g in groups)
    groups = [groups[0]] + [g for g in groups[1:] if g.count > 1]

    paired = lambda w: w.T.reshape(pairs, 2 * hd, d)
    wq = paired(w_query)
    bq = b_query.reshape(pairs, 2 * hd, 1)
    w_kv = jnp.concatenate([paired(w_key), paired(w_value)], axis=1)
    b_v = b_value.reshape(pairs, 2 * hd, 1)
    b_kv = jnp.concatenate([jnp.zeros_like(b_v), b_v], axis=1)
    vecs = jnp.stack([b_out, norm1_gain, norm1_bias, norm2_gain, norm2_bias, final_gain, final_bias, b_outer])
    b_in = b_inner.reshape(1, ff)

    def hop(value, slot):
        return lax.ppermute(value, "blk", [(i, i + 1) for i in range(slot - 1, n - 1)])

    run_own = lambda b, after: own_call(b, me, lengths, tokens, wq, bq, w_kv, b_kv, (b + 1) % buckets, after)
    run_far = lambda b, after: far_call(b, me, lengths, held[b][1:], own[b][0], own[b][1], own[b][2], w_kv, b_kv, after)
    run_mid = lambda b, out, after: mid_call(
        b, me, lengths, attns[b], tokens, cotangent, w_out, w_inner, w_outer, vecs, b_in, out, after
    )
    held = [[tokens[b]] for b in range(buckets)]
    own, mids, attns, lses, out = [], [], [], [], []
    moving = {}
    if n == 4 and buckets == 3:
        plan = [
            ([(0, 1)], [(0, 2), (1, 1)]),
            ([(0, 2), (1, 1)], [(0, 3)]),
            ([(0, 3)], [(1, 2), (2, 1)]),
            ([(1, 2)], [(1, 3)]),
            ([(1, 3), (2, 1)], [(2, 2)]),
            ([(2, 2)], [(2, 3)]),
            ([(2, 3)], []),
        ]
    else:
        plan = []
        for b in range(buckets):
            for slot in range(1, n):
                source = held[b][-1]
                held[b].append(hop(source, slot))
    if plan:
        moving[0, 1] = hop(tokens[0], 1)

    def passing(kernel, last):
        if kernel >= len(plan):
            return [last]
        arrived, next_hops = plan[kernel]
        fresh = [b for b, slot in next_hops if slot == 1]
        held_on = [(b, slot - 1) for b, slot in next_hops if slot > 1 and (b, slot - 1) not in arrived]
        values = [moving.pop(k) for k in arrived] + [held[b][slot] for b, slot in held_on]
        passed = gate(values + [own[b - 1][3] for b in fresh], [last])
        for k, value in zip(arrived, passed):
            held[k[0]].append(value)
        for (b, slot), value in zip(held_on, passed[len(arrived) :]):
            held[b][slot] = value
        starts = dict(zip(fresh, passed[len(values) :]))
        for b, slot in next_hops:
            moving[b, slot] = hop(starts[b] if slot == 1 else held[b][slot - 1], slot)
        return passed[:1]

    after = [vecs, b_in]
    for b in range(buckets):
        own.append(run_own(b, after))
        after = passing(b, own[b][0])
    for b in range(buckets):
        attn, lse = run_far(b, after)
        attns.append(attn)
        lses.append(lse)
        after = passing(buckets + 2 * b, lse)
        mids.append(run_mid(b, out, after))
        out = [mids[b][0]]
        after = passing(buckets + 2 * b + 1, mids[b][9])
    column = lambda i: [m[i] for m in mids]
    kept, sent = wgrad_call(
        places, devices, column(5), column(7), column(4), column(6), attns, column(8), column(9)
    )

    final_rows = HEADS // 4 * (6 * hd + 16)
    final_rows += -final_rows % (16 * lax.axis_size("batch") // 2)

    board = Board(places)
    big = board.start(sum_over_devices(kept, sent, groups))
    waiting = [sent]
    mine, returns = [], []
    resting = lambda: [p for p in board.active if p is not big] if board.ticks == 1 else None
    sums = None
    for b in range(buckets):
        g, delta, branch = mids[b][2], mids[b][3], mids[b][1]
        args = (own[b][0], g, lses[b], delta, w_kv, b_kv, wq, branch)
        dx = {}
        last = final_rows if b + 1 == buckets else 0
        cut = max(1, n // 2) if b >= SPLIT_FROM else 0
        pieces = lambda i, dx=dx, cut=cut: (dx[0], i) if i < n - max(cut, 1) else (dx[1], i - (n - cut))
        if cut:
            there = held[b][n - 1 : cut - 1 : -1]
            dx[0], dq, sums = back_call(b, cut, n - 1, places, me, lengths, there, *args, None, sums, 0, waiting)
            returns.append(board.start(send_back(pieces, n)))
            waiting = board.tick([sums], resting())
            there = held[b][cut - 1 :: -1]
            dx[1], own_part, sums = back_call(b, 0, cut - 1, places, me, lengths, there, *args, dq, sums, last, waiting)
            if not last:
                waiting = board.tick([sums], resting())
        else:
            dx[0], own_part, sums = back_call(b, 0, n - 1, places, me, lengths, held[b][::-1], *args, None, sums, last, waiting)
            returns.append(board.start(send_back(pieces, n)))
            waiting = board.tick([sums])
        mine.append(own_part)
    after = [sums[1]]
    whole, grads, done = [], None, set()
    alone = 2
    landed = lambda: [r.result for r in returns if r.result is not None]
    if board.active:
        after = board.tick(after + landed())[:1]
    small_first = Process(sum_over_devices(*gate(list(sums), after), groups, n > 1))
    board.active.append(small_first)
    while board.active:
        sent = board.tick(landed() + after, [small_first] if alone > 0 else None)
        alone, after = alone - 1, sent[:1]
        ready = [b for b in range(buckets) if b not in done and returns[b].result is not None]
        if grads is None and big.result is not None:
            grads = big_call(places, *big.result, ff, sent)
            after = [grads[3]]
        elif ready:
            b = ready[0]
            whole = [tokens_call(b, buckets, mine[b], returns[b].result, whole, sent)]
            done.add(b)
            after = whole
    for b in range(buckets):
        if b not in done:
            whole = [tokens_call(b, buckets, mine[b], returns[b].result, whole, [])]
    grad_wq, grad_wk, grad_wv, bias = small_call(places, *small_first.result)
    grad_w_outer, grad_w_inner, grad_w_out, v = grads
    return (
        out[0], whole[0], grad_wq, grad_wk, grad_wv, grad_w_out, bias[0], bias[1], v[7],
        v[5], v[6], v[0], v[1], v[2], v[3],
        grad_w_inner, v[8 : 8 + ff // d].reshape(ff), grad_w_outer, v[4],
    )


def solution(mesh):
    rows = P("batch", "blk", None)
    in_specs = (rows, P("batch")) + (P(),) * 17 + (rows,)
    out_specs = (rows, rows) + (P(),) * 17
    return jax.shard_map(on_device, mesh=mesh, in_specs=in_specs, out_specs=out_specs, check_vma=False)
```
